32 devices in a mesh: wide: 16 (over z, y, x), narrow: 2 (over core).
Axes of the slice: x: 2, y: 2, z: 4, core: 2. Of those that a mesh axis runs over, the one named last changes fastest.
Arguments:
- features: bfloat16 [2048, 512], P('wide'), may hold values from -34 to 34
- proxies: float32 [65536, 512], P(('wide', 'narrow')), may hold values from -6 to 6
- sample_ids: int32 [32768], P(('wide', 'narrow')), may hold values from 0 to 2047
- positives: int32 [2048], replicated, may hold values from 0 to 32767
- loss_weight: float32 [2048], replicated, may hold values from 1 to 10
Outputs:
- feature_grad: float32 [2048, 512], P('wide')
- proxy_grad: float32 [32768, 512], P(('wide', 'narrow'))
The draws below stay inside these ranges and needn't reach their ends.
All inputs are finite; a program needn't handle non-finite values.
Results may differ from the reference program's by a relative error of at most 0.01.
Values may be sent and summed in bfloat16 or wider, within the bound.
No kernel may reach another device: no remote copies, remote signals or barrier semaphores. Data moves between devices by JAX's collectives and lax.ppermute only.
A program may use at most 128 MiB of HBM per device.

```python
import math
import jax
import jax.numpy as jnp
from jax import lax

E = 512
S_DEV = 1024
P_DEV = 2048
FEATS = 2048
CANDS = 32768
PROXIES = 65536
N_WIDE = 16
N_NARROW = 2


def draw_features(key, part):
    key = jax.random.fold_in(key, 11)
    key_rows = jax.random.fold_in(key, 0)
    return jnp.clip(jax.random.normal(key_rows, (FEATS, E), jnp.float32), -6.0, 6.0).astype(jnp.bfloat16)


def with_ends(drawn, own_key, low, largest):
    spot = [jax.random.randint(jax.random.fold_in(own_key, axis), (), 0, length) for axis, length in enumerate(drawn.shape)]
    longest = drawn.shape.index(max(drawn.shape))
    next_to = spot[:longest] + [(spot[longest] + 1) % drawn.shape[longest]] + spot[longest + 1:]
    return drawn.at[tuple(spot)].set(low).at[tuple(next_to)].set(largest)


def block_levels(own_key, dims, pieces, least, largest):
    gain = 1.0
    for axis_at, blocks in pieces:
        heights = jax.random.uniform(jax.random.fold_in(jax.random.fold_in(own_key, 6), axis_at), (blocks,), jnp.float32, least / len(pieces), largest / len(pieces))
        gain = gain * jnp.repeat(jnp.exp(heights), dims[axis_at] // blocks).reshape((-1,) + (1,) * (len(dims) - 1 - axis_at))
    return gain


def bell_draw(key, shape, deviation, reach, shards=(), dtype=jnp.bfloat16):
    drawn = deviation * jax.random.normal(key, shape, jnp.float32)
    if shards:
        drawn = drawn * block_levels(key, shape, shards, -0.22, 0.18)
    return jnp.clip(drawn, -reach, reach).astype(dtype)


def setup_inputs(seed: int = 0) -> dict:
    seeds = jax.random.split(jax.random.key(seed), 6)
    return {
        "features": draw_features(jax.random.fold_in(seeds[5], 71), 0),
        "proxies": bell_draw(seeds[1], (PROXIES, E), 1.0, 6.0, ((0, 32),), jnp.float32),
        "sample_ids": with_ends(jax.random.randint(seeds[2], (CANDS,), 0, P_DEV), jax.random.fold_in(seeds[2], 1), 0, P_DEV - 1).astype(jnp.int32),
        "positives": with_ends(jax.random.randint(seeds[3], (FEATS,), 0, CANDS), jax.random.fold_in(seeds[3], 1), 0, CANDS - 1).astype(jnp.int32),
        "loss_weight": jnp.clip(jnp.exp(jax.random.uniform(seeds[4], (FEATS,), jnp.float32, math.log(1.0), math.log(10.0))), 1.0, 10.0),
    }


logit_scale = 3.0
epsilon = 1e-06

def reference(features, proxies, sample_ids, positives, loss_weight):
    device_count = N_WIDE * N_NARROW
    owner = (jnp.arange(CANDS) // S_DEV).astype(jnp.int32)
    row_ids = owner * P_DEV + sample_ids.astype(jnp.int32)
    picked = proxies[row_ids]
    lengths = jnp.sqrt(lax.optimization_barrier(jnp.sum(picked * picked, axis=1, keepdims=True)) + epsilon)
    unit_rows = picked / lengths
    unit_low = unit_rows.astype(jnp.bfloat16)
    unit_wide = lax.optimization_barrier(unit_low).astype(jnp.float32)
    feat_wide = features.astype(jnp.float32)
    blocks = unit_wide.reshape(device_count, S_DEV, E)

    def block_stats(unit_block):
        logits = logit_scale * jnp.dot(feat_wide, unit_block.T)
        top = lax.optimization_barrier(jnp.max(logits, axis=1))
        return (top, lax.optimization_barrier(jnp.sum(jnp.exp(logits - top[:, None]), axis=1)))
    tops, totals = lax.map(block_stats, blocks)
    row_max = lax.optimization_barrier(jnp.max(tops, axis=0))
    row_total = lax.optimization_barrier(jnp.sum(totals * jnp.exp(tops - row_max[None, :]), axis=0))
    offsets = (jnp.arange(device_count) * S_DEV).astype(jnp.int32)

    def block_step(accum_grad, inputs):
        unit_block, offset = inputs
        logits = logit_scale * jnp.dot(feat_wide, unit_block.T)
        soft = jnp.exp(logits - row_max[:, None]) / row_total[:, None]
        cand_ids = offset + jnp.arange(S_DEV).astype(jnp.int32)
        onehot = (positives[:, None] == cand_ids[None, :]).astype(jnp.float32)
        grad_low = (loss_weight[:, None] * (soft - onehot)).astype(jnp.bfloat16)
        grad_wide = lax.optimization_barrier(grad_low).astype(jnp.float32)
        accum_grad = accum_grad + logit_scale * jnp.dot(grad_wide, unit_block)
        unit_grad = logit_scale * jnp.dot(grad_wide.T, feat_wide)
        return (accum_grad, unit_grad)
    start_grad = jnp.zeros((FEATS, E), jnp.float32)
    feature_grad, unit_grads = lax.scan(block_step, start_grad, (blocks, offsets))
    unit_grad = unit_grads.reshape(CANDS, E)
    inner = lax.optimization_barrier(jnp.sum(unit_rows * unit_grad, axis=1, keepdims=True))
    proxy_grad = (unit_grad - unit_rows * inner) / lengths
    return (feature_grad, proxy_grad)
```

```python
import jax
import jax.numpy as jnp
from jax import lax
from jax.sharding import PartitionSpec as P

logit_scale = 3.0
epsilon = 1e-06


def swap(x, axis, size, bit):
    return lax.ppermute(x, axis, [(i, i ^ (1 << bit)) for i in range(size)])


def bits_of(size):
    return size.bit_length() - 1


def flip_blocks(x, bit, axis):
    shape = x.shape
    step = 1 << bit
    y = x.reshape(shape[:axis] + (shape[axis] // (2 * step), 2, step) + shape[axis + 1:])
    return jnp.flip(y, axis + 1).reshape(shape)


def gather_wide(part, wide):
    rows, cols = part.shape
    top = bits_of(wide) - 1
    blocks = part[None]
    for bit in range(top, 1, -1):
        other = swap(blocks, "wide", wide, bit)
        blocks = jnp.stack([blocks, other], axis=0 if bit == top else 1)
        blocks = blocks.reshape((-1, rows, cols))
    half = cols // 2
    left, right = blocks[:, :, :half], blocks[:, :, half:]
    left_x = swap(left, "wide", wide, 0)
    right_y = swap(right, "wide", wide, 1)
    left = jnp.stack([left, left_x], axis=1)
    right = jnp.stack([right, right_y], axis=1)
    left_y = swap(left, "wide", wide, 1)
    right_x = swap(right, "wide", wide, 0)
    left = jnp.stack([left, left_y], axis=1)
    right = jnp.stack([right, right_x], axis=2)
    return jnp.concatenate([left, right], axis=-1).reshape(wide, rows, cols)


def make(wide, narrow):
    def per_device(features, proxies, sample_ids, positives, loss_weight):
        sample_count = sample_ids.shape[0]
        rows, width = features.shape
        cols = width // narrow
        count = positives.shape[0]
        w = lax.axis_index("wide")
        n = lax.axis_index("narrow")
        order = w ^ jnp.arange(wide)
        narrow_order = n ^ jnp.arange(narrow)

        part = lax.dynamic_slice(features, (0, n * cols), (rows, cols))
        part = gather_wide(part, wide).reshape(count, cols)[None]
        for bit in range(bits_of(narrow)):
            part = jnp.concatenate([part, swap(part, "narrow", narrow, bit)], 0)
        if narrow == 2:
            first = jnp.where(n == 0, part[0], part[1])
            second = jnp.where(n == 0, part[1], part[0])
            gathered = jnp.concatenate([first, second], axis=1)
        else:
            gathered = jnp.take(part, narrow_order, axis=0).transpose(1, 0, 2).reshape(count, width)

        picked = jnp.take(proxies, sample_ids, axis=0)
        lengths = jnp.sqrt(jnp.sum(picked * picked, axis=1, keepdims=True) + epsilon)
        unit_rows = picked / lengths
        unit_low = unit_rows.astype(jnp.bfloat16)
        positives = jnp.take(positives.reshape(wide, rows), order, axis=0).reshape(count)
        loss_weight = jnp.take(loss_weight.reshape(wide, rows), order, axis=0).reshape(count)

        logits = logit_scale * lax.dot_general(
            gathered, unit_low, (((1,), (1,)), ((), ())), preferred_element_type=jnp.float32
        )
        local_max = jnp.max(logits, axis=1)
        shifted = jnp.exp(logits - local_max[:, None])
        local_total = jnp.sum(shifted, axis=1)

        stats = jnp.stack([local_max, local_total]).reshape(2, wide, rows)

        def merge(stats, other):
            top = jnp.maximum(stats[0], other[0])
            total = stats[1] * jnp.exp(stats[0] - top) + other[1] * jnp.exp(other[0] - top)
            return jnp.stack([top, total])

        for bit in range(bits_of(narrow)):
            stats = merge(stats, swap(stats, "narrow", narrow, bit))
        for bit in range(bits_of(wide)):
            stats = merge(stats, flip_blocks(swap(stats, "wide", wide, bit), bit, 1))
        stats = stats.reshape(2, count)
        soft = shifted * (jnp.exp(local_max - stats[0]) / stats[1])[:, None]

        base_id = lax.axis_index(("wide", "narrow")) * sample_count
        cand_ids = base_id + jnp.arange(sample_count, dtype=jnp.int32)
        onehot = (positives[:, None] == cand_ids[None, :]).astype(jnp.float32)
        grad_logits = (loss_weight[:, None] * (soft - onehot)).astype(jnp.bfloat16)

        unit_order = jnp.take(unit_low.reshape(sample_count, narrow, cols), narrow_order, axis=1)
        shares = logit_scale * jnp.dot(
            grad_logits, unit_order.reshape(sample_count, width), preferred_element_type=jnp.float32
        )
        shares = shares.reshape(count, narrow, cols)
        for bit in range(bits_of(narrow) - 1, -1, -1):
            half = 1 << bit
            other = swap(shares[:, half:].astype(jnp.bfloat16), "narrow", narrow, bit)
            shares = shares[:, :half] + other.astype(jnp.float32)
        shares = shares.reshape(wide // 4, 2, 2, rows, cols)
        half = cols // 2
        left, right = shares[..., :half], shares[..., half:]

        def send(x, bit):
            return swap(x.astype(jnp.bfloat16), "wide", wide, bit).astype(jnp.float32)

        left_in = send(left[:, 1], 1)
        right_in = send(right[:, :, 1], 0)
        left = left[:, 0] + left_in
        right = right[:, :, 0] + right_in
        left_in = send(left[:, 1], 0)
        right_in = send(right[:, 1], 1)
        left = left[:, 0] + left_in
        right = right[:, 0] + right_in
        shares = jnp.concatenate([left, right], axis=-1)
        for bit in range(bits_of(wide) - 3, -1, -1):
            half = 1 << bit
            shares = shares[:half] + send(shares[half:], bit + 2)
        mine = shares
        for bit in range(bits_of(narrow)):
            mine = jnp.concatenate([mine, swap(mine, "narrow", narrow, bit)], 0)
        if narrow == 2:
            first = jnp.where(n == 0, mine[0], mine[1])
            second = jnp.where(n == 0, mine[1], mine[0])
            feature_grad = jnp.concatenate([first, second], axis=1)
        else:
            feature_grad = jnp.take(mine, narrow_order, axis=0).transpose(1, 0, 2).reshape(rows, width)

        unit_grad = logit_scale * lax.dot_general(
            grad_logits, gathered, (((0,), (0,)), ((), ())), preferred_element_type=jnp.float32
        )
        inner = jnp.sum(unit_rows * unit_grad, axis=1, keepdims=True)
        proxy_grad = (unit_grad - unit_rows * inner) / lengths
        return (feature_grad, proxy_grad)

    return per_device


def solution(mesh):
    placed = (P("wide", None), P(("wide", "narrow"), None), P(("wide", "narrow")), P(), P())
    return jax.shard_map(
        make(mesh.shape["wide"], mesh.shape["narrow"]),
        mesh=mesh,
        in_specs=placed,
        out_specs=(P("wide", None), P(("wide", "narrow"), None)),
        check_vma=False,
    )
```

```python
import functools
import math

import jax
import jax.numpy as jnp
from jax import lax
from jax.experimental import pallas as pl
from jax.experimental.pallas import tpu as pltpu
from jax.sharding import PartitionSpec as P

logit_scale = 3.0
epsilon = 1e-06
exp2_scale = logit_scale * math.log2(math.e)
chunk = 256
both = ("wide", "narrow")
whole = pl.BlockSpec(memory_space=pltpu.VMEM)
params = pltpu.CompilerParams(vmem_limit_bytes=20 * 1024 * 1024)


def t_bit(n):
    return 1 if n % 2 == 0 else 2


def s_bit(n):
    return 3 - t_bit(n)


def exchange(x, sizes, partner):
    wide, narrow = sizes
    pairs = []
    for w in range(wide):
        for n in range(narrow):
            pw, pn = partner(w, n)
            pairs.append((w * narrow + n, pw * narrow + pn))
    return lax.ppermute(x, both, pairs)


def logits_kernel(group_count, part_count, unit_ref, *refs):
    parts = refs[: group_count * part_count]
    shifted_ref, stats_ref = refs[group_count * part_count:]
    step = 0
    for g in range(group_count):
        group = parts[g * part_count:(g + 1) * part_count]
        cols = group[0].shape[1]
        for row in range(0, group[0].shape[0], chunk):
            dots = None
            for k, part in enumerate(group):
                prod = lax.dot_general(
                    unit_ref[:, k * cols:(k + 1) * cols], part[row:row + chunk, :],
                    (((1,), (1,)), ((), ())), preferred_element_type=jnp.float32,
                )
                dots = prod if dots is None else dots + prod
            top = jnp.max(dots, axis=0, keepdims=True)
            shifted = jnp.exp2((dots - top) * exp2_scale)
            total = jnp.sum(shifted, axis=0, keepdims=True)
            shifted_ref[:, step * chunk:(step + 1) * chunk] = shifted
            for b in range(chunk // 128):
                at = step * (chunk // 128) + b
                stats_ref[0, at:at + 1, :] = top[:, b * 128:(b + 1) * 128]
                stats_ref[1, at:at + 1, :] = total[:, b * 128:(b + 1) * 128]
            step += 1


def logits_call(unit, groups):
    rows = groups[0][0].shape[0]
    count = len(groups) * rows
    samples = unit.shape[0]
    flat = [part for group in groups for part in group]
    return pl.pallas_call(
        functools.partial(logits_kernel, len(groups), len(groups[0])),
        out_shape=(
            jax.ShapeDtypeStruct((samples, count), jnp.float32),
            jax.ShapeDtypeStruct((2, count // 128, 128), jnp.float32),
        ),
        in_specs=[whole] * (1 + len(flat)),
        out_specs=(whole, whole),
        compiler_params=params,
        cost_estimate=pl.CostEstimate(
            flops=2 * samples * count * unit.shape[1],
            bytes_accessed=4 * samples * count,
            transcendentals=samples * count,
        ),
        name="logits",
    )(unit, *flat)


def grad_kernel(first, steps, unit_t_ref, shifted_ref, scale_ref, weight_ref, at_ref, grad_ref, keep_ref, send_ref):
    samples = shifted_ref.shape[0]
    half = unit_t_ref.shape[0] // 2
    per = chunk // 128
    cand = lax.broadcasted_iota(jnp.int32, (samples, chunk), 0)

    def row(ref, at):
        return jnp.concatenate([ref[at + b:at + b + 1, :] for b in range(per)], axis=1)

    for out, at in enumerate(steps):
        cols = slice((at - first) * chunk, (at - first + 1) * chunk)
        scale, weight, spot = row(scale_ref, at * per), row(weight_ref, at * per), row(at_ref, at * per)
        soft = shifted_ref[:, cols] * scale
        grad = (weight * jnp.where(cand == spot, soft - 1.0, soft)).astype(jnp.bfloat16)
        out_cols = slice(out * chunk, (out + 1) * chunk)
        grad_ref[:, out_cols] = grad
        shares = logit_scale * jnp.dot(unit_t_ref[...], grad, preferred_element_type=jnp.float32)
        keep_ref[:, out_cols] = shares[:half]
        send_ref[:, out_cols] = shares[half:].astype(jnp.bfloat16)


def grad_call(unit_t, shifted, scale, weight, spots, first, steps):
    samples = shifted.shape[0]
    width = unit_t.shape[0]
    count = len(steps) * chunk
    return pl.pallas_call(
        functools.partial(grad_kernel, first, steps),
        out_shape=(
            jax.ShapeDtypeStruct((samples, count), jnp.bfloat16),
            jax.ShapeDtypeStruct((width // 2, count), jnp.float32),
            jax.ShapeDtypeStruct((width // 2, count), jnp.bfloat16),
        ),
        in_specs=[whole] * 5,
        out_specs=(whole,) * 3,
        compiler_params=params,
        cost_estimate=pl.CostEstimate(
            flops=2 * samples * count * width, bytes_accessed=6 * samples * count, transcendentals=0
        ),
        name="grads",
    )(unit_t, shifted, scale, weight, spots)


def proxy_kernel(group_count, part_count, rows, late_ref, early_ref, *refs):
    parts = refs[:group_count * part_count]
    picked_ref, out_ref = refs[group_count * part_count:]
    size, cols = parts[0].shape
    grads = [late_ref] + [early_ref.at[:, g * size:(g + 1) * size] for g in range(group_count - 1)]
    n = lax.axis_index("narrow")
    places = []
    for k in range(part_count):
        if part_count == 1:
            places.append(slice(0, cols))
        else:
            places.append(pl.ds(pl.multiple_of((n ^ k) * cols, cols), cols))
    for row in range(0, picked_ref.shape[0], rows):
        at = slice(row, row + rows)
        sums = []
        for k in range(part_count):
            total = None
            for g in range(group_count):
                prod = jnp.dot(
                    grads[g][at, :], parts[g * part_count + k][...], preferred_element_type=jnp.float32
                )
                total = prod if total is None else total + prod
            sums.append(logit_scale * total)
        picked = [picked_ref[at, place] for place in places]
        square = functools.reduce(jnp.add, [jnp.sum(p * p, axis=1, keepdims=True) for p in picked])
        inverse = 1.0 / jnp.sqrt(square + epsilon)
        inner = functools.reduce(jnp.add, [jnp.sum(p * s, axis=1, keepdims=True) for p, s in zip(picked, sums)])
        slope = inner * inverse * inverse
        for place, p, s in zip(places, picked, sums):
            out_ref[at, place] = (s - p * slope) * inverse


def proxy_call(late, early, groups, picked):
    samples, width = picked.shape
    count = late.shape[1] + early.shape[1]
    flat = [part for group in groups for part in group]
    return pl.pallas_call(
        functools.partial(proxy_kernel, len(groups), len(groups[0]), 256),
        out_shape=jax.ShapeDtypeStruct((samples, width), jnp.float32),
        in_specs=[whole] * (len(flat) + 3),
        out_specs=whole,
        compiler_params=params,
        cost_estimate=pl.CostEstimate(
            flops=2 * samples * count * width, bytes_accessed=4 * samples * count, transcendentals=0
        ),
        name="proxy_grads",
    )(late, early, *flat, picked)


def merge_kernel(flips, swap, *refs):
    ins, out_ref = refs[:-1], refs[-1]
    blocks = out_ref.shape[0] // 2
    for b in range(blocks):
        spots = [swap(f, b) for f in flips]
        tops = [ref[at:at + 1, :] for ref, at in zip(ins, spots)]
        totals = [ref[blocks + at:blocks + at + 1, :] for ref, at in zip(ins, spots)]
        top = functools.reduce(jnp.maximum, tops)
        total = functools.reduce(
            jnp.add, [t * jnp.exp2((m - top) * exp2_scale) for m, t in zip(tops, totals)]
        )
        out_ref[b:b + 1, :] = top
        out_ref[blocks + b:blocks + b + 1, :] = total


def merge(stats, flips, swap):
    return pl.pallas_call(
        functools.partial(merge_kernel, flips, swap),
        out_shape=jax.ShapeDtypeStruct(stats[0].shape, jnp.float32),
        in_specs=[whole] * len(stats),
        out_specs=whole,
        compiler_params=params,
        name="merge_stats",
    )(*stats)


def prep_kernel(part_count, picked_ref, unit_ref, unit_t_ref):
    samples, width = picked_ref.shape
    cols = width // part_count
    n = lax.axis_index("narrow")
    for row in range(0, samples, 256):
        at = slice(row, row + 256)
        if part_count == 1:
            picked = picked_ref[at, :]
        else:
            picked = jnp.concatenate(
                [picked_ref[at, pl.ds(pl.multiple_of((n ^ k) * cols, cols), cols)] for k in range(part_count)],
                axis=1,
            )
        lengths = jnp.sqrt(jnp.sum(picked * picked, axis=1, keepdims=True) + epsilon)
        unit = picked / lengths
        unit_ref[at, :] = unit.astype(jnp.bfloat16)
        unit_t_ref[:, at] = unit.T.astype(jnp.bfloat16)


def prep_call(picked, part_count):
    samples, width = picked.shape
    return pl.pallas_call(
        functools.partial(prep_kernel, part_count),
        out_shape=(
            jax.ShapeDtypeStruct((samples, width), jnp.bfloat16),
            jax.ShapeDtypeStruct((width, samples), jnp.bfloat16),
        ),
        in_specs=[whole],
        out_specs=(whole, whole),
        compiler_params=params,
        cost_estimate=pl.CostEstimate(flops=4 * samples * width, bytes_accessed=8 * samples * width, transcendentals=0),
        name="unit_rows",
    )(picked)


def finish_kernel(*refs):
    ins, out_ref = refs[:-1], refs[-1]
    total = functools.reduce(jnp.add, [ref[...].astype(jnp.float32) for ref in ins])
    out_ref[...] = total.T


def finish_call(own, others):
    return pl.pallas_call(
        finish_kernel,
        out_shape=jax.ShapeDtypeStruct((own.shape[1], own.shape[0]), jnp.float32),
        in_specs=[whole] * (1 + len(others)),
        out_specs=whole,
        compiler_params=params,
        name="feature_sums",
    )(own, *others)


def join_kernel(own_ref, other_ref, out_ref):
    cols = own_ref.shape[1]
    n = lax.axis_index("narrow")
    out_ref[:, pl.ds(pl.multiple_of(n * cols, cols), cols)] = own_ref[...]
    out_ref[:, pl.ds(pl.multiple_of((1 - n) * cols, cols), cols)] = other_ref[...]


def join_call(own, other):
    return pl.pallas_call(
        join_kernel,
        out_shape=jax.ShapeDtypeStruct((own.shape[0], 2 * own.shape[1]), jnp.float32),
        in_specs=[whole] * 2,
        out_specs=whole,
        compiler_params=params,
        name="feature_grad",
    )(own, other)


def make(wide, narrow):
    depth = wide // 4
    sizes = (wide, narrow)
    send = functools.partial(exchange, sizes=sizes)

    def to_t(x):
        return send(x, partner=lambda w, n: (w ^ t_bit(n), n))

    def to_s(x):
        return send(x, partner=lambda w, n: (w ^ s_bit(n), n))

    def to_ts(x):
        return send(x, partner=lambda w, n: (w ^ 3, n))

    def to_z(x, k):
        return send(x, partner=lambda w, n: (w ^ (k << 2), n))

    def to_core(x, k):
        return send(x, partner=lambda w, n: (w, n ^ k))

    def per_device(features, proxies, sample_ids, positives, loss_weight):
        samples = sample_ids.shape[0]
        rows, width = features.shape
        w = lax.axis_index("wide")
        n = lax.axis_index("narrow")
        odd = n % 2

        if narrow == 2:
            cols = width // 2
            part = jnp.where(n == 0, features[:, :cols], features[:, cols:])
        else:
            part = features
        group_j = jnp.concatenate([part] + [to_z(part, k) for k in range(1, depth)], axis=0)
        group_t = to_t(group_j)
        group_s = to_s(group_j)
        group_d = to_s(group_t)
        if narrow == 2:
            groups = [
                (group_j, to_core(group_j, 1)),
                (group_t, to_core(group_s, 1)),
                (group_s, to_core(group_t, 1)),
                (group_d, to_core(group_d, 1)),
            ]
        else:
            groups = [(group_j,), (group_t,), (group_s,), (group_d,)]

        picked = proxies.at[sample_ids].get(mode="promise_in_bounds")
        unit, unit_t = prep_call(picked, 2 if narrow == 2 else 1)
        if narrow != 2:
            unit_t = jnp.take(unit_t.reshape(narrow, width // narrow, samples), n ^ jnp.arange(narrow), axis=0)
            unit_t = unit_t.reshape(width, samples)

        g = jnp.arange(4)[:, None]
        offset = jnp.where(odd == 0, g, (g % 2) * 2 + g // 2) + 4 * jnp.arange(depth)[None, :]
        order = (w ^ offset).reshape(-1)
        base = (w * narrow + n) * samples
        spots = jnp.take(positives.reshape(wide, rows), order, axis=0) - base
        weight = jnp.take(loss_weight.reshape(wide, rows), order, axis=0)

        shifted_early, stats_early = logits_call(unit, groups[:3])
        shifted_late, stats_late = logits_call(unit, groups[3:])
        own = jnp.concatenate([stats_early, stats_late], axis=1).reshape(2 * wide, rows)
        stats = own
        for bit in range(narrow.bit_length() - 1):
            def swap_groups(flip, b):
                g, z = divmod(b, depth)
                return ((g % 2) * 2 + g // 2) * depth + z if flip else b
            stats = merge([stats, to_core(stats, 1 << bit)], (0, int(bit == 0)), swap_groups)
        others = [to_z(stats, k) for k in range(1, depth)]
        stats = merge([stats] + others, tuple(range(depth)), lambda k, b: b ^ k)
        others = [to_t(stats), to_s(stats), to_ts(stats)]
        stats = merge([stats] + others, (0, 1, 2, 3), lambda k, b: b ^ (k * depth))
        scale = jnp.exp2((own[:wide] - stats[:wide]) * exp2_scale) / stats[wide:]

        per = depth * rows // chunk
        order_t, order_s, order_j = range(per, 2 * per), range(2 * per, 3 * per), range(per)
        grad_d, keep_d, send_d = grad_call(
            unit_t, shifted_late, scale, weight, spots, 3 * per, tuple(range(3 * per, 4 * per))
        )
        unit_t, send_d = lax.optimization_barrier((unit_t, send_d))
        grad_r, keep_r, send_r = grad_call(
            unit_t, shifted_early, scale, weight, spots, 0, (*order_t, *order_s, *order_j)
        )
        size = depth * rows

        low = jnp.bfloat16

        def within(keep, out, names):
            keep = {k: keep[:, i * size:(i + 1) * size] for i, k in enumerate(names)}
            for bit in range(narrow.bit_length() - 2, -1, -1):
                other = to_core(out, 1 << bit)
                there = dict(T="S", S="T") if bit == 0 else {}
                for k in names:
                    i = names.index(there.get(k, k))
                    keep[k] = keep[k] + other[:, i * size:(i + 1) * size].astype(jnp.float32)
                if bit:
                    half = keep[names[0]].shape[0] // 2
                    out = jnp.concatenate([keep[k][half:].astype(low) for k in names], axis=1)
                    keep = {k: v[:half] for k, v in keep.items()}
            return keep

        sum_d = within(keep_d, send_d, "D")["D"]
        from_d = to_s(sum_d.astype(low)).astype(jnp.float32)
        sums = within(keep_r, send_r, "TSJ")
        from_s = to_s(sums["S"].astype(low))
        from_t = to_t((sums["T"] + from_d).astype(low))
        proxy_grad = proxy_call(grad_d, grad_r, [groups[3], groups[1], groups[2], groups[0]], picked)
        from_s, proxy_grad = lax.optimization_barrier((from_s, proxy_grad))
        sum_j = sums["J"] + from_t.astype(jnp.float32) + from_s.astype(jnp.float32)
        others = [to_z(sum_j[:, k * rows:(k + 1) * rows].astype(low), k) for k in range(1, depth)]
        mine = finish_call(sum_j[:, :rows], others)
        if narrow == 2:
            feature_grad = join_call(mine, to_core(mine, 1))
        else:
            mine = mine[None]
            for bit in range(narrow.bit_length() - 1):
                mine = jnp.concatenate([mine, to_core(mine, 1 << bit)], axis=0)
            feature_grad = jnp.take(mine, n ^ jnp.arange(narrow), axis=0).transpose(1, 0, 2).reshape(rows, width)
        return (feature_grad, proxy_grad)

    return per_device


def solution(mesh):
    placed = (P("wide", None), P(("wide", "narrow"), None), P(("wide", "narrow")), P(), P())
    return jax.shard_map(
        make(mesh.shape["wide"], mesh.shape["narrow"]),
        mesh=mesh,
        in_specs=placed,
        out_specs=(P("wide", None), P(("wide", "narrow"), None)),
        check_vma=False,
    )
```

```python
import functools
import math

import jax
import jax.numpy as jnp
from jax import lax
from jax.experimental import pallas as pl
from jax.experimental.pallas import tpu as pltpu
from jax.sharding import PartitionSpec as P

logit_scale = 3.0
epsilon = 1e-06
exp2_scale = logit_scale * math.log2(math.e)
chunk = 256
both = ("wide", "narrow")
whole = pl.BlockSpec(memory_space=pltpu.VMEM)
params = pltpu.CompilerParams(vmem_limit_bytes=8 * 1024 * 1024)


def t_bit(n):
    return 1 if n % 2 == 0 else 2


def s_bit(n):
    return 3 - t_bit(n)


def exchange(x, sizes, partner):
    wide, narrow = sizes
    pairs = []
    for w in range(wide):
        for n in range(narrow):
            pw, pn = partner(w, n)
            pairs.append((w * narrow + n, pw * narrow + pn))
    return lax.ppermute(x, both, pairs)


def logits_kernel(group_count, part_count, unit_ref, *refs):
    parts = refs[: group_count * part_count]
    shifted_ref, stats_ref = refs[group_count * part_count:]
    step = 0
    for g in range(group_count):
        group = parts[g * part_count:(g + 1) * part_count]
        cols = group[0].shape[1]
        for row in range(0, group[0].shape[0], chunk):
            dots = None
            for k, part in enumerate(group):
                prod = lax.dot_general(
                    unit_ref[:, k * cols:(k + 1) * cols], part[row:row + chunk, :],
                    (((1,), (1,)), ((), ())), preferred_element_type=jnp.float32,
                )
                dots = prod if dots is None else dots + prod
            top = jnp.max(dots, axis=0, keepdims=True)
            shifted = jnp.exp2((dots - top) * exp2_scale)
            total = jnp.sum(shifted, axis=0, keepdims=True)
            shifted_ref[:, step * chunk:(step + 1) * chunk] = shifted
            for b in range(chunk // 128):
                at = step * (chunk // 128) + b
                stats_ref[0, at:at + 1, :] = top[:, b * 128:(b + 1) * 128]
                stats_ref[1, at:at + 1, :] = total[:, b * 128:(b + 1) * 128]
            step += 1


def logits_call(unit, groups):
    rows = groups[0][0].shape[0]
    count = len(groups) * rows
    samples = unit.shape[0]
    flat = [part for group in groups for part in group]
    return pl.pallas_call(
        functools.partial(logits_kernel, len(groups), len(groups[0])),
        out_shape=(
            jax.ShapeDtypeStruct((samples, count), jnp.float32),
            jax.ShapeDtypeStruct((2, count // 128, 128), jnp.float32),
        ),
        in_specs=[whole] * (1 + len(flat)),
        out_specs=(whole, whole),
        compiler_params=params,
        cost_estimate=pl.CostEstimate(
            flops=2 * samples * count * unit.shape[1],
            bytes_accessed=4 * samples * count,
            transcendentals=samples * count,
        ),
        name="logits",
    )(unit, *flat)


def grad_kernel(first, steps, unit_t_ref, shifted_ref, scale_ref, weight_ref, at_ref, grad_ref, keep_ref, send_ref):
    samples = shifted_ref.shape[0]
    half = unit_t_ref.shape[0] // 2
    per = chunk // 128
    cand = lax.broadcasted_iota(jnp.int32, (samples, chunk), 0)

    def row(ref, at):
        return jnp.concatenate([ref[at + b:at + b + 1, :] for b in range(per)], axis=1)

    for out, at in enumerate(steps):
        cols = slice((at - first) * chunk, (at - first + 1) * chunk)
        scale, weight, spot = row(scale_ref, at * per), row(weight_ref, at * per), row(at_ref, at * per)
        soft = shifted_ref[:, cols] * scale
        grad = (weight * jnp.where(cand == spot, soft - 1.0, soft)).astype(jnp.bfloat16)
        out_cols = slice(out * chunk, (out + 1) * chunk)
        grad_ref[:, out_cols] = grad
        shares = logit_scale * jnp.dot(unit_t_ref[...], grad, preferred_element_type=jnp.float32)
        keep_ref[:, out_cols] = shares[:half]
        send_ref[:, out_cols] = shares[half:].astype(jnp.bfloat16)


def grad_call(unit_t, shifted, scale, weight, spots, first, steps):
    samples = shifted.shape[0]
    width = unit_t.shape[0]
    count = len(steps) * chunk
    return pl.pallas_call(
        functools.partial(grad_kernel, first, steps),
        out_shape=(
            jax.ShapeDtypeStruct((samples, count), jnp.bfloat16),
            jax.ShapeDtypeStruct((width // 2, count), jnp.float32),
            jax.ShapeDtypeStruct((width // 2, count), jnp.bfloat16),
        ),
        in_specs=[whole] * 5,
        out_specs=(whole,) * 3,
        compiler_params=params,
        cost_estimate=pl.CostEstimate(
            flops=2 * samples * count * width, bytes_accessed=6 * samples * count, transcendentals=0
        ),
        name="grads",
    )(unit_t, shifted, scale, weight, spots)


def proxy_kernel(group_count, part_count, rows, late_ref, early_ref, *refs):
    parts = refs[:group_count * part_count]
    picked_ref, out_ref = refs[group_count * part_count:]
    size, cols = parts[0].shape
    grads = [late_ref] + [early_ref.at[:, g * size:(g + 1) * size] for g in range(group_count - 1)]
    n = lax.axis_index("narrow")
    places = []
    for k in range(part_count):
        if part_count == 1:
            places.append(slice(0, cols))
        else:
            places.append(pl.ds(pl.multiple_of((n ^ k) * cols, cols), cols))
    for row in range(0, picked_ref.shape[0], rows):
        at = slice(row, row + rows)
        sums = []
        for k in range(part_count):
            total = None
            for g in range(group_count):
                prod = jnp.dot(
                    grads[g][at, :], parts[g * part_count + k][...], preferred_element_type=jnp.float32
                )
                total = prod if total is None else total + prod
            sums.append(logit_scale * total)
        picked = [picked_ref[at, place] for place in places]
        square = functools.reduce(jnp.add, [jnp.sum(p * p, axis=1, keepdims=True) for p in picked])
        inverse = 1.0 / jnp.sqrt(square + epsilon)
        inner = functools.reduce(jnp.add, [jnp.sum(p * s, axis=1, keepdims=True) for p, s in zip(picked, sums)])
        slope = inner * inverse * inverse
        for place, p, s in zip(places, picked, sums):
            out_ref[at, place] = (s - p * slope) * inverse


def proxy_call(late, early, groups, picked):
    samples, width = picked.shape
    count = late.shape[1] + early.shape[1]
    flat = [part for group in groups for part in group]
    return pl.pallas_call(
        functools.partial(proxy_kernel, len(groups), len(groups[0]), 256),
        out_shape=jax.ShapeDtypeStruct((samples, width), jnp.float32),
        in_specs=[whole] * (len(flat) + 3),
        out_specs=whole,
        compiler_params=params,
        cost_estimate=pl.CostEstimate(
            flops=2 * samples * count * width, bytes_accessed=4 * samples * count, transcendentals=0
        ),
        name="proxy_grads",
    )(late, early, *flat, picked)


def merge_kernel(flips, swap, *refs):
    ins, out_ref = refs[:-1], refs[-1]
    blocks = out_ref.shape[0] // 2
    for b in range(blocks):
        spots = [swap(f, b) for f in flips]
        tops = [ref[at:at + 1, :] for ref, at in zip(ins, spots)]
        totals = [ref[blocks + at:blocks + at + 1, :] for ref, at in zip(ins, spots)]
        top = functools.reduce(jnp.maximum, tops)
        total = functools.reduce(
            jnp.add, [t * jnp.exp2((m - top) * exp2_scale) for m, t in zip(tops, totals)]
        )
        out_ref[b:b + 1, :] = top
        out_ref[blocks + b:blocks + b + 1, :] = total


def merge(stats, flips, swap):
    return pl.pallas_call(
        functools.partial(merge_kernel, flips, swap),
        out_shape=jax.ShapeDtypeStruct(stats[0].shape, jnp.float32),
        in_specs=[whole] * len(stats),
        out_specs=whole,
        compiler_params=params,
        name="merge_stats",
    )(*stats)


def prep_kernel(part_count, picked_ref, unit_ref, unit_t_ref):
    samples, width = picked_ref.shape
    cols = width // part_count
    n = lax.axis_index("narrow")
    for row in range(0, samples, 256):
        at = slice(row, row + 256)
        if part_count == 1:
            picked = picked_ref[at, :]
        else:
            picked = jnp.concatenate(
                [picked_ref[at, pl.ds(pl.multiple_of((n ^ k) * cols, cols), cols)] for k in range(part_count)],
                axis=1,
            )
        lengths = jnp.sqrt(jnp.sum(picked * picked, axis=1, keepdims=True) + epsilon)
        unit = picked / lengths
        unit_ref[at, :] = unit.astype(jnp.bfloat16)
        unit_t_ref[:, at] = unit.T.astype(jnp.bfloat16)


def prep_call(picked, part_count):
    samples, width = picked.shape
    return pl.pallas_call(
        functools.partial(prep_kernel, part_count),
        out_shape=(
            jax.ShapeDtypeStruct((samples, width), jnp.bfloat16),
            jax.ShapeDtypeStruct((width, samples), jnp.bfloat16),
        ),
        in_specs=[whole],
        out_specs=(whole, whole),
        compiler_params=params,
        cost_estimate=pl.CostEstimate(flops=4 * samples * width, bytes_accessed=8 * samples * width, transcendentals=0),
        name="unit_rows",
    )(picked)


def finish_kernel(*refs):
    ins, out_ref = refs[:-1], refs[-1]
    total = functools.reduce(jnp.add, [ref[...].astype(jnp.float32) for ref in ins])
    out_ref[...] = total.T


def finish_call(own, others):
    return pl.pallas_call(
        finish_kernel,
        out_shape=jax.ShapeDtypeStruct((own.shape[1], own.shape[0]), jnp.float32),
        in_specs=[whole] * (1 + len(others)),
        out_specs=whole,
        compiler_params=params,
        name="feature_sums",
    )(own, *others)


def join_kernel(own_ref, other_ref, out_ref):
    cols = own_ref.shape[1]
    n = lax.axis_index("narrow")
    out_ref[:, pl.ds(pl.multiple_of(n * cols, cols), cols)] = own_ref[...]
    out_ref[:, pl.ds(pl.multiple_of((1 - n) * cols, cols), cols)] = other_ref[...]


def join_call(own, other):
    return pl.pallas_call(
        join_kernel,
        out_shape=jax.ShapeDtypeStruct((own.shape[0], 2 * own.shape[1]), jnp.float32),
        in_specs=[whole] * 2,
        out_specs=whole,
        compiler_params=params,
        name="feature_grad",
    )(own, other)


def make(wide, narrow):
    depth = wide // 4
    sizes = (wide, narrow)
    send = functools.partial(exchange, sizes=sizes)

    def to_t(x):
        return send(x, partner=lambda w, n: (w ^ t_bit(n), n))

    def to_s(x):
        return send(x, partner=lambda w, n: (w ^ s_bit(n), n))

    def to_ts(x):
        return send(x, partner=lambda w, n: (w ^ 3, n))

    def to_z(x, k):
        return send(x, partner=lambda w, n: (w ^ (k << 2), n))

    def to_core(x, k):
        return send(x, partner=lambda w, n: (w, n ^ k))

    def per_device(features, proxies, sample_ids, positives, loss_weight):
        samples = sample_ids.shape[0]
        rows, width = features.shape
        w = lax.axis_index("wide")
        n = lax.axis_index("narrow")
        odd = n % 2

        if narrow == 2:
            cols = width // 2
            part = jnp.where(n == 0, features[:, :cols], features[:, cols:])
        else:
            part = features
        picked = proxies.at[sample_ids].get(mode="promise_in_bounds")
        zs = [to_z(part, k) for k in range(1, depth)]
        *zs, picked = lax.optimization_barrier((*zs, picked))
        group_j = jnp.concatenate([part] + zs, axis=0)
        group_t, group_s = lax.optimization_barrier((to_t(group_j), to_s(group_j)))
        group_d = to_s(group_t)
        groups = [(group_j,), (group_t,), (group_s,)]
        if narrow == 2:
            others = [to_core(group_j, 1), to_core(group_s, 1), to_core(group_t, 1)]
            groups = [(*group, other) for group, other in zip(groups, others)]

        unit, unit_t = prep_call(picked, 2 if narrow == 2 else 1)
        if narrow != 2:
            unit_t = jnp.take(unit_t.reshape(narrow, width // narrow, samples), n ^ jnp.arange(narrow), axis=0)
            unit_t = unit_t.reshape(width, samples)

        g = jnp.arange(4)[:, None]
        offset = jnp.where(odd == 0, g, (g % 2) * 2 + g // 2) + 4 * jnp.arange(depth)[None, :]
        order = (w ^ offset).reshape(-1)
        base = (w * narrow + n) * samples
        spots = jnp.take(positives.reshape(wide, rows), order, axis=0) - base
        weight = jnp.take(loss_weight.reshape(wide, rows), order, axis=0)

        shifted_early, stats_early = logits_call(unit, groups)
        group_d, stats_early = lax.optimization_barrier((group_d, stats_early))
        groups.append((group_d, to_core(group_d, 1)) if narrow == 2 else (group_d,))
        shifted_late, stats_late = logits_call(unit, groups[3:])
        own = jnp.concatenate([stats_early, stats_late], axis=1).reshape(2 * wide, rows)
        stats = own
        for bit in range(narrow.bit_length() - 1):
            def swap_groups(flip, b):
                g, z = divmod(b, depth)
                return ((g % 2) * 2 + g // 2) * depth + z if flip else b
            stats = merge([stats, to_core(stats, 1 << bit)], (0, int(bit == 0)), swap_groups)
        others = [to_z(stats, k) for k in range(1, depth)]
        stats = merge([stats] + others, tuple(range(depth)), lambda k, b: b ^ k)
        others = [to_t(stats), to_s(stats), to_ts(stats)]
        stats = merge([stats] + others, (0, 1, 2, 3), lambda k, b: b ^ (k * depth))
        scale = jnp.exp2((own[:wide] - stats[:wide]) * exp2_scale) / stats[wide:]

        per = depth * rows // chunk
        order_t, order_s, order_j = range(per, 2 * per), range(2 * per, 3 * per), range(per)
        grad_d, keep_d, send_d = grad_call(
            unit_t, shifted_late, scale, weight, spots, 3 * per, tuple(range(3 * per, 4 * per))
        )
        size = depth * rows
        low = jnp.bfloat16

        def within(keep, out, names):
            keep = {k: keep[:, i * size:(i + 1) * size] for i, k in enumerate(names)}
            for bit in range(narrow.bit_length() - 2, -1, -1):
                other = to_core(out, 1 << bit)
                there = dict(T="S", S="T") if bit == 0 else {}
                for k in names:
                    i = names.index(there.get(k, k))
                    keep[k] = keep[k] + other[:, i * size:(i + 1) * size].astype(jnp.float32)
                if bit:
                    half = keep[names[0]].shape[0] // 2
                    out = jnp.concatenate([keep[k][half:].astype(low) for k in names], axis=1)
                    keep = {k: v[:half] for k, v in keep.items()}
            return keep

        sum_d = within(keep_d, send_d, "D")["D"].astype(low)
        unit_t, sum_d = lax.optimization_barrier((unit_t, sum_d))
        grad_r, keep_r, send_r = grad_call(
            unit_t, shifted_early, scale, weight, spots, 0, (*order_t, *order_s, *order_j)
        )
        from_d = to_s(sum_d).astype(jnp.float32)
        sums = within(keep_r, send_r, "TSJ")
        from_s = to_s(sums["S"].astype(low))
        from_t = to_t((sums["T"] + from_d).astype(low))
        proxy_grad = proxy_call(grad_d, grad_r, [groups[3], groups[1], groups[2], groups[0]], picked)
        from_s, proxy_grad = lax.optimization_barrier((from_s, proxy_grad))
        sum_j = sums["J"] + from_t.astype(jnp.float32) + from_s.astype(jnp.float32)
        others = [to_z(sum_j[:, k * rows:(k + 1) * rows].astype(low), k) for k in range(1, depth)]
        mine = finish_call(sum_j[:, :rows], others)
        if narrow == 2:
            feature_grad = join_call(mine, to_core(mine, 1))
        else:
            mine = mine[None]
            for bit in range(narrow.bit_length() - 1):
                mine = jnp.concatenate([mine, to_core(mine, 1 << bit)], axis=0)
            feature_grad = jnp.take(mine, n ^ jnp.arange(narrow), axis=0).transpose(1, 0, 2).reshape(rows, width)
        return (feature_grad, proxy_grad)

    return per_device


def solution(mesh):
    placed = (P("wide", None), P(("wide", "narrow"), None), P(("wide", "narrow")), P(), P())
    return jax.shard_map(
        make(mesh.shape["wide"], mesh.shape["narrow"]),
        mesh=mesh,
        in_specs=placed,
        out_specs=(P("wide", None), P(("wide", "narrow"), None)),
        check_vma=False,
    )
```

```python
import functools
import math

import jax
import jax.numpy as jnp
from jax import lax
from jax.experimental import pallas as pl
from jax.experimental.pallas import tpu as pltpu
from jax.sharding import PartitionSpec as P

logit_scale = 3.0
epsilon = 1e-06
exp2_scale = logit_scale * math.log2(math.e)
chunk = 256
both = ("wide", "narrow")
whole = pl.BlockSpec(memory_space=pltpu.VMEM)
params = pltpu.CompilerParams(vmem_limit_bytes=8 * 1024 * 1024)


def t_bit(n):
    return 1 if n % 2 == 0 else 2


def s_bit(n):
    return 3 - t_bit(n)


def exchange(x, sizes, partner):
    wide, narrow = sizes
    pairs = []
    for w in range(wide):
        for n in range(narrow):
            pw, pn = partner(w, n)
            pairs.append((w * narrow + n, pw * narrow + pn))
    return lax.ppermute(x, both, pairs)


def logits_kernel(group_count, part_count, unit_ref, *refs):
    parts = refs[: group_count * part_count]
    shifted_ref, stats_ref = refs[group_count * part_count:]
    step = 0
    for g in range(group_count):
        group = parts[g * part_count:(g + 1) * part_count]
        cols = group[0].shape[1]
        for row in range(0, group[0].shape[0], chunk):
            dots = None
            for k, part in enumerate(group):
                prod = lax.dot_general(
                    unit_ref[:, k * cols:(k + 1) * cols], part[row:row + chunk, :],
                    (((1,), (1,)), ((), ())), preferred_element_type=jnp.float32,
                )
                dots = prod if dots is None else dots + prod
            top = jnp.max(dots, axis=0, keepdims=True)
            shifted = jnp.exp2((dots - top) * exp2_scale)
            total = jnp.sum(shifted, axis=0, keepdims=True)
            shifted_ref[:, step * chunk:(step + 1) * chunk] = shifted.astype(jnp.bfloat16)
            for b in range(chunk // 128):
                at = step * (chunk // 128) + b
                stats_ref[0, at:at + 1, :] = top[:, b * 128:(b + 1) * 128]
                stats_ref[1, at:at + 1, :] = total[:, b * 128:(b + 1) * 128]
            step += 1


def logits_call(unit, groups):
    rows = groups[0][0].shape[0]
    count = len(groups) * rows
    samples = unit.shape[0]
    flat = [part for group in groups for part in group]
    return pl.pallas_call(
        functools.partial(logits_kernel, len(groups), len(groups[0])),
        out_shape=(
            jax.ShapeDtypeStruct((samples, count), jnp.bfloat16),
            jax.ShapeDtypeStruct((2, count // 128, 128), jnp.float32),
        ),
        in_specs=[whole] * (1 + len(flat)),
        out_specs=(whole, whole),
        compiler_params=params,
        cost_estimate=pl.CostEstimate(
            flops=2 * samples * count * unit.shape[1],
            bytes_accessed=4 * samples * count,
            transcendentals=samples * count,
        ),
        name="logits",
    )(unit, *flat)


def grad_kernel(first, steps, unit_t_ref, shifted_ref, scale_ref, weight_ref, at_ref, grad_ref, keep_ref, send_ref):
    samples = shifted_ref.shape[0]
    half = unit_t_ref.shape[0] // 2
    per = chunk // 128
    cand = lax.broadcasted_iota(jnp.int32, (samples, chunk), 0)

    def row(ref, at):
        return jnp.concatenate([ref[at + b:at + b + 1, :] for b in range(per)], axis=1)

    for out, at in enumerate(steps):
        cols = slice((at - first) * chunk, (at - first + 1) * chunk)
        scale, weight, spot = row(scale_ref, at * per), row(weight_ref, at * per), row(at_ref, at * per)
        soft = shifted_ref[:, cols].astype(jnp.float32) * scale
        grad = (weight * jnp.where(cand == spot, soft - 1.0, soft)).astype(jnp.bfloat16)
        out_cols = slice(out * chunk, (out + 1) * chunk)
        grad_ref[:, out_cols] = grad
        shares = logit_scale * jnp.dot(unit_t_ref[...], grad, preferred_element_type=jnp.float32)
        keep_ref[:, out_cols] = shares[:half]
        send_ref[:, out_cols] = shares[half:].astype(jnp.bfloat16)


def grad_call(unit_t, shifted, scale, weight, spots, first, steps):
    samples = shifted.shape[0]
    width = unit_t.shape[0]
    count = len(steps) * chunk
    return pl.pallas_call(
        functools.partial(grad_kernel, first, steps),
        out_shape=(
            jax.ShapeDtypeStruct((samples, count), jnp.bfloat16),
            jax.ShapeDtypeStruct((width // 2, count), jnp.float32),
            jax.ShapeDtypeStruct((width // 2, count), jnp.bfloat16),
        ),
        in_specs=[whole] * 5,
        out_specs=(whole,) * 3,
        compiler_params=params,
        cost_estimate=pl.CostEstimate(
            flops=2 * samples * count * width, bytes_accessed=6 * samples * count, transcendentals=0
        ),
        name="grads",
    )(unit_t, shifted, scale, weight, spots)


def proxy_kernel(group_count, part_count, rows, late_ref, early_ref, *refs):
    parts = refs[:group_count * part_count]
    picked_ref, out_ref = refs[group_count * part_count:]
    size, cols = parts[0].shape
    grads = [late_ref] + [early_ref.at[:, g * size:(g + 1) * size] for g in range(group_count - 1)]
    n = lax.axis_index("narrow")
    places = []
    for k in range(part_count):
        if part_count == 1:
            places.append(slice(0, cols))
        else:
            places.append(pl.ds(pl.multiple_of((n ^ k) * cols, cols), cols))
    for row in range(0, picked_ref.shape[0], rows):
        at = slice(row, row + rows)
        sums = []
        for k in range(part_count):
            total = None
            for g in range(group_count):
                prod = jnp.dot(
                    grads[g][at, :], parts[g * part_count + k][...], preferred_element_type=jnp.float32
                )
                total = prod if total is None else total + prod
            sums.append(logit_scale * total)
        picked = [picked_ref[at, place] for place in places]
        square = functools.reduce(jnp.add, [jnp.sum(p * p, axis=1, keepdims=True) for p in picked])
        inverse = 1.0 / jnp.sqrt(square + epsilon)
        inner = functools.reduce(jnp.add, [jnp.sum(p * s, axis=1, keepdims=True) for p, s in zip(picked, sums)])
        slope = inner * inverse * inverse
        for place, p, s in zip(places, picked, sums):
            out_ref[at, place] = (s - p * slope) * inverse


def proxy_call(late, early, groups, picked):
    samples, width = picked.shape
    count = late.shape[1] + early.shape[1]
    flat = [part for group in groups for part in group]
    return pl.pallas_call(
        functools.partial(proxy_kernel, len(groups), len(groups[0]), 256),
        out_shape=jax.ShapeDtypeStruct((samples, width), jnp.float32),
        in_specs=[whole] * (len(flat) + 3),
        out_specs=whole,
        compiler_params=params,
        cost_estimate=pl.CostEstimate(
            flops=2 * samples * count * width, bytes_accessed=4 * samples * count, transcendentals=0
        ),
        name="proxy_grads",
    )(late, early, *flat, picked)


def merge_kernel(flips, swap, *refs):
    ins, out_ref = refs[:-1], refs[-1]
    blocks = out_ref.shape[0] // 2
    for b in range(blocks):
        spots = [swap(f, b) for f in flips]
        tops = [ref[at:at + 1, :] for ref, at in zip(ins, spots)]
        totals = [ref[blocks + at:blocks + at + 1, :] for ref, at in zip(ins, spots)]
        top = functools.reduce(jnp.maximum, tops)
        total = functools.reduce(
            jnp.add, [t * jnp.exp2((m - top) * exp2_scale) for m, t in zip(tops, totals)]
        )
        out_ref[b:b + 1, :] = top
        out_ref[blocks + b:blocks + b + 1, :] = total


def merge(stats, flips, swap):
    return pl.pallas_call(
        functools.partial(merge_kernel, flips, swap),
        out_shape=jax.ShapeDtypeStruct(stats[0].shape, jnp.float32),
        in_specs=[whole] * len(stats),
        out_specs=whole,
        compiler_params=params,
        name="merge_stats",
    )(*stats)


def prep_kernel(part_count, picked_ref, unit_ref, unit_t_ref):
    samples, width = picked_ref.shape
    cols = width // part_count
    n = lax.axis_index("narrow")
    for row in range(0, samples, 256):
        at = slice(row, row + 256)
        if part_count == 1:
            picked = picked_ref[at, :]
        else:
            picked = jnp.concatenate(
                [picked_ref[at, pl.ds(pl.multiple_of((n ^ k) * cols, cols), cols)] for k in range(part_count)],
                axis=1,
            )
        lengths = jnp.sqrt(jnp.sum(picked * picked, axis=1, keepdims=True) + epsilon)
        unit = picked / lengths
        unit_ref[at, :] = unit.astype(jnp.bfloat16)
        unit_t_ref[:, at] = unit.T.astype(jnp.bfloat16)


def prep_call(picked, part_count):
    samples, width = picked.shape
    return pl.pallas_call(
        functools.partial(prep_kernel, part_count),
        out_shape=(
            jax.ShapeDtypeStruct((samples, width), jnp.bfloat16),
            jax.ShapeDtypeStruct((width, samples), jnp.bfloat16),
        ),
        in_specs=[whole],
        out_specs=(whole, whole),
        compiler_params=params,
        cost_estimate=pl.CostEstimate(flops=4 * samples * width, bytes_accessed=8 * samples * width, transcendentals=0),
        name="unit_rows",
    )(picked)


def finish_kernel(*refs):
    ins, out_ref = refs[:-1], refs[-1]
    total = functools.reduce(jnp.add, [ref[...].astype(jnp.float32) for ref in ins])
    out_ref[...] = total.T


def finish_call(own, others):
    return pl.pallas_call(
        finish_kernel,
        out_shape=jax.ShapeDtypeStruct((own.shape[1], own.shape[0]), jnp.float32),
        in_specs=[whole] * (1 + len(others)),
        out_specs=whole,
        compiler_params=params,
        name="feature_sums",
    )(own, *others)


def join_kernel(own_ref, other_ref, out_ref):
    cols = own_ref.shape[1]
    n = lax.axis_index("narrow")
    out_ref[:, pl.ds(pl.multiple_of(n * cols, cols), cols)] = own_ref[...]
    out_ref[:, pl.ds(pl.multiple_of((1 - n) * cols, cols), cols)] = other_ref[...]


def join_call(own, other):
    return pl.pallas_call(
        join_kernel,
        out_shape=jax.ShapeDtypeStruct((own.shape[0], 2 * own.shape[1]), jnp.float32),
        in_specs=[whole] * 2,
        out_specs=whole,
        compiler_params=params,
        name="feature_grad",
    )(own, other)


def make(wide, narrow):
    depth = wide // 4
    sizes = (wide, narrow)
    send = functools.partial(exchange, sizes=sizes)

    def to_t(x):
        return send(x, partner=lambda w, n: (w ^ t_bit(n), n))

    def to_s(x):
        return send(x, partner=lambda w, n: (w ^ s_bit(n), n))

    def to_ts(x):
        return send(x, partner=lambda w, n: (w ^ 3, n))

    def to_z(x, k):
        return send(x, partner=lambda w, n: (w ^ (k << 2), n))

    def to_core(x, k):
        return send(x, partner=lambda w, n: (w, n ^ k))

    def per_device(features, proxies, sample_ids, positives, loss_weight):
        samples = sample_ids.shape[0]
        rows, width = features.shape
        w = lax.axis_index("wide")
        n = lax.axis_index("narrow")
        odd = n % 2

        if narrow == 2:
            cols = width // 2
            part = jnp.where(n == 0, features[:, :cols], features[:, cols:])
        else:
            part = features
        picked = proxies.at[sample_ids].get(mode="promise_in_bounds")
        zs = [to_z(part, k) for k in range(1, depth)]
        *zs, picked = lax.optimization_barrier((*zs, picked))
        group_j = jnp.concatenate([part] + zs, axis=0)
        group_t, group_s = lax.optimization_barrier((to_t(group_j), to_s(group_j)))
        group_d = to_s(group_t)
        groups = [(group_j,), (group_t,), (group_s,)]
        if narrow == 2:
            others = [to_core(group_j, 1), to_core(group_s, 1), to_core(group_t, 1)]
            groups = [(*group, other) for group, other in zip(groups, others)]

        unit, unit_t = prep_call(picked, 2 if narrow == 2 else 1)
        if narrow != 2:
            unit_t = jnp.take(unit_t.reshape(narrow, width // narrow, samples), n ^ jnp.arange(narrow), axis=0)
            unit_t = unit_t.reshape(width, samples)

        g = jnp.arange(4)[:, None]
        offset = jnp.where(odd == 0, g, (g % 2) * 2 + g // 2) + 4 * jnp.arange(depth)[None, :]
        order = (w ^ offset).reshape(-1)
        base = (w * narrow + n) * samples
        spots = jnp.take(positives.reshape(wide, rows), order, axis=0) - base
        weight = jnp.take(loss_weight.reshape(wide, rows), order, axis=0)

        shifted_early, stats_early = logits_call(unit, groups)
        group_d, stats_early = lax.optimization_barrier((group_d, stats_early))
        groups.append((group_d, to_core(group_d, 1)) if narrow == 2 else (group_d,))
        shifted_late, stats_late = logits_call(unit, groups[3:])
        own = jnp.concatenate([stats_early, stats_late], axis=1).reshape(2 * wide, rows)
        stats = own
        for bit in range(narrow.bit_length() - 1):
            def swap_groups(flip, b):
                g, z = divmod(b, depth)
                return ((g % 2) * 2 + g // 2) * depth + z if flip else b
            stats = merge([stats, to_core(stats, 1 << bit)], (0, int(bit == 0)), swap_groups)
        far = w ^ jnp.arange(wide)
        low_bits = jnp.where(odd == 0, far % 4, (far % 2) * 2 + far // 2 % 2)
        place = low_bits * depth + far // 4
        blocks = jnp.take(stats.reshape(2, wide, rows), place, axis=1).transpose(1, 0, 2)
        blocks = lax.all_to_all(blocks, "wide", 0, 0)
        top = jnp.max(blocks[:, 0], axis=0)
        total = jnp.sum(blocks[:, 1] * jnp.exp2((blocks[:, 0] - top) * exp2_scale), axis=0)
        blocks = jnp.broadcast_to(jnp.stack([top, total])[None], blocks.shape)
        blocks = lax.all_to_all(blocks, "wide", 0, 0)
        stats = jnp.take(blocks, order, axis=0).transpose(1, 0, 2).reshape(2 * wide, rows)
        scale = jnp.exp2((own[:wide] - stats[:wide]) * exp2_scale) / stats[wide:]

        per = depth * rows // chunk
        order_t, order_s, order_j = range(per, 2 * per), range(2 * per, 3 * per), range(per)
        grad_d, keep_d, send_d = grad_call(
            unit_t, shifted_late, scale, weight, spots, 3 * per, tuple(range(3 * per, 4 * per))
        )
        size = depth * rows
        low = jnp.bfloat16

        def within(keep, out, names):
            keep = {k: keep[:, i * size:(i + 1) * size] for i, k in enumerate(names)}
            for bit in range(narrow.bit_length() - 2, -1, -1):
                other = to_core(out, 1 << bit)
                there = dict(T="S", S="T") if bit == 0 else {}
                for k in names:
                    i = names.index(there.get(k, k))
                    keep[k] = keep[k] + other[:, i * size:(i + 1) * size].astype(jnp.float32)
                if bit:
                    half = keep[names[0]].shape[0] // 2
                    out = jnp.concatenate([keep[k][half:].astype(low) for k in names], axis=1)
                    keep = {k: v[:half] for k, v in keep.items()}
            return keep

        sum_d = within(keep_d, send_d, "D")["D"].astype(low)
        unit_t, sum_d = lax.optimization_barrier((unit_t, sum_d))
        grad_r, keep_r, send_r = grad_call(
            unit_t, shifted_early, scale, weight, spots, 0, (*order_t, *order_s, *order_j)
        )
        from_d = to_s(sum_d).astype(jnp.float32)
        sums = within(keep_r, send_r, "TSJ")
        from_s = to_s(sums["S"].astype(low))
        from_t = to_t((sums["T"] + from_d).astype(low))
        proxy_grad = proxy_call(grad_d, grad_r, [groups[3], groups[1], groups[2], groups[0]], picked)
        from_s, proxy_grad = lax.optimization_barrier((from_s, proxy_grad))
        sum_j = sums["J"] + from_t.astype(jnp.float32) + from_s.astype(jnp.float32)
        others = [to_z(sum_j[:, k * rows:(k + 1) * rows].astype(low), k) for k in range(1, depth)]
        mine = finish_call(sum_j[:, :rows], others)
        if narrow == 2:
            feature_grad = join_call(mine, to_core(mine, 1))
        else:
            mine = mine[None]
            for bit in range(narrow.bit_length() - 1):
                mine = jnp.concatenate([mine, to_core(mine, 1 << bit)], axis=0)
            feature_grad = jnp.take(mine, n ^ jnp.arange(narrow), axis=0).transpose(1, 0, 2).reshape(rows, width)
        return (feature_grad, proxy_grad)

    return per_device


def solution(mesh):
    placed = (P("wide", None), P(("wide", "narrow"), None), P(("wide", "narrow")), P(), P())
    return jax.shard_map(
        make(mesh.shape["wide"], mesh.shape["narrow"]),
        mesh=mesh,
        in_specs=placed,
        out_specs=(P("wide", None), P(("wide", "narrow"), None)),
        check_vma=False,
    )
```

```python
import functools
import math

import jax
import jax.numpy as jnp
from jax import lax
from jax.experimental import pallas as pl
from jax.experimental.pallas import tpu as pltpu
from jax.sharding import PartitionSpec as P

logit_scale = 3.0
epsilon = 1e-06
exp2_scale = logit_scale * math.log2(math.e)
chunk = 256
both = ("wide", "narrow")
whole = pl.BlockSpec(memory_space=pltpu.VMEM)
params = pltpu.CompilerParams(vmem_limit_bytes=8 * 1024 * 1024)
light = pl.CostEstimate(flops=0, bytes_accessed=1 << 19, transcendentals=0)


def t_bit(n):
    return 1 if n % 2 == 0 else 2


def s_bit(n):
    return 3 - t_bit(n)


def exchange(x, sizes, partner):
    wide, narrow = sizes
    pairs = []
    for w in range(wide):
        for n in range(narrow):
            pw, pn = partner(w, n)
            pairs.append((w * narrow + n, pw * narrow + pn))
    return lax.ppermute(x, both, pairs)


def logits_kernel(group_count, part_count, with_early, unit_ref, *refs):
    parts = refs[: group_count * part_count]
    shifted_ref, stats_ref = refs[-2:]
    per = chunk // 128
    first = 0
    if with_early:
        early_ref = refs[group_count * part_count]
        first = early_ref.shape[0] // 2
        half = stats_ref.shape[0] // 2
        stats_ref[0:first, :] = early_ref[0:first, :]
        stats_ref[half:half + first, :] = early_ref[first:, :]
    half = stats_ref.shape[0] // 2
    step = 0
    for g in range(group_count):
        group = parts[g * part_count:(g + 1) * part_count]
        cols = group[0].shape[1]
        for row in range(0, group[0].shape[0], chunk):
            dots = None
            for k, part in enumerate(group):
                prod = lax.dot_general(
                    unit_ref[:, k * cols:(k + 1) * cols], part[row:row + chunk, :],
                    (((1,), (1,)), ((), ())), preferred_element_type=jnp.float32,
                )
                dots = prod if dots is None else dots + prod
            top = jnp.max(dots, axis=0, keepdims=True)
            shifted = jnp.exp2((dots - top) * exp2_scale)
            total = jnp.sum(shifted, axis=0, keepdims=True)
            shifted_ref[:, step * chunk:(step + 1) * chunk] = shifted
            for b in range(per):
                at = first + step * per + b
                stats_ref[at:at + 1, :] = top[:, b * 128:(b + 1) * 128]
                stats_ref[half + at:half + at + 1, :] = total[:, b * 128:(b + 1) * 128]
            step += 1


def logits_call(unit, groups, early=None):
    rows = groups[0][0].shape[0]
    count = len(groups) * rows
    samples = unit.shape[0]
    flat = [part for group in groups for part in group]
    lines = 2 * count // 128
    if early is not None:
        lines += early.shape[0]
        flat.append(early)
    return pl.pallas_call(
        functools.partial(logits_kernel, len(groups), len(groups[0]), early is not None),
        out_shape=(
            jax.ShapeDtypeStruct((samples, count), jnp.float32),
            jax.ShapeDtypeStruct((lines, 128), jnp.float32),
        ),
        in_specs=[whole] * (1 + len(flat)),
        out_specs=(whole, whole),
        compiler_params=params,
        cost_estimate=pl.CostEstimate(
            flops=2 * samples * count * unit.shape[1],
            bytes_accessed=4 * samples * count,
            transcendentals=samples * count,
        ),
        name="logits",
    )(unit, *flat)


def grad_kernel(first, steps, depth, unit_t_ref, shifted_ref, scale_ref, weight_ref, at_ref, grad_ref, keep_ref, send_ref):
    samples = shifted_ref.shape[0]
    half = unit_t_ref.shape[0] // 2
    per = chunk // 128
    w, n = lax.axis_index("wide"), lax.axis_index("narrow")
    base = (w * lax.axis_size("narrow") + n) * samples
    cand = lax.broadcasted_iota(jnp.int32, (samples, chunk), 0) + base

    def row(ref, at):
        return jnp.concatenate([ref[at + b:at + b + 1, :] for b in range(per)], axis=1)

    def far_row(ref, at):
        lines = []
        for b in range(at, at + per):
            g, z = divmod(b, depth)
            offset = jnp.where(n % 2 == 0, 4 * z + g, 4 * z + (g % 2) * 2 + g // 2)
            lines.append(ref[pl.ds(jnp.bitwise_xor(w, offset), 1), :])
        return jnp.concatenate(lines, axis=1)

    for out, at in enumerate(steps):
        cols = slice((at - first) * chunk, (at - first + 1) * chunk)
        scale, weight, spot = row(scale_ref, at * per), far_row(weight_ref, at * per), far_row(at_ref, at * per)
        soft = shifted_ref[:, cols] * scale
        grad = (weight * jnp.where(cand == spot, soft - 1.0, soft)).astype(jnp.bfloat16)
        out_cols = slice(out * chunk, (out + 1) * chunk)
        grad_ref[:, out_cols] = grad
        shares = logit_scale * jnp.dot(unit_t_ref[...], grad, preferred_element_type=jnp.float32)
        keep_ref[:, out_cols] = shares[:half]
        send_ref[:, out_cols] = shares[half:].astype(jnp.bfloat16)


def grad_call(unit_t, shifted, scale, weight, spots, first, steps, depth):
    samples = shifted.shape[0]
    width = unit_t.shape[0]
    count = len(steps) * chunk
    return pl.pallas_call(
        functools.partial(grad_kernel, first, steps, depth),
        out_shape=(
            jax.ShapeDtypeStruct((samples, count), jnp.bfloat16),
            jax.ShapeDtypeStruct((width // 2, count), jnp.float32),
            jax.ShapeDtypeStruct((width // 2, count), jnp.bfloat16),
        ),
        in_specs=[whole] * 5,
        out_specs=(whole,) * 3,
        compiler_params=params,
        cost_estimate=pl.CostEstimate(
            flops=2 * samples * count * width, bytes_accessed=6 * samples * count, transcendentals=0
        ),
        name="grads",
    )(unit_t, shifted, scale, weight, spots)


def proxy_kernel(group_count, part_count, rows, late_ref, early_ref, *refs):
    parts = refs[:group_count * part_count]
    *picked_refs, out_ref = refs[group_count * part_count:]
    size, cols = parts[0].shape
    grads = [late_ref] + [early_ref.at[:, g * size:(g + 1) * size] for g in range(group_count - 1)]
    n = lax.axis_index("narrow")
    places = []
    for k in range(part_count):
        if part_count == 1:
            places.append(slice(0, cols))
        else:
            places.append(pl.ds(pl.multiple_of((n ^ k) * cols, cols), cols))
    each = picked_refs[0].shape[0]
    for row in range(0, out_ref.shape[0], rows):
        at = slice(row, row + rows)
        picked_ref, here = picked_refs[row // each], slice(row % each, row % each + rows)
        sums = []
        for k in range(part_count):
            total = None
            for g in range(group_count):
                prod = jnp.dot(
                    grads[g][at, :], parts[g * part_count + k][...], preferred_element_type=jnp.float32
                )
                total = prod if total is None else total + prod
            sums.append(logit_scale * total)
        picked = [picked_ref[here, place] for place in places]
        square = functools.reduce(jnp.add, [jnp.sum(p * p, axis=1, keepdims=True) for p in picked])
        inverse = 1.0 / jnp.sqrt(square + epsilon)
        inner = functools.reduce(jnp.add, [jnp.sum(p * s, axis=1, keepdims=True) for p, s in zip(picked, sums)])
        slope = inner * inverse * inverse
        for place, p, s in zip(places, picked, sums):
            out_ref[at, place] = (s - p * slope) * inverse


def proxy_call(late, early, groups, picked):
    samples, width = late.shape[0], picked[0].shape[1]
    count = late.shape[1] + early.shape[1]
    flat = [part for group in groups for part in group]
    return pl.pallas_call(
        functools.partial(proxy_kernel, len(groups), len(groups[0]), 256),
        out_shape=jax.ShapeDtypeStruct((samples, width), jnp.float32),
        in_specs=[whole] * (len(flat) + 2 + len(picked)),
        out_specs=whole,
        compiler_params=params,
        cost_estimate=pl.CostEstimate(
            flops=2 * samples * count * width, bytes_accessed=4 * samples * count, transcendentals=0
        ),
        name="proxy_grads",
    )(late, early, *flat, *picked)


def merge_kernel(flips, swap, with_scale, *refs):
    ins, out_ref = refs[:-1], refs[-1]
    if with_scale:
        own_ref, ins = ins[-1], ins[:-1]
    blocks = ins[0].shape[0] // 2
    for b in range(blocks):
        spots = [swap(f, b) for f in flips]
        tops = [ref[at:at + 1, :] for ref, at in zip(ins, spots)]
        totals = [ref[blocks + at:blocks + at + 1, :] for ref, at in zip(ins, spots)]
        top = functools.reduce(jnp.maximum, tops)
        total = functools.reduce(
            jnp.add, [t * jnp.exp2((m - top) * exp2_scale) for m, t in zip(tops, totals)]
        )
        if with_scale:
            out_ref[b:b + 1, :] = jnp.exp2((own_ref[b:b + 1, :] - top) * exp2_scale) / total
        else:
            out_ref[b:b + 1, :] = top
            out_ref[blocks + b:blocks + b + 1, :] = total


def merge(stats, flips, swap, own=None):
    lines = stats[0].shape[0]
    if own is not None:
        stats, lines = [*stats, own], lines // 2
    return pl.pallas_call(
        functools.partial(merge_kernel, flips, swap, own is not None),
        out_shape=jax.ShapeDtypeStruct((lines, 128), jnp.float32),
        in_specs=[whole] * len(stats),
        out_specs=whole,
        compiler_params=params,
        cost_estimate=light,
        name="merge_stats",
    )(*stats)


def stack_kernel(*refs):
    rows = refs[0].shape[0]
    for k, ref in enumerate(refs[:-1]):
        refs[-1][k * rows:(k + 1) * rows, :] = ref[...]


def stack_call(parts):
    rows, cols = parts[0].shape
    return pl.pallas_call(
        stack_kernel,
        out_shape=jax.ShapeDtypeStruct((len(parts) * rows, cols), parts[0].dtype),
        in_specs=[whole] * len(parts),
        out_specs=whole,
        compiler_params=params,
        cost_estimate=light,
        name="stack_blocks",
    )(*parts)


def add_kernel(ins, outs, size, *refs):
    for name, out_ref in zip(outs, refs[len(ins):]):
        total = None
        for places, ref in zip(ins, refs):
            if name in places:
                at = places.index(name)
                term = ref[:, at * size:(at + 1) * size].astype(jnp.float32)
                total = term if total is None else total + term
        out_ref[...] = total.astype(out_ref.dtype)


def add_call(arrays, ins, outs, size):
    rows = arrays[0].shape[0]
    result = pl.pallas_call(
        functools.partial(add_kernel, ins, outs, size),
        out_shape=[jax.ShapeDtypeStruct((rows, size), jnp.bfloat16) for _ in outs],
        in_specs=[whole] * len(arrays),
        out_specs=[whole] * len(outs),
        compiler_params=params,
        cost_estimate=light,
        name="add_shares",
    )(*arrays)
    return result


def own_kernel(ins, count, size, *refs):
    cols = size // count
    for k, out_ref in enumerate(refs[len(ins):]):
        total = None
        for places, ref in zip(ins, refs):
            at = places.index("J") * size + k * cols
            term = ref[:, at:at + cols].astype(jnp.float32)
            total = term if total is None else total + term
        out_ref[...] = total.astype(out_ref.dtype)


def own_call(arrays, ins, count, size):
    rows = arrays[0].shape[0]
    return pl.pallas_call(
        functools.partial(own_kernel, ins, count, size),
        out_shape=[
            jax.ShapeDtypeStruct((rows, size // count), jnp.bfloat16 if k else jnp.float32) for k in range(count)
        ],
        in_specs=[whole] * len(arrays),
        out_specs=[whole] * count,
        compiler_params=params,
        cost_estimate=light,
        name="add_shares_z",
    )(*arrays)


def prep_kernel(part_count, *refs):
    *picked_refs, unit_ref, unit_t_ref = refs
    each, width = picked_refs[0].shape
    cols = width // part_count
    n = lax.axis_index("narrow")
    for line in range(0, unit_ref.shape[0], 256):
        picked_ref, row = picked_refs[line // each], line % each
        at = slice(row, row + 256)
        if part_count == 1:
            picked = picked_ref[at, :]
        else:
            picked = jnp.concatenate(
                [picked_ref[at, pl.ds(pl.multiple_of((n ^ k) * cols, cols), cols)] for k in range(part_count)],
                axis=1,
            )
        lengths = jnp.sqrt(jnp.sum(picked * picked, axis=1, keepdims=True) + epsilon)
        unit = picked / lengths
        unit_ref[line:line + 256, :] = unit.astype(jnp.bfloat16)
        unit_t_ref[:, line:line + 256] = unit.T.astype(jnp.bfloat16)


def prep_call(picked, part_count):
    samples, width = sum(p.shape[0] for p in picked), picked[0].shape[1]
    return pl.pallas_call(
        functools.partial(prep_kernel, part_count),
        out_shape=(
            jax.ShapeDtypeStruct((samples, width), jnp.bfloat16),
            jax.ShapeDtypeStruct((width, samples), jnp.bfloat16),
        ),
        in_specs=[whole] * len(picked),
        out_specs=(whole, whole),
        compiler_params=params,
        cost_estimate=pl.CostEstimate(flops=4 * samples * width, bytes_accessed=8 * samples * width, transcendentals=0),
        name="unit_rows",
    )(*picked)


def finish_kernel(*refs):
    ins, out_ref = refs[:-1], refs[-1]
    total = functools.reduce(jnp.add, [ref[...].astype(jnp.float32) for ref in ins])
    out_ref[...] = total.T


def finish_call(own, others):
    return pl.pallas_call(
        finish_kernel,
        out_shape=jax.ShapeDtypeStruct((own.shape[1], own.shape[0]), jnp.float32),
        in_specs=[whole] * (1 + len(others)),
        out_specs=whole,
        compiler_params=params,
        cost_estimate=light,
        name="feature_sums",
    )(own, *others)


def join_kernel(own_ref, other_ref, out_ref):
    cols = own_ref.shape[1]
    n = lax.axis_index("narrow")
    out_ref[:, pl.ds(pl.multiple_of(n * cols, cols), cols)] = own_ref[...]
    out_ref[:, pl.ds(pl.multiple_of((1 - n) * cols, cols), cols)] = other_ref[...]


def join_call(own, other):
    return pl.pallas_call(
        join_kernel,
        out_shape=jax.ShapeDtypeStruct((own.shape[0], 2 * own.shape[1]), jnp.float32),
        in_specs=[whole] * 2,
        out_specs=whole,
        compiler_params=params,
        cost_estimate=light,
        name="feature_grad",
    )(own, other)


def make(wide, narrow):
    depth = wide // 4
    sizes = (wide, narrow)
    send = functools.partial(exchange, sizes=sizes)

    def to_t(x):
        return send(x, partner=lambda w, n: (w ^ t_bit(n), n))

    def to_s(x):
        return send(x, partner=lambda w, n: (w ^ s_bit(n), n))

    def to_ts(x):
        return send(x, partner=lambda w, n: (w ^ 3, n))

    def to_z(x, k):
        return send(x, partner=lambda w, n: (w ^ (k << 2), n))

    def to_core(x, k):
        return send(x, partner=lambda w, n: (w, n ^ k))

    def per_device(features, proxies, sample_ids, positives, loss_weight):
        samples = sample_ids.shape[0]
        rows, width = features.shape
        w = lax.axis_index("wide")
        n = lax.axis_index("narrow")

        if narrow == 2:
            cols = width // 2
            part = jnp.where(n == 0, features[:, :cols], features[:, cols:])
        else:
            part = features
        near = samples // 2
        picked = [
            proxies.at[ids].get(mode="promise_in_bounds") for ids in (sample_ids[:near], sample_ids[near:])
        ]
        zs = [to_z(part, k) for k in range(1, depth)]
        *zs, picked[0] = lax.optimization_barrier((*zs, picked[0]))
        group_j = stack_call([part] + zs)
        group_t, group_s, picked[1] = lax.optimization_barrier((to_t(group_j), to_s(group_j), picked[1]))
        group_d = to_s(group_t)
        groups = [(group_j,), (group_t,), (group_s,)]
        if narrow == 2:
            others = [to_core(group_j, 1), to_core(group_s, 1), to_core(group_t, 1)]
            groups = [(*group, other) for group, other in zip(groups, others)]

        unit, unit_t = prep_call(picked, 2 if narrow == 2 else 1)
        if narrow != 2:
            unit_t = jnp.take(unit_t.reshape(narrow, width // narrow, samples), n ^ jnp.arange(narrow), axis=0)
            unit_t = unit_t.reshape(width, samples)

        spots = positives.reshape(wide, rows)
        weight = loss_weight.reshape(wide, rows)

        shifted_early, stats_early = logits_call(unit, groups)
        group_d, stats_early = lax.optimization_barrier((group_d, stats_early))
        groups.append((group_d, to_core(group_d, 1)) if narrow == 2 else (group_d,))
        shifted_late, own = logits_call(unit, groups[3:], stats_early)
        stats = own

        def swap_groups(flip, b):
            g, z = divmod(b, depth)
            return ((g % 2) * 2 + g // 2) * depth + z if flip else b

        for bit in range(narrow.bit_length() - 1):
            stats = merge([stats, to_core(stats, 1 << bit)], (0, int(bit == 0)), swap_groups)
        others = [to_z(stats, k) for k in range(1, depth)]
        stats = merge([stats] + others, tuple(range(depth)), lambda k, b: b ^ k)
        others = [to_t(stats), to_s(stats), to_ts(stats)]
        scale = merge([stats] + others, (0, 1, 2, 3), lambda k, b: b ^ (k * depth), own)

        per = depth * rows // chunk
        order_t, order_s, order_j = range(per, 2 * per), range(2 * per, 3 * per), range(per)
        size = depth * rows
        low = jnp.bfloat16
        grad_d, keep_d, send_d = grad_call(
            unit_t, shifted_late, scale, weight, spots, 3 * per, tuple(range(3 * per, 4 * per)), depth
        )
        grad_r, keep_r, send_r = grad_call(
            unit_t, shifted_early, scale, weight, spots, 0, (*order_t, *order_s, *order_j), depth
        )

        def within(keep, out, names):
            for bit in range(narrow.bit_length() - 2, 0, -1):
                keep = keep + to_core(out, 1 << bit).astype(jnp.float32)
                half = keep.shape[0] // 2
                keep, out = keep[:half], keep[half:].astype(low)
            return [keep, to_core(out, 1)], [names, names.translate(str.maketrans("TS", "ST"))]

        arrays, places = within(keep_d, send_d, "D")
        arrays[1], send_r = lax.optimization_barrier((arrays[1], send_r))
        sum_d, = add_call(arrays, places, "D", size)
        arrays, places = within(keep_r, send_r, "TSJ")
        from_d = to_s(sum_d)
        sum_t, sum_s = add_call([*arrays, from_d], [*places, "T"], "TS", size)
        from_t, from_s = to_t(sum_t), to_s(sum_s)
        proxy_grad = proxy_call(grad_d, grad_r, [groups[3], groups[1], groups[2], groups[0]], picked)
        from_s, proxy_grad = lax.optimization_barrier((from_s, proxy_grad))
        mine, *others = own_call([*arrays, from_t, from_s], [*places, "J", "J"], depth, size)
        mine = finish_call(mine, [to_z(other, k) for k, other in enumerate(others, 1)])
        if narrow == 2:
            feature_grad = join_call(mine, to_core(mine, 1))
        else:
            mine = mine[None]
            for bit in range(narrow.bit_length() - 1):
                mine = jnp.concatenate([mine, to_core(mine, 1 << bit)], axis=0)
            feature_grad = jnp.take(mine, n ^ jnp.arange(narrow), axis=0).transpose(1, 0, 2).reshape(rows, width)
        return (feature_grad, proxy_grad)

    return per_device


def solution(mesh):
    placed = (P("wide", None), P(("wide", "narrow"), None), P(("wide", "narrow")), P(), P())
    return jax.shard_map(
        make(mesh.shape["wide"], mesh.shape["narrow"]),
        mesh=mesh,
        in_specs=placed,
        out_specs=(P("wide", None), P(("wide", "narrow"), None)),
        check_vma=False,
    )
```

```python
import functools
import math

import jax
import jax.numpy as jnp
from jax import lax
from jax.experimental import pallas as pl
from jax.experimental.pallas import tpu as pltpu
from jax.sharding import PartitionSpec as P

logit_scale = 3.0
epsilon = 1e-06
exp2_scale = logit_scale * math.log2(math.e)
chunk = 256
both = ("wide", "narrow")
whole = pl.BlockSpec(memory_space=pltpu.VMEM)
params = pltpu.CompilerParams(vmem_limit_bytes=8 * 1024 * 1024)
light = pl.CostEstimate(flops=0, bytes_accessed=1 << 19, transcendentals=0)


def t_bit(n):
    return 1 if n % 2 == 0 else 2


def s_bit(n):
    return 3 - t_bit(n)


def exchange(x, sizes, partner):
    wide, narrow = sizes
    pairs = []
    for w in range(wide):
        for n in range(narrow):
            pw, pn = partner(w, n)
            pairs.append((w * narrow + n, pw * narrow + pn))
    return lax.ppermute(x, both, pairs)


def logits_kernel(group_count, part_count, with_early, unit_ref, *refs):
    parts = refs[: group_count * part_count]
    shifted_ref, stats_ref = refs[-2:]
    per = chunk // 128
    first = 0
    if with_early:
        early_ref = refs[group_count * part_count]
        first = early_ref.shape[0] // 2
        half = stats_ref.shape[0] // 2
        stats_ref[0:first, :] = early_ref[0:first, :]
        stats_ref[half:half + first, :] = early_ref[first:, :]
    half = stats_ref.shape[0] // 2
    step = 0
    for g in range(group_count):
        group = parts[g * part_count:(g + 1) * part_count]
        cols = group[0].shape[1]
        for row in range(0, group[0].shape[0], chunk):
            dots = None
            for k, part in enumerate(group):
                prod = lax.dot_general(
                    unit_ref[:, k * cols:(k + 1) * cols], part[row:row + chunk, :],
                    (((1,), (1,)), ((), ())), preferred_element_type=jnp.float32,
                )
                dots = prod if dots is None else dots + prod
            top = jnp.max(dots, axis=0, keepdims=True)
            shifted = jnp.exp2((dots - top) * exp2_scale)
            total = jnp.sum(shifted, axis=0, keepdims=True)
            shifted_ref[:, step * chunk:(step + 1) * chunk] = shifted
            for b in range(per):
                at = first + step * per + b
                stats_ref[at:at + 1, :] = top[:, b * 128:(b + 1) * 128]
                stats_ref[half + at:half + at + 1, :] = total[:, b * 128:(b + 1) * 128]
            step += 1


def logits_call(unit, groups, early=None):
    rows = groups[0][0].shape[0]
    count = len(groups) * rows
    samples = unit.shape[0]
    flat = [part for group in groups for part in group]
    lines = 2 * count // 128
    if early is not None:
        lines += early.shape[0]
        flat.append(early)
    return pl.pallas_call(
        functools.partial(logits_kernel, len(groups), len(groups[0]), early is not None),
        out_shape=(
            jax.ShapeDtypeStruct((samples, count), jnp.float32),
            jax.ShapeDtypeStruct((lines, 128), jnp.float32),
        ),
        in_specs=[whole] * (1 + len(flat)),
        out_specs=(whole, whole),
        compiler_params=params,
        cost_estimate=pl.CostEstimate(
            flops=2 * samples * count * unit.shape[1],
            bytes_accessed=4 * samples * count,
            transcendentals=samples * count,
        ),
        name="logits",
    )(unit, *flat)


def grad_kernel(first, steps, depth, unit_t_ref, shifted_ref, scale_ref, weight_ref, at_ref, grad_ref, keep_ref, send_ref):
    samples = shifted_ref.shape[0]
    half = unit_t_ref.shape[0] // 2
    per = chunk // 128
    w, n = lax.axis_index("wide"), lax.axis_index("narrow")
    base = (w * lax.axis_size("narrow") + n) * samples
    cand = lax.broadcasted_iota(jnp.int32, (samples, chunk), 0) + base

    def row(ref, at):
        return jnp.concatenate([ref[at + b:at + b + 1, :] for b in range(per)], axis=1)

    def far_row(ref, at):
        lines = []
        for b in range(at, at + per):
            g, z = divmod(b, depth)
            offset = jnp.where(n % 2 == 0, 4 * z + g, 4 * z + (g % 2) * 2 + g // 2)
            lines.append(ref[pl.ds(jnp.bitwise_xor(w, offset), 1), :])
        return jnp.concatenate(lines, axis=1)

    for out, at in enumerate(steps):
        cols = slice((at - first) * chunk, (at - first + 1) * chunk)
        scale, weight, spot = row(scale_ref, at * per), far_row(weight_ref, at * per), far_row(at_ref, at * per)
        soft = shifted_ref[:, cols] * scale
        grad = (weight * jnp.where(cand == spot, soft - 1.0, soft)).astype(jnp.bfloat16)
        out_cols = slice(out * chunk, (out + 1) * chunk)
        grad_ref[:, out_cols] = grad
        shares = logit_scale * jnp.dot(unit_t_ref[...], grad, preferred_element_type=jnp.float32)
        keep_ref[:, out_cols] = shares[:half]
        send_ref[:, out_cols] = shares[half:].astype(jnp.bfloat16)


def grad_call(unit_t, shifted, scale, weight, spots, first, steps, depth):
    samples = shifted.shape[0]
    width = unit_t.shape[0]
    count = len(steps) * chunk
    return pl.pallas_call(
        functools.partial(grad_kernel, first, steps, depth),
        out_shape=(
            jax.ShapeDtypeStruct((samples, count), jnp.bfloat16),
            jax.ShapeDtypeStruct((width // 2, count), jnp.float32),
            jax.ShapeDtypeStruct((width // 2, count), jnp.bfloat16),
        ),
        in_specs=[whole] * 5,
        out_specs=(whole,) * 3,
        compiler_params=params,
        cost_estimate=pl.CostEstimate(
            flops=2 * samples * count * width, bytes_accessed=6 * samples * count, transcendentals=0
        ),
        name="grads",
    )(unit_t, shifted, scale, weight, spots)


def proxy_kernel(group_count, part_count, rows, late_ref, early_ref, *refs):
    parts = refs[:group_count * part_count]
    *picked_refs, out_ref = refs[group_count * part_count:]
    size, cols = parts[0].shape
    grads = [late_ref] + [early_ref.at[:, g * size:(g + 1) * size] for g in range(group_count - 1)]
    n = lax.axis_index("narrow")
    places = []
    for k in range(part_count):
        if part_count == 1:
            places.append(slice(0, cols))
        else:
            places.append(pl.ds(pl.multiple_of((n ^ k) * cols, cols), cols))
    each = picked_refs[0].shape[0]
    for row in range(0, out_ref.shape[0], rows):
        at = slice(row, row + rows)
        picked_ref, here = picked_refs[row // each], slice(row % each, row % each + rows)
        sums = []
        for k in range(part_count):
            total = None
            for g in range(group_count):
                prod = jnp.dot(
                    grads[g][at, :], parts[g * part_count + k][...], preferred_element_type=jnp.float32
                )
                total = prod if total is None else total + prod
            sums.append(logit_scale * total)
        picked = [picked_ref[here, place] for place in places]
        square = functools.reduce(jnp.add, [jnp.sum(p * p, axis=1, keepdims=True) for p in picked])
        inverse = 1.0 / jnp.sqrt(square + epsilon)
        inner = functools.reduce(jnp.add, [jnp.sum(p * s, axis=1, keepdims=True) for p, s in zip(picked, sums)])
        slope = inner * inverse * inverse
        for place, p, s in zip(places, picked, sums):
            out_ref[at, place] = (s - p * slope) * inverse


def proxy_call(late, early, groups, picked):
    samples, width = late.shape[0], picked[0].shape[1]
    count = late.shape[1] + early.shape[1]
    flat = [part for group in groups for part in group]
    return pl.pallas_call(
        functools.partial(proxy_kernel, len(groups), len(groups[0]), 256),
        out_shape=jax.ShapeDtypeStruct((samples, width), jnp.float32),
        in_specs=[whole] * (len(flat) + 2 + len(picked)),
        out_specs=whole,
        compiler_params=params,
        cost_estimate=pl.CostEstimate(
            flops=2 * samples * count * width, bytes_accessed=4 * samples * count, transcendentals=0
        ),
        name="proxy_grads",
    )(late, early, *flat, *picked)


def merge_kernel(flips, swap, with_scale, *refs):
    ins, out_ref = refs[:-1], refs[-1]
    if with_scale:
        own_ref, ins = ins[-1], ins[:-1]
    blocks = ins[0].shape[0] // 2
    for b in range(blocks):
        spots = [swap(f, b) for f in flips]
        tops = [ref[at:at + 1, :] for ref, at in zip(ins, spots)]
        totals = [ref[blocks + at:blocks + at + 1, :] for ref, at in zip(ins, spots)]
        top = functools.reduce(jnp.maximum, tops)
        total = functools.reduce(
            jnp.add, [t * jnp.exp2((m - top) * exp2_scale) for m, t in zip(tops, totals)]
        )
        if with_scale:
            out_ref[b:b + 1, :] = jnp.exp2((own_ref[b:b + 1, :] - top) * exp2_scale) / total
        else:
            out_ref[b:b + 1, :] = top
            out_ref[blocks + b:blocks + b + 1, :] = total


def merge(stats, flips, swap, own=None):
    lines = stats[0].shape[0]
    if own is not None:
        stats, lines = [*stats, own], lines // 2
    return pl.pallas_call(
        functools.partial(merge_kernel, flips, swap, own is not None),
        out_shape=jax.ShapeDtypeStruct((lines, 128), jnp.float32),
        in_specs=[whole] * len(stats),
        out_specs=whole,
        compiler_params=params,
        cost_estimate=light,
        name="merge_stats",
    )(*stats)


def stack_kernel(places, *refs):
    rows = refs[0].shape[0]
    for k, ref in zip(places, refs):
        refs[-1][k * rows:(k + 1) * rows, :] = ref[...]


def stack_call(parts, places):
    rows, cols = parts[0].shape
    return pl.pallas_call(
        functools.partial(stack_kernel, places),
        out_shape=jax.ShapeDtypeStruct((len(parts) * rows, cols), parts[0].dtype),
        in_specs=[whole] * len(parts),
        out_specs=whole,
        compiler_params=params,
        cost_estimate=light,
        name="stack_blocks",
    )(*parts)


def add_kernel(ins, outs, size, *refs):
    for name, out_ref in zip(outs, refs[len(ins):]):
        total = None
        for places, ref in zip(ins, refs):
            if name in places:
                at = places.index(name)
                term = ref[:, at * size:(at + 1) * size].astype(jnp.float32)
                total = term if total is None else total + term
        out_ref[...] = total.astype(out_ref.dtype)


def add_call(arrays, ins, outs, size):
    rows = arrays[0].shape[0]
    result = pl.pallas_call(
        functools.partial(add_kernel, ins, outs, size),
        out_shape=[jax.ShapeDtypeStruct((rows, size), jnp.bfloat16) for _ in outs],
        in_specs=[whole] * len(arrays),
        out_specs=[whole] * len(outs),
        compiler_params=params,
        cost_estimate=light,
        name="add_shares",
    )(*arrays)
    return result


def own_kernel(ins, count, size, *refs):
    cols = size // count
    for k, out_ref in enumerate(refs[len(ins):]):
        total = None
        for places, ref in zip(ins, refs):
            at = places.index("J") * size + k * cols
            term = ref[:, at:at + cols].astype(jnp.float32)
            total = term if total is None else total + term
        out_ref[...] = total.astype(out_ref.dtype)


def own_call(arrays, ins, count, size):
    rows = arrays[0].shape[0]
    return pl.pallas_call(
        functools.partial(own_kernel, ins, count, size),
        out_shape=[
            jax.ShapeDtypeStruct((rows, size // count), jnp.bfloat16 if k else jnp.float32) for k in range(count)
        ],
        in_specs=[whole] * len(arrays),
        out_specs=[whole] * count,
        compiler_params=params,
        cost_estimate=light,
        name="add_shares_z",
    )(*arrays)


def prep_kernel(part_count, *refs):
    *picked_refs, unit_ref, unit_t_ref = refs
    each, width = picked_refs[0].shape
    cols = width // part_count
    n = lax.axis_index("narrow")
    for line in range(0, unit_ref.shape[0], 256):
        picked_ref, row = picked_refs[line // each], line % each
        at = slice(row, row + 256)
        if part_count == 1:
            picked = picked_ref[at, :]
        else:
            picked = jnp.concatenate(
                [picked_ref[at, pl.ds(pl.multiple_of((n ^ k) * cols, cols), cols)] for k in range(part_count)],
                axis=1,
            )
        lengths = jnp.sqrt(jnp.sum(picked * picked, axis=1, keepdims=True) + epsilon)
        unit = picked / lengths
        unit_ref[line:line + 256, :] = unit.astype(jnp.bfloat16)
        unit_t_ref[:, line:line + 256] = unit.T.astype(jnp.bfloat16)


def prep_call(picked, part_count):
    samples, width = sum(p.shape[0] for p in picked), picked[0].shape[1]
    return pl.pallas_call(
        functools.partial(prep_kernel, part_count),
        out_shape=(
            jax.ShapeDtypeStruct((samples, width), jnp.bfloat16),
            jax.ShapeDtypeStruct((width, samples), jnp.bfloat16),
        ),
        in_specs=[whole] * len(picked),
        out_specs=(whole, whole),
        compiler_params=params,
        cost_estimate=pl.CostEstimate(flops=4 * samples * width, bytes_accessed=8 * samples * width, transcendentals=0),
        name="unit_rows",
    )(*picked)


def finish_kernel(*refs):
    ins, out_ref = refs[:-1], refs[-1]
    total = functools.reduce(jnp.add, [ref[...].astype(jnp.float32) for ref in ins])
    out_ref[...] = total.T


def finish_call(own, others):
    return pl.pallas_call(
        finish_kernel,
        out_shape=jax.ShapeDtypeStruct((own.shape[1], own.shape[0]), jnp.float32),
        in_specs=[whole] * (1 + len(others)),
        out_specs=whole,
        compiler_params=params,
        cost_estimate=light,
        name="feature_sums",
    )(own, *others)


def join_kernel(own_ref, other_ref, out_ref):
    cols = own_ref.shape[1]
    n = lax.axis_index("narrow")
    out_ref[:, pl.ds(pl.multiple_of(n * cols, cols), cols)] = own_ref[...]
    out_ref[:, pl.ds(pl.multiple_of((1 - n) * cols, cols), cols)] = other_ref[...]


def join_call(own, other):
    return pl.pallas_call(
        join_kernel,
        out_shape=jax.ShapeDtypeStruct((own.shape[0], 2 * own.shape[1]), jnp.float32),
        in_specs=[whole] * 2,
        out_specs=whole,
        compiler_params=params,
        cost_estimate=light,
        name="feature_grad",
    )(own, other)


def make(wide, narrow):
    depth = wide // 4
    sizes = (wide, narrow)
    send = functools.partial(exchange, sizes=sizes)

    def to_t(x):
        return send(x, partner=lambda w, n: (w ^ t_bit(n), n))

    def to_s(x):
        return send(x, partner=lambda w, n: (w ^ s_bit(n), n))

    def to_ts(x):
        return send(x, partner=lambda w, n: (w ^ 3, n))

    def to_z(x, k):
        return send(x, partner=lambda w, n: (w ^ (k << 2), n))

    far_first = sorted(range(1, depth), key=lambda k: (k == 1, k))

    def reach(parts):
        return [to_z(parts[k] if isinstance(parts, dict) else parts, k) for k in far_first]

    def to_core(x, k):
        return send(x, partner=lambda w, n: (w, n ^ k))

    def per_device(features, proxies, sample_ids, positives, loss_weight):
        samples = sample_ids.shape[0]
        rows, width = features.shape
        w = lax.axis_index("wide")
        n = lax.axis_index("narrow")

        if narrow == 2:
            cols = width // 2
            part = jnp.where(n == 0, features[:, :cols], features[:, cols:])
        else:
            part = features
        zs = reach(part)
        *zs, sample_ids = lax.optimization_barrier((*zs, sample_ids))
        picked = proxies.at[sample_ids].get(mode="promise_in_bounds", wrap_negative_indices=False)
        group_j = stack_call([part] + zs, [0] + far_first)
        group_t, group_s, picked = lax.optimization_barrier((to_t(group_j), to_s(group_j), picked))
        picked = [picked]
        group_d = to_s(group_t)
        groups = [(group_j,), (group_t,), (group_s,)]
        if narrow == 2:
            others = [to_core(group_j, 1), to_core(group_s, 1), to_core(group_t, 1)]
            groups = [(*group, other) for group, other in zip(groups, others)]

        unit, unit_t = prep_call(picked, 2 if narrow == 2 else 1)
        if narrow != 2:
            unit_t = jnp.take(unit_t.reshape(narrow, width // narrow, samples), n ^ jnp.arange(narrow), axis=0)
            unit_t = unit_t.reshape(width, samples)

        spots = positives.reshape(wide, rows)
        weight = loss_weight.reshape(wide, rows)

        shifted_early, stats_early = logits_call(unit, groups)
        group_d, stats_early = lax.optimization_barrier((group_d, stats_early))
        groups.append((group_d, to_core(group_d, 1)) if narrow == 2 else (group_d,))
        shifted_late, own = logits_call(unit, groups[3:], stats_early)
        stats = own

        def swap_groups(flip, b):
            g, z = divmod(b, depth)
            return ((g % 2) * 2 + g // 2) * depth + z if flip else b

        for bit in range(narrow.bit_length() - 1):
            stats = merge([stats, to_core(stats, 1 << bit)], (0, int(bit == 0)), swap_groups)
        others = reach(stats)
        stats = merge([stats] + others, [0] + far_first, lambda k, b: b ^ k)
        others = [to_t(stats), to_s(stats), to_ts(stats)]
        scale = merge([stats] + others, (0, 1, 2, 3), lambda k, b: b ^ (k * depth), own)

        per = depth * rows // chunk
        order_t, order_s, order_j = range(per, 2 * per), range(2 * per, 3 * per), range(per)
        size = depth * rows
        low = jnp.bfloat16
        grad_d, keep_d, send_d = grad_call(
            unit_t, shifted_late, scale, weight, spots, 3 * per, tuple(range(3 * per, 4 * per)), depth
        )
        grad_r, keep_r, send_r = grad_call(
            unit_t, shifted_early, scale, weight, spots, 0, (*order_t, *order_s, *order_j), depth
        )

        def within(keep, out, names):
            for bit in range(narrow.bit_length() - 2, 0, -1):
                keep = keep + to_core(out, 1 << bit).astype(jnp.float32)
                half = keep.shape[0] // 2
                keep, out = keep[:half], keep[half:].astype(low)
            return [keep, to_core(out, 1)], [names, names.translate(str.maketrans("TS", "ST"))]

        arrays, places = within(keep_d, send_d, "D")
        arrays[1], send_r = lax.optimization_barrier((arrays[1], send_r))
        sum_d, = add_call(arrays, places, "D", size)
        arrays, places = within(keep_r, send_r, "TSJ")
        from_d = to_s(sum_d)
        sum_s, = add_call(arrays, places, "S", size)
        from_s = to_s(sum_s)
        sum_t, = add_call([*arrays, from_d], [*places, "T"], "T", size)
        from_t = to_t(sum_t)
        from_s, grad_r = lax.optimization_barrier((from_s, grad_r))
        proxy_grad = proxy_call(grad_d, grad_r, [groups[3], groups[1], groups[2], groups[0]], picked)
        from_t, proxy_grad = lax.optimization_barrier((from_t, proxy_grad))
        mine, *others = own_call([*arrays, from_t, from_s], [*places, "J", "J"], depth, size)
        mine = finish_call(mine, reach(dict(enumerate(others, 1))))
        if narrow == 2:
            feature_grad = join_call(mine, to_core(mine, 1))
        else:
            mine = mine[None]
            for bit in range(narrow.bit_length() - 1):
                mine = jnp.concatenate([mine, to_core(mine, 1 << bit)], axis=0)
            feature_grad = jnp.take(mine, n ^ jnp.arange(narrow), axis=0).transpose(1, 0, 2).reshape(rows, width)
        return (feature_grad, proxy_grad)

    return per_device


def solution(mesh):
    placed = (P("wide", None), P(("wide", "narrow"), None), P(("wide", "narrow")), P(), P())
    return jax.shard_map(
        make(mesh.shape["wide"], mesh.shape["narrow"]),
        mesh=mesh,
        in_specs=placed,
        out_specs=(P("wide", None), P(("wide", "narrow"), None)),
        check_vma=False,
    )
```

```python
import functools
import math

import jax
import jax.numpy as jnp
from jax import lax
from jax.experimental import pallas as pl
from jax.experimental.pallas import tpu as pltpu
from jax.sharding import PartitionSpec as P

logit_scale = 3.0
epsilon = 1e-06
exp2_scale = logit_scale * math.log2(math.e)
chunk = 256
both = ("wide", "narrow")
whole = pl.BlockSpec(memory_space=pltpu.VMEM)
params = pltpu.CompilerParams(vmem_limit_bytes=8 * 1024 * 1024)
light = pl.CostEstimate(flops=0, bytes_accessed=1 << 19, transcendentals=0)
heavy = pl.CostEstimate(flops=0, bytes_accessed=10 << 20, transcendentals=0)


def t_bit(n):
    return 1 if n % 2 == 0 else 2


def s_bit(n):
    return 3 - t_bit(n)


def exchange(x, sizes, partner):
    wide, narrow = sizes
    pairs = []
    for w in range(wide):
        for n in range(narrow):
            pw, pn = partner(w, n)
            pairs.append((w * narrow + n, pw * narrow + pn))
    return lax.ppermute(x, both, pairs)


def logits_kernel(group_count, part_count, with_early, unit_ref, *refs):
    parts = refs[: group_count * part_count]
    shifted_ref, stats_ref = refs[-2:]
    per = chunk // 128
    first = 0
    if with_early:
        early_ref = refs[group_count * part_count]
        first = early_ref.shape[0] // 2
        half = stats_ref.shape[0] // 2
        stats_ref[0:first, :] = early_ref[0:first, :]
        stats_ref[half:half + first, :] = early_ref[first:, :]
    half = stats_ref.shape[0] // 2
    step = 0
    for g in range(group_count):
        group = parts[g * part_count:(g + 1) * part_count]
        cols = group[0].shape[1]
        for row in range(0, group[0].shape[0], chunk):
            dots = None
            for k, part in enumerate(group):
                prod = lax.dot_general(
                    unit_ref[:, k * cols:(k + 1) * cols], part[row:row + chunk, :],
                    (((1,), (1,)), ((), ())), preferred_element_type=jnp.float32,
                )
                dots = prod if dots is None else dots + prod
            top = jnp.max(dots, axis=0, keepdims=True)
            shifted = jnp.exp2((dots - top) * exp2_scale)
            total = jnp.sum(shifted, axis=0, keepdims=True)
            shifted_ref[:, step * chunk:(step + 1) * chunk] = shifted
            for b in range(per):
                at = first + step * per + b
                stats_ref[at:at + 1, :] = top[:, b * 128:(b + 1) * 128]
                stats_ref[half + at:half + at + 1, :] = total[:, b * 128:(b + 1) * 128]
            step += 1


def logits_call(unit, groups, early=None):
    rows = groups[0][0].shape[0]
    count = len(groups) * rows
    samples = unit.shape[0]
    flat = [part for group in groups for part in group]
    lines = 2 * count // 128
    if early is not None:
        lines += early.shape[0]
        flat.append(early)
    return pl.pallas_call(
        functools.partial(logits_kernel, len(groups), len(groups[0]), early is not None),
        out_shape=(
            jax.ShapeDtypeStruct((samples, count), jnp.float32),
            jax.ShapeDtypeStruct((lines, 128), jnp.float32),
        ),
        in_specs=[whole] * (1 + len(flat)),
        out_specs=(whole, whole),
        compiler_params=params,
        cost_estimate=pl.CostEstimate(
            flops=2 * samples * count * unit.shape[1],
            bytes_accessed=4 * samples * count,
            transcendentals=samples * count,
        ),
        name="logits",
    )(unit, *flat)


def grad_kernel(first, steps, depth, unit_t_ref, shifted_ref, scale_ref, weight_ref, at_ref, grad_ref, keep_ref, send_ref):
    samples = shifted_ref.shape[0]
    half = unit_t_ref.shape[0] // 2
    per = chunk // 128
    w, n = lax.axis_index("wide"), lax.axis_index("narrow")
    base = (w * lax.axis_size("narrow") + n) * samples
    cand = lax.broadcasted_iota(jnp.int32, (samples, chunk), 0) + base

    def row(ref, at):
        return jnp.concatenate([ref[at + b:at + b + 1, :] for b in range(per)], axis=1)

    def far_row(ref, at):
        lines = []
        for b in range(at, at + per):
            g, z = divmod(b, depth)
            offset = jnp.where(n % 2 == 0, 4 * z + g, 4 * z + (g % 2) * 2 + g // 2)
            lines.append(ref[pl.ds(jnp.bitwise_xor(w, offset), 1), :])
        return jnp.concatenate(lines, axis=1)

    for out, at in enumerate(steps):
        cols = slice((at - first) * chunk, (at - first + 1) * chunk)
        scale, weight, spot = row(scale_ref, at * per), far_row(weight_ref, at * per), far_row(at_ref, at * per)
        soft = shifted_ref[:, cols] * scale
        grad = (weight * jnp.where(cand == spot, soft - 1.0, soft)).astype(jnp.bfloat16)
        out_cols = slice(out * chunk, (out + 1) * chunk)
        grad_ref[:, out_cols] = grad
        shares = logit_scale * jnp.dot(unit_t_ref[...], grad, preferred_element_type=jnp.float32)
        keep_ref[:, out_cols] = shares[:half]
        send_ref[:, out_cols] = shares[half:].astype(jnp.bfloat16)


def grad_call(unit_t, shifted, scale, weight, spots, first, steps, depth):
    samples = shifted.shape[0]
    width = unit_t.shape[0]
    count = len(steps) * chunk
    return pl.pallas_call(
        functools.partial(grad_kernel, first, steps, depth),
        out_shape=(
            jax.ShapeDtypeStruct((samples, count), jnp.bfloat16),
            jax.ShapeDtypeStruct((width // 2, count), jnp.float32),
            jax.ShapeDtypeStruct((width // 2, count), jnp.bfloat16),
        ),
        in_specs=[whole] * 5,
        out_specs=(whole,) * 3,
        compiler_params=params,
        cost_estimate=pl.CostEstimate(
            flops=2 * samples * count * width, bytes_accessed=6 * samples * count, transcendentals=0
        ),
        name="grads",
    )(unit_t, shifted, scale, weight, spots)


def proxy_kernel(group_count, part_count, rows, late_ref, early_ref, *refs):
    parts = refs[:group_count * part_count]
    *picked_refs, out_ref = refs[group_count * part_count:]
    size, cols = parts[0].shape
    grads = [late_ref] + [early_ref.at[:, g * size:(g + 1) * size] for g in range(group_count - 1)]
    n = lax.axis_index("narrow")
    places = []
    for k in range(part_count):
        if part_count == 1:
            places.append(slice(0, cols))
        else:
            places.append(pl.ds(pl.multiple_of((n ^ k) * cols, cols), cols))
    tiles = [(ref, row) for ref in picked_refs for row in range(0, ref.shape[0], rows)]
    for tile, (picked_ref, row) in enumerate(tiles):
        at, here = slice(tile * rows, (tile + 1) * rows), slice(row, row + rows)
        sums = []
        for k in range(part_count):
            total = None
            for g in range(group_count):
                prod = jnp.dot(
                    grads[g][at, :], parts[g * part_count + k][...], preferred_element_type=jnp.float32
                )
                total = prod if total is None else total + prod
            sums.append(logit_scale * total)
        picked = [picked_ref[here, place] for place in places]
        square = functools.reduce(jnp.add, [jnp.sum(p * p, axis=1, keepdims=True) for p in picked])
        inverse = 1.0 / jnp.sqrt(square + epsilon)
        inner = functools.reduce(jnp.add, [jnp.sum(p * s, axis=1, keepdims=True) for p, s in zip(picked, sums)])
        slope = inner * inverse * inverse
        for place, p, s in zip(places, picked, sums):
            out_ref[at, place] = (s - p * slope) * inverse


def proxy_call(late, early, groups, picked):
    samples, width = late.shape[0], picked[0].shape[1]
    count = late.shape[1] + early.shape[1]
    flat = [part for group in groups for part in group]
    return pl.pallas_call(
        functools.partial(proxy_kernel, len(groups), len(groups[0]), 256),
        out_shape=jax.ShapeDtypeStruct((samples, width), jnp.float32),
        in_specs=[whole] * (len(flat) + 2 + len(picked)),
        out_specs=whole,
        compiler_params=params,
        cost_estimate=pl.CostEstimate(
            flops=2 * samples * count * width, bytes_accessed=4 * samples * count, transcendentals=0
        ),
        name="proxy_grads",
    )(late, early, *flat, *picked)


def merge_kernel(flips, swap, with_scale, *refs):
    ins, out_ref = refs[:-1], refs[-1]
    if with_scale:
        own_ref, ins = ins[-1], ins[:-1]
    blocks = ins[0].shape[0] // 2
    for b in range(blocks):
        spots = [swap(f, b) for f in flips]
        tops = [ref[at:at + 1, :] for ref, at in zip(ins, spots)]
        totals = [ref[blocks + at:blocks + at + 1, :] for ref, at in zip(ins, spots)]
        top = functools.reduce(jnp.maximum, tops)
        total = functools.reduce(
            jnp.add, [t * jnp.exp2((m - top) * exp2_scale) for m, t in zip(tops, totals)]
        )
        if with_scale:
            out_ref[b:b + 1, :] = jnp.exp2((own_ref[b:b + 1, :] - top) * exp2_scale) / total
        else:
            out_ref[b:b + 1, :] = top
            out_ref[blocks + b:blocks + b + 1, :] = total


def merge(stats, flips, swap, own=None):
    lines = stats[0].shape[0]
    if own is not None:
        stats, lines = [*stats, own], lines // 2
    return pl.pallas_call(
        functools.partial(merge_kernel, flips, swap, own is not None),
        out_shape=jax.ShapeDtypeStruct((lines, 128), jnp.float32),
        in_specs=[whole] * len(stats),
        out_specs=whole,
        compiler_params=params,
        cost_estimate=light,
        name="merge_stats",
    )(*stats)


def stack_kernel(places, *refs):
    rows = refs[0].shape[0]
    for k, ref in zip(places, refs):
        refs[-1][k * rows:(k + 1) * rows, :] = ref[...]


def stack_call(parts, places):
    rows, cols = parts[0].shape
    return pl.pallas_call(
        functools.partial(stack_kernel, places),
        out_shape=jax.ShapeDtypeStruct((len(parts) * rows, cols), parts[0].dtype),
        in_specs=[whole] * len(parts),
        out_specs=whole,
        compiler_params=params,
        cost_estimate=light,
        name="stack_blocks",
    )(*parts)


def add_kernel(ins, outs, size, *refs):
    for name, out_ref in zip(outs, refs[len(ins):]):
        total = None
        for places, ref in zip(ins, refs):
            if name in places:
                at = places.index(name)
                term = ref[:, at * size:(at + 1) * size].astype(jnp.float32)
                total = term if total is None else total + term
        out_ref[...] = total.astype(out_ref.dtype)


def add_call(arrays, ins, outs, size, dtype=jnp.bfloat16, cost=light):
    rows = arrays[0].shape[0]
    result = pl.pallas_call(
        functools.partial(add_kernel, ins, outs, size),
        out_shape=[jax.ShapeDtypeStruct((rows, size), dtype) for _ in outs],
        in_specs=[whole] * len(arrays),
        out_specs=[whole] * len(outs),
        compiler_params=params,
        cost_estimate=cost,
        name="add_shares",
    )(*arrays)
    return result


def own_kernel(ins, count, size, *refs):
    cols = size // count
    for k, out_ref in enumerate(refs[len(ins):]):
        total = None
        for places, ref in zip(ins, refs):
            at = places.index("J") * size + k * cols
            term = ref[:, at:at + cols].astype(jnp.float32)
            total = term if total is None else total + term
        out_ref[...] = total.astype(out_ref.dtype)


def own_call(arrays, ins, count, size):
    rows = arrays[0].shape[0]
    return pl.pallas_call(
        functools.partial(own_kernel, ins, count, size),
        out_shape=[
            jax.ShapeDtypeStruct((rows, size // count), jnp.bfloat16 if k else jnp.float32) for k in range(count)
        ],
        in_specs=[whole] * len(arrays),
        out_specs=[whole] * count,
        compiler_params=params,
        cost_estimate=light,
        name="add_shares_z",
    )(*arrays)


def prep_kernel(part_count, *refs):
    *picked_refs, unit_ref, unit_t_ref = refs
    width = picked_refs[0].shape[1]
    cols = width // part_count
    tiles = [(ref, row) for ref in picked_refs for row in range(0, ref.shape[0], 256)]
    n = lax.axis_index("narrow")
    for line, (picked_ref, row) in enumerate(tiles):
        line *= 256
        at = slice(row, row + 256)
        if part_count == 1:
            picked = picked_ref[at, :]
        else:
            picked = jnp.concatenate(
                [picked_ref[at, pl.ds(pl.multiple_of((n ^ k) * cols, cols), cols)] for k in range(part_count)],
                axis=1,
            )
        lengths = jnp.sqrt(jnp.sum(picked * picked, axis=1, keepdims=True) + epsilon)
        unit = picked / lengths
        unit_ref[line:line + 256, :] = unit.astype(jnp.bfloat16)
        unit_t_ref[:, line:line + 256] = unit.T.astype(jnp.bfloat16)


def prep_call(picked, part_count):
    samples, width = sum(p.shape[0] for p in picked), picked[0].shape[1]
    return pl.pallas_call(
        functools.partial(prep_kernel, part_count),
        out_shape=(
            jax.ShapeDtypeStruct((samples, width), jnp.bfloat16),
            jax.ShapeDtypeStruct((width, samples), jnp.bfloat16),
        ),
        in_specs=[whole] * len(picked),
        out_specs=(whole, whole),
        compiler_params=params,
        cost_estimate=pl.CostEstimate(flops=4 * samples * width, bytes_accessed=8 * samples * width, transcendentals=0),
        name="unit_rows",
    )(*picked)


def finish_kernel(*refs):
    ins, out_ref = refs[:-1], refs[-1]
    total = functools.reduce(jnp.add, [ref[...].astype(jnp.float32) for ref in ins])
    out_ref[...] = total.T


def finish_call(own, others):
    return pl.pallas_call(
        finish_kernel,
        out_shape=jax.ShapeDtypeStruct((own.shape[1], own.shape[0]), jnp.float32),
        in_specs=[whole] * (1 + len(others)),
        out_specs=whole,
        compiler_params=params,
        cost_estimate=light,
        name="feature_sums",
    )(own, *others)


def join_kernel(own_ref, other_ref, out_ref):
    cols = own_ref.shape[1]
    n = lax.axis_index("narrow")
    out_ref[:, pl.ds(pl.multiple_of(n * cols, cols), cols)] = own_ref[...]
    out_ref[:, pl.ds(pl.multiple_of((1 - n) * cols, cols), cols)] = other_ref[...]


def join_call(own, other):
    return pl.pallas_call(
        join_kernel,
        out_shape=jax.ShapeDtypeStruct((own.shape[0], 2 * own.shape[1]), jnp.float32),
        in_specs=[whole] * 2,
        out_specs=whole,
        compiler_params=params,
        cost_estimate=light,
        name="feature_grad",
    )(own, other)


def make(wide, narrow):
    depth = wide // 4
    sizes = (wide, narrow)
    send = functools.partial(exchange, sizes=sizes)

    def to_t(x):
        return send(x, partner=lambda w, n: (w ^ t_bit(n), n))

    def to_s(x):
        return send(x, partner=lambda w, n: (w ^ s_bit(n), n))

    def to_ts(x):
        return send(x, partner=lambda w, n: (w ^ 3, n))

    def to_z(x, k):
        return send(x, partner=lambda w, n: (w ^ (k << 2), n))

    far_first = sorted(range(1, depth), key=lambda k: (k == 1, k))

    def reach(parts):
        return [to_z(parts[k] if isinstance(parts, dict) else parts, k) for k in far_first]

    def to_core(x, k):
        return send(x, partner=lambda w, n: (w, n ^ k))

    def per_device(features, proxies, sample_ids, positives, loss_weight):
        samples = sample_ids.shape[0]
        rows, width = features.shape
        w = lax.axis_index("wide")
        n = lax.axis_index("narrow")

        if narrow == 2:
            cols = width // 2
            part = jnp.where(n == 0, features[:, :cols], features[:, cols:])
        else:
            part = features
        zs = reach(part)
        near = samples // 4
        picked = [
            proxies.at[ids].get(mode="promise_in_bounds", wrap_negative_indices=False)
            for ids in (sample_ids[:near], sample_ids[near:])
        ]
        *zs, picked[0] = lax.optimization_barrier((*zs, picked[0]))
        group_j = stack_call([part] + zs, [0] + far_first)
        group_t, group_s, picked[1] = lax.optimization_barrier((to_t(group_j), to_s(group_j), picked[1]))
        group_d = to_s(group_t)
        groups = [(group_j,), (group_t,), (group_s,)]
        if narrow == 2:
            others = [to_core(group_j, 1), to_core(group_s, 1), to_core(group_t, 1)]
            groups = [(*group, other) for group, other in zip(groups, others)]

        unit, unit_t = prep_call(picked, 2 if narrow == 2 else 1)
        if narrow != 2:
            unit_t = jnp.take(unit_t.reshape(narrow, width // narrow, samples), n ^ jnp.arange(narrow), axis=0)
            unit_t = unit_t.reshape(width, samples)

        spots = positives.reshape(wide, rows)
        weight = loss_weight.reshape(wide, rows)

        shifted_early, stats_early = logits_call(unit, groups)
        group_d, stats_early = lax.optimization_barrier((group_d, stats_early))
        groups.append((group_d, to_core(group_d, 1)) if narrow == 2 else (group_d,))
        shifted_late, own = logits_call(unit, groups[3:], stats_early)
        stats = own

        def swap_groups(flip, b):
            g, z = divmod(b, depth)
            return ((g % 2) * 2 + g // 2) * depth + z if flip else b

        for bit in range(narrow.bit_length() - 1):
            stats = merge([stats, to_core(stats, 1 << bit)], (0, int(bit == 0)), swap_groups)
        others = reach(stats)
        stats = merge([stats] + others, [0] + far_first, lambda k, b: b ^ k)
        others = [to_t(stats), to_s(stats), to_ts(stats)]
        scale = merge([stats] + others, (0, 1, 2, 3), lambda k, b: b ^ (k * depth), own)

        per = depth * rows // chunk
        order_t, order_s, order_j = range(per, 2 * per), range(2 * per, 3 * per), range(per)
        size = depth * rows
        low = jnp.bfloat16
        grad_d, keep_d, send_d = grad_call(
            unit_t, shifted_late, scale, weight, spots, 3 * per, tuple(range(3 * per, 4 * per)), depth
        )
        grad_r, keep_r, send_r = grad_call(
            unit_t, shifted_early, scale, weight, spots, 0, (*order_t, *order_s, *order_j), depth
        )

        def within(keep, out, names):
            for bit in range(narrow.bit_length() - 2, 0, -1):
                keep = keep + to_core(out, 1 << bit).astype(jnp.float32)
                half = keep.shape[0] // 2
                keep, out = keep[:half], keep[half:].astype(low)
            return [keep, to_core(out, 1)], [names, names.translate(str.maketrans("TS", "ST"))]

        arrays, places = within(keep_d, send_d, "D")
        arrays[1], send_r = lax.optimization_barrier((arrays[1], send_r))
        sum_d, = add_call(arrays, places, "D", size)
        arrays, places = within(keep_r, send_r, "TSJ")
        from_d = to_s(sum_d)
        sum_s, = add_call(arrays, places, "S", size)
        from_s = to_s(sum_s)
        sum_t, = add_call([*arrays, from_d], [*places, "T"], "T", size)
        from_t = to_t(sum_t)
        sum_j, = add_call([*arrays, from_s], [*places, "J"], "J", size, jnp.float32, heavy)
        mine, *others = own_call([sum_j, from_t], "JJ", depth, size)
        others = reach(dict(enumerate(others, 1)))
        proxy_grad = proxy_call(grad_d, grad_r, [groups[3], groups[1], groups[2], groups[0]], picked)
        *others, proxy_grad = lax.optimization_barrier((*others, proxy_grad))
        mine = finish_call(mine, others)
        if narrow == 2:
            feature_grad = join_call(mine, to_core(mine, 1))
        else:
            mine = mine[None]
            for bit in range(narrow.bit_length() - 1):
                mine = jnp.concatenate([mine, to_core(mine, 1 << bit)], axis=0)
            feature_grad = jnp.take(mine, n ^ jnp.arange(narrow), axis=0).transpose(1, 0, 2).reshape(rows, width)
        return (feature_grad, proxy_grad)

    return per_device


def solution(mesh):
    placed = (P("wide", None), P(("wide", "narrow"), None), P(("wide", "narrow")), P(), P())
    return jax.shard_map(
        make(mesh.shape["wide"], mesh.shape["narrow"]),
        mesh=mesh,
        in_specs=placed,
        out_specs=(P("wide", None), P(("wide", "narrow"), None)),
        check_vma=False,
    )
```

```python
import functools
import math

import jax
import jax.numpy as jnp
from jax import lax
from jax.experimental import pallas as pl
from jax.experimental.pallas import tpu as pltpu
from jax.sharding import PartitionSpec as P

logit_scale = 3.0
epsilon = 1e-06
exp2_scale = logit_scale * math.log2(math.e)
chunk = 256
both = ("wide", "narrow")
whole = pl.BlockSpec(memory_space=pltpu.VMEM)
params = pltpu.CompilerParams(vmem_limit_bytes=8 * 1024 * 1024)
light = pl.CostEstimate(flops=0, bytes_accessed=1 << 19, transcendentals=0)
heavy = pl.CostEstimate(flops=0, bytes_accessed=10 << 20, transcendentals=0)


def t_bit(n):
    return 1 if n % 2 == 0 else 2


def s_bit(n):
    return 3 - t_bit(n)


def exchange(x, sizes, partner, senders=None):
    wide, narrow = sizes
    pairs = []
    for w in range(wide):
        for n in range(narrow) if senders is None else senders:
            pw, pn = partner(w, n)
            pairs.append((w * narrow + n, pw * narrow + pn))
    return lax.ppermute(x, both, pairs)


def logits_kernel(group_count, part_count, with_early, unit_ref, *refs):
    parts = refs[: group_count * part_count]
    shifted_ref, stats_ref = refs[-2:]
    per = chunk // 128
    first = 0
    if with_early:
        early_ref = refs[group_count * part_count]
        first = early_ref.shape[0] // 2
        half = stats_ref.shape[0] // 2
        stats_ref[0:first, :] = early_ref[0:first, :]
        stats_ref[half:half + first, :] = early_ref[first:, :]
    half = stats_ref.shape[0] // 2
    step = 0
    for g in range(group_count):
        group = parts[g * part_count:(g + 1) * part_count]
        cols = group[0].shape[1]
        for row in range(0, group[0].shape[0], chunk):
            dots = None
            for k, part in enumerate(group):
                prod = lax.dot_general(
                    unit_ref[:, k * cols:(k + 1) * cols], part[row:row + chunk, :],
                    (((1,), (1,)), ((), ())), preferred_element_type=jnp.float32,
                )
                dots = prod if dots is None else dots + prod
            top = jnp.max(dots, axis=0, keepdims=True)
            shifted = jnp.exp2((dots - top) * exp2_scale)
            total = jnp.sum(shifted, axis=0, keepdims=True)
            shifted_ref[:, step * chunk:(step + 1) * chunk] = shifted
            for b in range(per):
                at = first + step * per + b
                stats_ref[at:at + 1, :] = top[:, b * 128:(b + 1) * 128]
                stats_ref[half + at:half + at + 1, :] = total[:, b * 128:(b + 1) * 128]
            step += 1


def logits_call(unit, groups, early=None):
    rows = groups[0][0].shape[0]
    count = len(groups) * rows
    samples = unit.shape[0]
    flat = [part for group in groups for part in group]
    lines = 2 * count // 128
    if early is not None:
        lines += early.shape[0]
        flat.append(early)
    return pl.pallas_call(
        functools.partial(logits_kernel, len(groups), len(groups[0]), early is not None),
        out_shape=(
            jax.ShapeDtypeStruct((samples, count), jnp.float32),
            jax.ShapeDtypeStruct((lines, 128), jnp.float32),
        ),
        in_specs=[whole] * (1 + len(flat)),
        out_specs=(whole, whole),
        compiler_params=params,
        cost_estimate=pl.CostEstimate(
            flops=2 * samples * count * unit.shape[1],
            bytes_accessed=4 * samples * count,
            transcendentals=samples * count,
        ),
        name="logits",
    )(unit, *flat)


def grad_kernel(first, steps, depth, unit_t_ref, shifted_ref, scale_ref, weight_ref, at_ref, grad_ref, keep_ref, send_ref):
    samples = shifted_ref.shape[0]
    half = unit_t_ref.shape[0] // 2
    per = chunk // 128
    w, n = lax.axis_index("wide"), lax.axis_index("narrow")
    base = (w * lax.axis_size("narrow") + n) * samples
    cand = lax.broadcasted_iota(jnp.int32, (samples, chunk), 0) + base

    def row(ref, at):
        return jnp.concatenate([ref[at + b:at + b + 1, :] for b in range(per)], axis=1)

    def far_row(ref, at):
        lines = []
        for b in range(at, at + per):
            g, z = divmod(b, depth)
            offset = jnp.where(n % 2 == 0, 4 * z + g, 4 * z + (g % 2) * 2 + g // 2)
            lines.append(ref[pl.ds(jnp.bitwise_xor(w, offset), 1), :])
        return jnp.concatenate(lines, axis=1)

    for out, at in enumerate(steps):
        cols = slice((at - first) * chunk, (at - first + 1) * chunk)
        scale, weight, spot = row(scale_ref, at * per), far_row(weight_ref, at * per), far_row(at_ref, at * per)
        soft = shifted_ref[:, cols] * scale
        grad = (weight * jnp.where(cand == spot, soft - 1.0, soft)).astype(jnp.bfloat16)
        out_cols = slice(out * chunk, (out + 1) * chunk)
        grad_ref[:, out_cols] = grad
        shares = logit_scale * jnp.dot(unit_t_ref[...], grad, preferred_element_type=jnp.float32)
        keep_ref[:, out_cols] = shares[:half]
        send_ref[:, out_cols] = shares[half:].astype(jnp.bfloat16)


def grad_call(unit_t, shifted, scale, weight, spots, first, steps, depth):
    samples = shifted.shape[0]
    width = unit_t.shape[0]
    count = len(steps) * chunk
    return pl.pallas_call(
        functools.partial(grad_kernel, first, steps, depth),
        out_shape=(
            jax.ShapeDtypeStruct((samples, count), jnp.bfloat16),
            jax.ShapeDtypeStruct((width // 2, count), jnp.float32),
            jax.ShapeDtypeStruct((width // 2, count), jnp.bfloat16),
        ),
        in_specs=[whole] * 5,
        out_specs=(whole,) * 3,
        compiler_params=params,
        cost_estimate=pl.CostEstimate(
            flops=2 * samples * count * width, bytes_accessed=6 * samples * count, transcendentals=0
        ),
        name="grads",
    )(unit_t, shifted, scale, weight, spots)


def proxy_kernel(group_count, part_count, rows, late_ref, early_ref, *refs):
    parts = refs[:group_count * part_count]
    *picked_refs, out_ref = refs[group_count * part_count:]
    size, cols = parts[0].shape
    grads = [late_ref] + [early_ref.at[:, g * size:(g + 1) * size] for g in range(group_count - 1)]
    n = lax.axis_index("narrow")
    places = []
    for k in range(part_count):
        if part_count == 1:
            places.append(slice(0, cols))
        else:
            places.append(pl.ds(pl.multiple_of((n ^ k) * cols, cols), cols))
    tiles = [(ref, row) for ref in picked_refs for row in range(0, ref.shape[0], rows)]
    for tile, (picked_ref, row) in enumerate(tiles):
        at, here = slice(tile * rows, (tile + 1) * rows), slice(row, row + rows)
        sums = []
        for k in range(part_count):
            total = None
            for g in range(group_count):
                prod = jnp.dot(
                    grads[g][at, :], parts[g * part_count + k][...], preferred_element_type=jnp.float32
                )
                total = prod if total is None else total + prod
            sums.append(logit_scale * total)
        picked = [picked_ref[here, place] for place in places]
        square = functools.reduce(jnp.add, [jnp.sum(p * p, axis=1, keepdims=True) for p in picked])
        inverse = 1.0 / jnp.sqrt(square + epsilon)
        inner = functools.reduce(jnp.add, [jnp.sum(p * s, axis=1, keepdims=True) for p, s in zip(picked, sums)])
        slope = inner * inverse * inverse
        for place, p, s in zip(places, picked, sums):
            out_ref[at, place] = (s - p * slope) * inverse


def proxy_call(late, early, groups, picked):
    samples, width = late.shape[0], picked[0].shape[1]
    count = late.shape[1] + early.shape[1]
    flat = [part for group in groups for part in group]
    return pl.pallas_call(
        functools.partial(proxy_kernel, len(groups), len(groups[0]), 256),
        out_shape=jax.ShapeDtypeStruct((samples, width), jnp.float32),
        in_specs=[whole] * (len(flat) + 2 + len(picked)),
        out_specs=whole,
        compiler_params=params,
        cost_estimate=pl.CostEstimate(
            flops=2 * samples * count * width, bytes_accessed=4 * samples * count, transcendentals=0
        ),
        name="proxy_grads",
    )(late, early, *flat, *picked)


def merge_kernel(flips, swap, with_scale, *refs):
    ins, out_ref = refs[:-1], refs[-1]
    if with_scale:
        own_ref, ins = ins[-1], ins[:-1]
    blocks = ins[0].shape[0] // 2
    for b in range(blocks):
        spots = [swap(f, b) for f in flips]
        tops = [ref[at:at + 1, :] for ref, at in zip(ins, spots)]
        totals = [ref[blocks + at:blocks + at + 1, :] for ref, at in zip(ins, spots)]
        top = functools.reduce(jnp.maximum, tops)
        total = functools.reduce(
            jnp.add, [t * jnp.exp2((m - top) * exp2_scale) for m, t in zip(tops, totals)]
        )
        if with_scale:
            out_ref[b:b + 1, :] = jnp.exp2((own_ref[b:b + 1, :] - top) * exp2_scale) / total
        else:
            out_ref[b:b + 1, :] = top
            out_ref[blocks + b:blocks + b + 1, :] = total


def merge(stats, flips, swap, own=None):
    lines = stats[0].shape[0]
    if own is not None:
        stats, lines = [*stats, own], lines // 2
    return pl.pallas_call(
        functools.partial(merge_kernel, flips, swap, own is not None),
        out_shape=jax.ShapeDtypeStruct((lines, 128), jnp.float32),
        in_specs=[whole] * len(stats),
        out_specs=whole,
        compiler_params=params,
        cost_estimate=light,
        name="merge_stats",
    )(*stats)


def scale_kernel(swap, own_ref, merged_ref, other_ref, out_ref):
    blocks = out_ref.shape[0]
    odd = lax.axis_index("narrow") % 2 == 1
    for b in range(blocks):
        far = swap(1, b)
        top = jnp.where(odd, merged_ref[b:b + 1, :], other_ref[far:far + 1, :])
        total = jnp.where(
            odd, merged_ref[blocks + b:blocks + b + 1, :], other_ref[blocks + far:blocks + far + 1, :]
        )
        out_ref[b:b + 1, :] = jnp.exp2((own_ref[b:b + 1, :] - top) * exp2_scale) / total


def scale_call(own, merged, other, swap):
    return pl.pallas_call(
        functools.partial(scale_kernel, swap),
        out_shape=jax.ShapeDtypeStruct((own.shape[0] // 2, 128), jnp.float32),
        in_specs=[whole] * 3,
        out_specs=whole,
        compiler_params=params,
        cost_estimate=light,
        name="scale_rows",
    )(own, merged, other)


def stack_kernel(places, *refs):
    rows = refs[0].shape[0]
    for k, ref in zip(places, refs):
        refs[-1][k * rows:(k + 1) * rows, :] = ref[...]


def stack_call(parts, places):
    rows, cols = parts[0].shape
    return pl.pallas_call(
        functools.partial(stack_kernel, places),
        out_shape=jax.ShapeDtypeStruct((len(parts) * rows, cols), parts[0].dtype),
        in_specs=[whole] * len(parts),
        out_specs=whole,
        compiler_params=params,
        cost_estimate=light,
        name="stack_blocks",
    )(*parts)


def add_kernel(ins, outs, size, *refs):
    for name, out_ref in zip(outs, refs[len(ins):]):
        total = None
        for places, ref in zip(ins, refs):
            if name in places:
                at = places.index(name)
                term = ref[:, at * size:(at + 1) * size].astype(jnp.float32)
                total = term if total is None else total + term
        out_ref[...] = total.astype(out_ref.dtype)


def add_call(arrays, ins, outs, size, dtype=jnp.bfloat16, cost=light):
    rows = arrays[0].shape[0]
    result = pl.pallas_call(
        functools.partial(add_kernel, ins, outs, size),
        out_shape=[jax.ShapeDtypeStruct((rows, size), dtype) for _ in outs],
        in_specs=[whole] * len(arrays),
        out_specs=[whole] * len(outs),
        compiler_params=params,
        cost_estimate=cost,
        name="add_shares",
    )(*arrays)
    return result


def own_kernel(ins, count, size, *refs):
    cols = size // count
    for k, out_ref in enumerate(refs[len(ins):]):
        total = None
        for places, ref in zip(ins, refs):
            at = places.index("J") * size + k * cols
            term = ref[:, at:at + cols].astype(jnp.float32)
            total = term if total is None else total + term
        out_ref[...] = total.astype(out_ref.dtype)


def own_call(arrays, ins, count, size):
    rows = arrays[0].shape[0]
    return pl.pallas_call(
        functools.partial(own_kernel, ins, count, size),
        out_shape=[
            jax.ShapeDtypeStruct((rows, size // count), jnp.bfloat16 if k else jnp.float32) for k in range(count)
        ],
        in_specs=[whole] * len(arrays),
        out_specs=[whole] * count,
        compiler_params=params,
        cost_estimate=light,
        name="add_shares_z",
    )(*arrays)


def prep_kernel(part_count, *refs):
    *picked_refs, unit_ref, unit_t_ref = refs
    width = picked_refs[0].shape[1]
    cols = width // part_count
    tiles = [(ref, row) for ref in picked_refs for row in range(0, ref.shape[0], 256)]
    n = lax.axis_index("narrow")
    for line, (picked_ref, row) in enumerate(tiles):
        line *= 256
        at = slice(row, row + 256)
        if part_count == 1:
            picked = picked_ref[at, :]
        else:
            picked = jnp.concatenate(
                [picked_ref[at, pl.ds(pl.multiple_of((n ^ k) * cols, cols), cols)] for k in range(part_count)],
                axis=1,
            )
        lengths = jnp.sqrt(jnp.sum(picked * picked, axis=1, keepdims=True) + epsilon)
        unit = picked / lengths
        unit_ref[line:line + 256, :] = unit.astype(jnp.bfloat16)
        unit_t_ref[:, line:line + 256] = unit.T.astype(jnp.bfloat16)


def prep_call(picked, part_count):
    samples, width = sum(p.shape[0] for p in picked), picked[0].shape[1]
    return pl.pallas_call(
        functools.partial(prep_kernel, part_count),
        out_shape=(
            jax.ShapeDtypeStruct((samples, width), jnp.bfloat16),
            jax.ShapeDtypeStruct((width, samples), jnp.bfloat16),
        ),
        in_specs=[whole] * len(picked),
        out_specs=(whole, whole),
        compiler_params=params,
        cost_estimate=pl.CostEstimate(flops=4 * samples * width, bytes_accessed=8 * samples * width, transcendentals=0),
        name="unit_rows",
    )(*picked)


def finish_kernel(*refs):
    ins, out_ref = refs[:-1], refs[-1]
    total = functools.reduce(jnp.add, [ref[...].astype(jnp.float32) for ref in ins])
    out_ref[...] = total.T


def finish_call(own, others):
    return pl.pallas_call(
        finish_kernel,
        out_shape=jax.ShapeDtypeStruct((own.shape[1], own.shape[0]), jnp.float32),
        in_specs=[whole] * (1 + len(others)),
        out_specs=whole,
        compiler_params=params,
        cost_estimate=light,
        name="feature_sums",
    )(own, *others)


def join_kernel(own_ref, other_ref, out_ref):
    cols = own_ref.shape[1]
    n = lax.axis_index("narrow")
    out_ref[:, pl.ds(pl.multiple_of(n * cols, cols), cols)] = own_ref[...]
    out_ref[:, pl.ds(pl.multiple_of((1 - n) * cols, cols), cols)] = other_ref[...]


def join_call(own, other):
    return pl.pallas_call(
        join_kernel,
        out_shape=jax.ShapeDtypeStruct((own.shape[0], 2 * own.shape[1]), jnp.float32),
        in_specs=[whole] * 2,
        out_specs=whole,
        compiler_params=params,
        cost_estimate=light,
        name="feature_grad",
    )(own, other)


def make(wide, narrow):
    depth = wide // 4
    sizes = (wide, narrow)
    send = functools.partial(exchange, sizes=sizes)

    def to_t(x, senders=None):
        return send(x, partner=lambda w, n: (w ^ t_bit(n), n), senders=senders)

    def to_s(x, senders=None):
        return send(x, partner=lambda w, n: (w ^ s_bit(n), n), senders=senders)

    def to_ts(x, senders=None):
        return send(x, partner=lambda w, n: (w ^ 3, n), senders=senders)

    def to_z(x, k, senders=None):
        return send(x, partner=lambda w, n: (w ^ (k << 2), n), senders=senders)

    far_first = sorted(range(1, depth), key=lambda k: (k == 1, k))

    def reach(parts, senders=None):
        return [to_z(parts[k] if isinstance(parts, dict) else parts, k, senders) for k in far_first]

    def to_core(x, k, senders=None):
        return send(x, partner=lambda w, n: (w, n ^ k), senders=senders)

    def per_device(features, proxies, sample_ids, positives, loss_weight):
        samples = sample_ids.shape[0]
        rows, width = features.shape
        w = lax.axis_index("wide")
        n = lax.axis_index("narrow")

        if narrow == 2:
            cols = width // 2
            part = jnp.where(n == 0, features[:, :cols], features[:, cols:])
        else:
            part = features
        zs = reach(part)
        near = samples // 4
        picked = [
            proxies.at[ids].get(mode="promise_in_bounds", wrap_negative_indices=False)
            for ids in (sample_ids[:near], sample_ids[near:])
        ]
        *zs, picked[0] = lax.optimization_barrier((*zs, picked[0]))
        group_j = stack_call([part] + zs, [0] + far_first)
        group_t, group_s, picked[1] = lax.optimization_barrier((to_t(group_j), to_s(group_j), picked[1]))
        group_d = to_s(group_t)
        groups = [(group_j,), (group_t,), (group_s,)]
        if narrow == 2:
            others = [to_core(group_j, 1), to_core(group_s, 1), to_core(group_t, 1)]
            groups = [(*group, other) for group, other in zip(groups, others)]

        unit, unit_t = prep_call(picked, 2 if narrow == 2 else 1)
        if narrow != 2:
            unit_t = jnp.take(unit_t.reshape(narrow, width // narrow, samples), n ^ jnp.arange(narrow), axis=0)
            unit_t = unit_t.reshape(width, samples)

        spots = positives.reshape(wide, rows)
        weight = loss_weight.reshape(wide, rows)

        shifted_early, stats_early = logits_call(unit, groups)
        group_d, stats_early = lax.optimization_barrier((group_d, stats_early))
        groups.append((group_d, to_core(group_d, 1)) if narrow == 2 else (group_d,))
        shifted_late, own = logits_call(unit, groups[3:], stats_early)
        stats = own

        def swap_groups(flip, b):
            g, z = divmod(b, depth)
            return ((g % 2) * 2 + g // 2) * depth + z if flip else b

        one = (1,) if narrow == 2 else None
        if narrow == 2:
            stats = merge([stats, to_core(stats, 1, (0,))], (0, 1), swap_groups)
        else:
            for bit in range(narrow.bit_length() - 1):
                stats = merge([stats, to_core(stats, 1 << bit)], (0, int(bit == 0)), swap_groups)
        others = reach(stats, one)
        stats = merge([stats] + others, [0] + far_first, lambda k, b: b ^ k)
        others = [to_t(stats, one), to_s(stats, one), to_ts(stats, one)]
        last = [stats] + others, (0, 1, 2, 3), lambda k, b: b ^ (k * depth)
        if narrow == 2:
            stats = merge(*last)
            scale = scale_call(own, stats, to_core(stats, 1, one), swap_groups)
        else:
            scale = merge(*last, own)

        per = depth * rows // chunk
        order_t, order_s, order_j = range(per, 2 * per), range(2 * per, 3 * per), range(per)
        size = depth * rows
        low = jnp.bfloat16
        grad_d, keep_d, send_d = grad_call(
            unit_t, shifted_late, scale, weight, spots, 3 * per, tuple(range(3 * per, 4 * per)), depth
        )
        grad_r, keep_r, send_r = grad_call(
            unit_t, shifted_early, scale, weight, spots, 0, (*order_t, *order_s, *order_j), depth
        )

        def within(keep, out, names):
            for bit in range(narrow.bit_length() - 2, 0, -1):
                keep = keep + to_core(out, 1 << bit).astype(jnp.float32)
                half = keep.shape[0] // 2
                keep, out = keep[:half], keep[half:].astype(low)
            return [keep, to_core(out, 1)], [names, names.translate(str.maketrans("TS", "ST"))]

        arrays, places = within(keep_d, send_d, "D")
        arrays[1], send_r = lax.optimization_barrier((arrays[1], send_r))
        sum_d, = add_call(arrays, places, "D", size)
        arrays, places = within(keep_r, send_r, "TSJ")
        from_d = to_s(sum_d)
        sum_s, = add_call(arrays, places, "S", size)
        from_s = to_s(sum_s)
        sum_t, = add_call([*arrays, from_d], [*places, "T"], "T", size)
        from_t = to_t(sum_t)
        sum_j, = add_call([*arrays, from_s], [*places, "J"], "J", size, jnp.float32, heavy)
        mine, *others = own_call([sum_j, from_t], "JJ", depth, size)
        others = reach(dict(enumerate(others, 1)))
        proxy_grad = proxy_call(grad_d, grad_r, [groups[3], groups[1], groups[2], groups[0]], picked)
        *others, proxy_grad = lax.optimization_barrier((*others, proxy_grad))
        mine = finish_call(mine, others)
        if narrow == 2:
            feature_grad = join_call(mine, to_core(mine, 1))
        else:
            mine = mine[None]
            for bit in range(narrow.bit_length() - 1):
                mine = jnp.concatenate([mine, to_core(mine, 1 << bit)], axis=0)
            feature_grad = jnp.take(mine, n ^ jnp.arange(narrow), axis=0).transpose(1, 0, 2).reshape(rows, width)
        return (feature_grad, proxy_grad)

    return per_device


def solution(mesh):
    placed = (P("wide", None), P(("wide", "narrow"), None), P(("wide", "narrow")), P(), P())
    return jax.shard_map(
        make(mesh.shape["wide"], mesh.shape["narrow"]),
        mesh=mesh,
        in_specs=placed,
        out_specs=(P("wide", None), P(("wide", "narrow"), None)),
        check_vma=False,
    )
```

```python
import functools
import math

import jax
import jax.numpy as jnp
from jax import lax
from jax.experimental import pallas as pl
from jax.experimental.pallas import tpu as pltpu
from jax.sharding import PartitionSpec as P

logit_scale = 3.0
epsilon = 1e-06
exp2_scale = logit_scale * math.log2(math.e)
chunk = 256
both = ("wide", "narrow")
whole = pl.BlockSpec(memory_space=pltpu.VMEM)
params = pltpu.CompilerParams(vmem_limit_bytes=8 * 1024 * 1024)
light = pl.CostEstimate(flops=0, bytes_accessed=1 << 19, transcendentals=0)
heavy = pl.CostEstimate(flops=0, bytes_accessed=10 << 20, transcendentals=0)


def t_bit(n):
    return 1 if n % 2 == 0 else 2


def s_bit(n):
    return 3 - t_bit(n)


def exchange(x, sizes, partner):
    wide, narrow = sizes
    pairs = []
    for w in range(wide):
        for n in range(narrow):
            pw, pn = partner(w, n)
            pairs.append((w * narrow + n, pw * narrow + pn))
    return lax.ppermute(x, both, pairs)


def logits_kernel(group_count, part_count, with_early, unit_ref, *refs):
    parts = refs[: group_count * part_count]
    shifted_ref, stats_ref = refs[-2:]
    per = chunk // 128
    first = 0
    if with_early:
        early_ref = refs[group_count * part_count]
        first = early_ref.shape[0] // 2
        half = stats_ref.shape[0] // 2
        stats_ref[0:first, :] = early_ref[0:first, :]
        stats_ref[half:half + first, :] = early_ref[first:, :]
    half = stats_ref.shape[0] // 2
    step = 0
    for g in range(group_count):
        group = parts[g * part_count:(g + 1) * part_count]
        cols = group[0].shape[1]
        for row in range(0, group[0].shape[0], chunk):
            dots = None
            for k, part in enumerate(group):
                prod = lax.dot_general(
                    unit_ref[:, k * cols:(k + 1) * cols], part[row:row + chunk, :],
                    (((1,), (1,)), ((), ())), preferred_element_type=jnp.float32,
                )
                dots = prod if dots is None else dots + prod
            top = jnp.max(dots, axis=0, keepdims=True)
            shifted = jnp.exp2((dots - top) * exp2_scale)
            total = jnp.sum(shifted, axis=0, keepdims=True)
            shifted_ref[:, step * chunk:(step + 1) * chunk] = shifted
            for b in range(per):
                at = first + step * per + b
                stats_ref[at:at + 1, :] = top[:, b * 128:(b + 1) * 128]
                stats_ref[half + at:half + at + 1, :] = total[:, b * 128:(b + 1) * 128]
            step += 1


def logits_call(unit, groups, early=None):
    rows = groups[0][0].shape[0]
    count = len(groups) * rows
    samples = unit.shape[0]
    flat = [part for group in groups for part in group]
    lines = 2 * count // 128
    if early is not None:
        lines += early.shape[0]
        flat.append(early)
    return pl.pallas_call(
        functools.partial(logits_kernel, len(groups), len(groups[0]), early is not None),
        out_shape=(
            jax.ShapeDtypeStruct((samples, count), jnp.float32),
            jax.ShapeDtypeStruct((lines, 128), jnp.float32),
        ),
        in_specs=[whole] * (1 + len(flat)),
        out_specs=(whole, whole),
        compiler_params=params,
        cost_estimate=pl.CostEstimate(
            flops=2 * samples * count * unit.shape[1],
            bytes_accessed=4 * samples * count,
            transcendentals=samples * count,
        ),
        name="logits",
    )(unit, *flat)


def grad_kernel(first, steps, depth, unit_t_ref, shifted_ref, scale_ref, weight_ref, at_ref, grad_ref, keep_ref, send_ref):
    samples = shifted_ref.shape[0]
    half = unit_t_ref.shape[0] // 2
    per = chunk // 128
    w, n = lax.axis_index("wide"), lax.axis_index("narrow")
    base = (w * lax.axis_size("narrow") + n) * samples
    cand = lax.broadcasted_iota(jnp.int32, (samples, chunk), 0) + base

    def row(ref, at):
        return jnp.concatenate([ref[at + b:at + b + 1, :] for b in range(per)], axis=1)

    def far_row(ref, at):
        lines = []
        for b in range(at, at + per):
            g, z = divmod(b, depth)
            offset = jnp.where(n % 2 == 0, 4 * z + g, 4 * z + (g % 2) * 2 + g // 2)
            lines.append(ref[pl.ds(jnp.bitwise_xor(w, offset), 1), :])
        return jnp.concatenate(lines, axis=1)

    for out, at in enumerate(steps):
        cols = slice((at - first) * chunk, (at - first + 1) * chunk)
        scale, weight, spot = row(scale_ref, at * per), far_row(weight_ref, at * per), far_row(at_ref, at * per)
        soft = shifted_ref[:, cols] * scale
        grad = (weight * jnp.where(cand == spot, soft - 1.0, soft)).astype(jnp.bfloat16)
        out_cols = slice(out * chunk, (out + 1) * chunk)
        grad_ref[:, out_cols] = grad
        shares = logit_scale * jnp.dot(unit_t_ref[...], grad, preferred_element_type=jnp.float32)
        keep_ref[:, out_cols] = shares[:half]
        send_ref[:, out_cols] = shares[half:].astype(jnp.bfloat16)


def grad_call(unit_t, shifted, scale, weight, spots, first, steps, depth):
    samples = shifted.shape[0]
    width = unit_t.shape[0]
    count = len(steps) * chunk
    return pl.pallas_call(
        functools.partial(grad_kernel, first, steps, depth),
        out_shape=(
            jax.ShapeDtypeStruct((samples, count), jnp.bfloat16),
            jax.ShapeDtypeStruct((width // 2, count), jnp.float32),
            jax.ShapeDtypeStruct((width // 2, count), jnp.bfloat16),
        ),
        in_specs=[whole] * 5,
        out_specs=(whole,) * 3,
        compiler_params=params,
        cost_estimate=pl.CostEstimate(
            flops=2 * samples * count * width, bytes_accessed=6 * samples * count, transcendentals=0
        ),
        name="grads",
    )(unit_t, shifted, scale, weight, spots)


def proxy_kernel(grad_count, group_count, part_count, rows, *refs):
    grad_refs, refs = refs[:grad_count], refs[grad_count:]
    parts = refs[:group_count * part_count]
    *picked_refs, out_ref = refs[group_count * part_count:]
    size, cols = parts[0].shape
    grads = [ref.at[:, at:at + size] for ref in grad_refs for at in range(0, ref.shape[1], size)]
    n = lax.axis_index("narrow")
    places = []
    for k in range(part_count):
        if part_count == 1:
            places.append(slice(0, cols))
        else:
            places.append(pl.ds(pl.multiple_of((n ^ k) * cols, cols), cols))
    tiles = [(ref, row) for ref in picked_refs for row in range(0, ref.shape[0], rows)]
    for tile, (picked_ref, row) in enumerate(tiles):
        at, here = slice(tile * rows, (tile + 1) * rows), slice(row, row + rows)
        sums = []
        for k in range(part_count):
            total = None
            for g in range(group_count):
                prod = jnp.dot(
                    grads[g][at, :], parts[g * part_count + k][...], preferred_element_type=jnp.float32
                )
                total = prod if total is None else total + prod
            sums.append(logit_scale * total)
        picked = [picked_ref[here, place] for place in places]
        square = functools.reduce(jnp.add, [jnp.sum(p * p, axis=1, keepdims=True) for p in picked])
        inverse = 1.0 / jnp.sqrt(square + epsilon)
        inner = functools.reduce(jnp.add, [jnp.sum(p * s, axis=1, keepdims=True) for p, s in zip(picked, sums)])
        slope = inner * inverse * inverse
        for place, p, s in zip(places, picked, sums):
            out_ref[at, place] = (s - p * slope) * inverse


def proxy_call(grads, groups, picked):
    samples, width = grads[0].shape[0], picked[0].shape[1]
    count = sum(grad.shape[1] for grad in grads)
    flat = [part for group in groups for part in group]
    return pl.pallas_call(
        functools.partial(proxy_kernel, len(grads), len(groups), len(groups[0]), 256),
        out_shape=jax.ShapeDtypeStruct((samples, width), jnp.float32),
        in_specs=[whole] * (len(grads) + len(flat) + len(picked)),
        out_specs=whole,
        compiler_params=params,
        cost_estimate=pl.CostEstimate(
            flops=2 * samples * count * width, bytes_accessed=4 * samples * count, transcendentals=0
        ),
        name="proxy_grads",
    )(*grads, *flat, *picked)


def merge_kernel(flips, swap, with_scale, *refs):
    ins, out_ref = refs[:-1], refs[-1]
    if with_scale:
        own_ref, ins = ins[-1], ins[:-1]
    blocks = ins[0].shape[0] // 2
    for b in range(blocks):
        spots = [swap(f, b) for f in flips]
        tops = [ref[at:at + 1, :] for ref, at in zip(ins, spots)]
        totals = [ref[blocks + at:blocks + at + 1, :] for ref, at in zip(ins, spots)]
        top = functools.reduce(jnp.maximum, tops)
        total = functools.reduce(
            jnp.add, [t * jnp.exp2((m - top) * exp2_scale) for m, t in zip(tops, totals)]
        )
        if with_scale:
            out_ref[b:b + 1, :] = jnp.exp2((own_ref[b:b + 1, :] - top) * exp2_scale) / total
        else:
            out_ref[b:b + 1, :] = top
            out_ref[blocks + b:blocks + b + 1, :] = total


def merge(stats, flips, swap, own=None):
    lines = stats[0].shape[0]
    if own is not None:
        stats, lines = [*stats, own], lines // 2
    return pl.pallas_call(
        functools.partial(merge_kernel, flips, swap, own is not None),
        out_shape=jax.ShapeDtypeStruct((lines, 128), jnp.float32),
        in_specs=[whole] * len(stats),
        out_specs=whole,
        compiler_params=params,
        cost_estimate=light,
        name="merge_stats",
    )(*stats)


def stack_kernel(places, *refs):
    rows = refs[0].shape[0]
    for k, ref in zip(places, refs):
        refs[-1][k * rows:(k + 1) * rows, :] = ref[...]


def stack_call(parts, places):
    rows, cols = parts[0].shape
    return pl.pallas_call(
        functools.partial(stack_kernel, places),
        out_shape=jax.ShapeDtypeStruct((len(parts) * rows, cols), parts[0].dtype),
        in_specs=[whole] * len(parts),
        out_specs=whole,
        compiler_params=params,
        cost_estimate=light,
        name="stack_blocks",
    )(*parts)


def add_kernel(ins, outs, size, *refs):
    for name, out_ref in zip(outs, refs[len(ins):]):
        total = None
        for places, ref in zip(ins, refs):
            if name in places:
                at = places.index(name)
                term = ref[:, at * size:(at + 1) * size].astype(jnp.float32)
                total = term if total is None else total + term
        out_ref[...] = total.astype(out_ref.dtype)


def add_call(arrays, ins, outs, size, dtype=jnp.bfloat16, cost=light):
    rows = arrays[0].shape[0]
    result = pl.pallas_call(
        functools.partial(add_kernel, ins, outs, size),
        out_shape=[jax.ShapeDtypeStruct((rows, size), dtype) for _ in outs],
        in_specs=[whole] * len(arrays),
        out_specs=[whole] * len(outs),
        compiler_params=params,
        cost_estimate=cost,
        name="add_shares",
    )(*arrays)
    return result


def own_kernel(ins, count, size, *refs):
    cols = size // count
    for k, out_ref in enumerate(refs[len(ins):]):
        total = None
        for places, ref in zip(ins, refs):
            at = places.index("J") * size + k * cols
            term = ref[:, at:at + cols].astype(jnp.float32)
            total = term if total is None else total + term
        out_ref[...] = total.astype(out_ref.dtype)


def own_call(arrays, ins, count, size):
    rows = arrays[0].shape[0]
    return pl.pallas_call(
        functools.partial(own_kernel, ins, count, size),
        out_shape=[
            jax.ShapeDtypeStruct((rows, size // count), jnp.bfloat16 if k else jnp.float32) for k in range(count)
        ],
        in_specs=[whole] * len(arrays),
        out_specs=[whole] * count,
        compiler_params=params,
        cost_estimate=light,
        name="add_shares_z",
    )(*arrays)


def prep_kernel(part_count, *refs):
    *picked_refs, unit_ref, unit_t_ref = refs
    width = picked_refs[0].shape[1]
    cols = width // part_count
    tiles = [(ref, row) for ref in picked_refs for row in range(0, ref.shape[0], 256)]
    n = lax.axis_index("narrow")
    for line, (picked_ref, row) in enumerate(tiles):
        line *= 256
        at = slice(row, row + 256)
        if part_count == 1:
            picked = picked_ref[at, :]
        else:
            picked = jnp.concatenate(
                [picked_ref[at, pl.ds(pl.multiple_of((n ^ k) * cols, cols), cols)] for k in range(part_count)],
                axis=1,
            )
        lengths = jnp.sqrt(jnp.sum(picked * picked, axis=1, keepdims=True) + epsilon)
        unit = picked / lengths
        unit_ref[line:line + 256, :] = unit.astype(jnp.bfloat16)
        unit_t_ref[:, line:line + 256] = unit.T.astype(jnp.bfloat16)


def prep_call(picked, part_count):
    samples, width = sum(p.shape[0] for p in picked), picked[0].shape[1]
    return pl.pallas_call(
        functools.partial(prep_kernel, part_count),
        out_shape=(
            jax.ShapeDtypeStruct((samples, width), jnp.bfloat16),
            jax.ShapeDtypeStruct((width, samples), jnp.bfloat16),
        ),
        in_specs=[whole] * len(picked),
        out_specs=(whole, whole),
        compiler_params=params,
        cost_estimate=pl.CostEstimate(flops=4 * samples * width, bytes_accessed=8 * samples * width, transcendentals=0),
        name="unit_rows",
    )(*picked)


def finish_kernel(*refs):
    ins, out_ref = refs[:-1], refs[-1]
    total = functools.reduce(jnp.add, [ref[...].astype(jnp.float32) for ref in ins])
    out_ref[...] = total.T


def finish_call(own, others):
    return pl.pallas_call(
        finish_kernel,
        out_shape=jax.ShapeDtypeStruct((own.shape[1], own.shape[0]), jnp.float32),
        in_specs=[whole] * (1 + len(others)),
        out_specs=whole,
        compiler_params=params,
        cost_estimate=light,
        name="feature_sums",
    )(own, *others)


def join_kernel(own_ref, other_ref, out_ref):
    cols = own_ref.shape[1]
    n = lax.axis_index("narrow")
    out_ref[:, pl.ds(pl.multiple_of(n * cols, cols), cols)] = own_ref[...]
    out_ref[:, pl.ds(pl.multiple_of((1 - n) * cols, cols), cols)] = other_ref[...]


def join_call(own, other):
    return pl.pallas_call(
        join_kernel,
        out_shape=jax.ShapeDtypeStruct((own.shape[0], 2 * own.shape[1]), jnp.float32),
        in_specs=[whole] * 2,
        out_specs=whole,
        compiler_params=params,
        cost_estimate=light,
        name="feature_grad",
    )(own, other)


def make(wide, narrow):
    depth = wide // 4
    sizes = (wide, narrow)
    send = functools.partial(exchange, sizes=sizes)

    def to_t(x):
        return send(x, partner=lambda w, n: (w ^ t_bit(n), n))

    def to_s(x):
        return send(x, partner=lambda w, n: (w ^ s_bit(n), n))

    def to_ts(x):
        return send(x, partner=lambda w, n: (w ^ 3, n))

    def to_z(x, k):
        return send(x, partner=lambda w, n: (w ^ (k << 2), n))

    far_first = sorted(range(1, depth), key=lambda k: (k == 1, k))

    def reach(parts):
        return [to_z(parts[k] if isinstance(parts, dict) else parts, k) for k in far_first]

    def to_core(x, k):
        return send(x, partner=lambda w, n: (w, n ^ k))

    def per_device(features, proxies, sample_ids, positives, loss_weight):
        samples = sample_ids.shape[0]
        rows, width = features.shape
        w = lax.axis_index("wide")
        n = lax.axis_index("narrow")

        if narrow == 2:
            cols = width // 2
            part = jnp.where(n == 0, features[:, :cols], features[:, cols:])
        else:
            part = features
        zs = reach(part)
        near = samples // 4
        picked = [
            proxies.at[ids].get(mode="promise_in_bounds", wrap_negative_indices=False)
            for ids in (sample_ids[:near], sample_ids[near:])
        ]
        *zs, picked[0] = lax.optimization_barrier((*zs, picked[0]))
        group_j = stack_call([part] + zs, [0] + far_first)
        group_t, group_s, picked[1] = lax.optimization_barrier((to_t(group_j), to_s(group_j), picked[1]))
        group_d = to_s(group_t)
        groups = [(group_j,), (group_t,), (group_s,)]
        if narrow == 2:
            others = [to_core(group_j, 1), to_core(group_s, 1), to_core(group_t, 1)]
            groups = [(*group, other) for group, other in zip(groups, others)]

        unit, unit_t = prep_call(picked, 2 if narrow == 2 else 1)
        if narrow != 2:
            unit_t = jnp.take(unit_t.reshape(narrow, width // narrow, samples), n ^ jnp.arange(narrow), axis=0)
            unit_t = unit_t.reshape(width, samples)

        spots = positives.reshape(wide, rows)
        weight = loss_weight.reshape(wide, rows)

        shifted_early, stats_early = logits_call(unit, groups)
        group_d, stats_early = lax.optimization_barrier((group_d, stats_early))
        groups.append((group_d, to_core(group_d, 1)) if narrow == 2 else (group_d,))
        shifted_late, own = logits_call(unit, groups[3:], stats_early)
        stats = own

        def swap_groups(flip, b):
            g, z = divmod(b, depth)
            return ((g % 2) * 2 + g // 2) * depth + z if flip else b

        for bit in range(narrow.bit_length() - 1):
            stats = merge([stats, to_core(stats, 1 << bit)], (0, int(bit == 0)), swap_groups)
        others = reach(stats)
        stats = merge([stats] + others, [0] + far_first, lambda k, b: b ^ k)
        others = [to_t(stats), to_s(stats), to_ts(stats)]
        scale = merge([stats] + others, (0, 1, 2, 3), lambda k, b: b ^ (k * depth), own)

        per = depth * rows // chunk
        order_t, order_s, order_j = range(per, 2 * per), range(2 * per, 3 * per), range(per)
        size = depth * rows
        low = jnp.bfloat16
        grad_d, keep_d, send_d = grad_call(
            unit_t, shifted_late, scale, weight, spots, 3 * per, tuple(range(3 * per, 4 * per)), depth
        )
        grad_r, keep_r, send_r = grad_call(
            unit_t, shifted_early, scale, weight, spots, 0, (*order_t, *order_s), depth
        )

        def within(keep, out, names):
            for bit in range(narrow.bit_length() - 2, 0, -1):
                keep = keep + to_core(out, 1 << bit).astype(jnp.float32)
                half = keep.shape[0] // 2
                keep, out = keep[:half], keep[half:].astype(low)
            return [keep, to_core(out, 1)], [names, names.translate(str.maketrans("TS", "ST"))]

        arrays, places = within(keep_d, send_d, "D")
        arrays[1], send_r = lax.optimization_barrier((arrays[1], send_r))
        sum_d, = add_call(arrays, places, "D", size)
        unit_t, sum_d = lax.optimization_barrier((unit_t, sum_d))
        grad_j, keep_j, send_j = grad_call(
            unit_t, shifted_early, scale, weight, spots, 0, tuple(order_j), depth
        )
        from_d = to_s(sum_d)
        arrays, places = within(keep_r, send_r, "TS")
        arrays_j, places_j = within(keep_j, send_j, "J")
        sum_s, = add_call(arrays, places, "S", size)
        from_s = to_s(sum_s)
        from_d, grad_j, _ = lax.optimization_barrier((from_d, grad_j, sum_s))
        sum_t, = add_call([*arrays, from_d], [*places, "T"], "T", size)
        from_t = to_t(sum_t)
        sum_j, = add_call([*arrays_j, from_s], [*places_j, "J"], "J", size, jnp.float32, heavy)
        mine, *others = own_call([sum_j, from_t], "JJ", depth, size)
        others = reach(dict(enumerate(others, 1)))
        proxy_grad = proxy_call(
            [grad_d, grad_r, grad_j], [groups[3], groups[1], groups[2], groups[0]], picked
        )
        *others, proxy_grad = lax.optimization_barrier((*others, proxy_grad))
        mine = finish_call(mine, others)
        if narrow == 2:
            feature_grad = join_call(mine, to_core(mine, 1))
        else:
            mine = mine[None]
            for bit in range(narrow.bit_length() - 1):
                mine = jnp.concatenate([mine, to_core(mine, 1 << bit)], axis=0)
            feature_grad = jnp.take(mine, n ^ jnp.arange(narrow), axis=0).transpose(1, 0, 2).reshape(rows, width)
        return (feature_grad, proxy_grad)

    return per_device


def solution(mesh):
    placed = (P("wide", None), P(("wide", "narrow"), None), P(("wide", "narrow")), P(), P())
    return jax.shard_map(
        make(mesh.shape["wide"], mesh.shape["narrow"]),
        mesh=mesh,
        in_specs=placed,
        out_specs=(P("wide", None), P(("wide", "narrow"), None)),
        check_vma=False,
    )
```

```python
import functools
import math

import jax
import jax.numpy as jnp
from jax import lax
from jax.experimental import pallas as pl
from jax.experimental.pallas import tpu as pltpu
from jax.sharding import PartitionSpec as P

logit_scale = 3.0
epsilon = 1e-06
exp2_scale = logit_scale * math.log2(math.e)
chunk = 256
both = ("wide", "narrow")
whole = pl.BlockSpec(memory_space=pltpu.VMEM)
params = pltpu.CompilerParams(vmem_limit_bytes=8 * 1024 * 1024)
light = pl.CostEstimate(flops=0, bytes_accessed=1 << 19, transcendentals=0)
heavy = pl.CostEstimate(flops=0, bytes_accessed=10 << 20, transcendentals=0)


def t_bit(n):
    return 1 if n % 2 == 0 else 2


def s_bit(n):
    return 3 - t_bit(n)


def exchange(x, sizes, partner):
    wide, narrow = sizes
    pairs = []
    for w in range(wide):
        for n in range(narrow):
            pw, pn = partner(w, n)
            pairs.append((w * narrow + n, pw * narrow + pn))
    return lax.ppermute(x, both, pairs)


def logits_kernel(group_count, part_count, with_early, unit_ref, *refs):
    parts = refs[: group_count * part_count]
    shifted_ref, stats_ref = refs[-2:]
    per = chunk // 128
    first = 0
    if with_early:
        early_ref = refs[group_count * part_count]
        first = early_ref.shape[0] // 2
        half = stats_ref.shape[0] // 2
        stats_ref[0:first, :] = early_ref[0:first, :]
        stats_ref[half:half + first, :] = early_ref[first:, :]
    half = stats_ref.shape[0] // 2
    step = 0
    for g in range(group_count):
        group = parts[g * part_count:(g + 1) * part_count]
        cols = group[0].shape[1]
        for row in range(0, group[0].shape[0], chunk):
            dots = None
            for k, part in enumerate(group):
                prod = lax.dot_general(
                    unit_ref[:, k * cols:(k + 1) * cols], part[row:row + chunk, :],
                    (((1,), (1,)), ((), ())), preferred_element_type=jnp.float32,
                )
                dots = prod if dots is None else dots + prod
            top = jnp.max(dots, axis=0, keepdims=True)
            shifted = jnp.exp2((dots - top) * exp2_scale)
            total = jnp.sum(shifted, axis=0, keepdims=True)
            shifted_ref[:, step * chunk:(step + 1) * chunk] = shifted
            for b in range(per):
                at = first + step * per + b
                stats_ref[at:at + 1, :] = top[:, b * 128:(b + 1) * 128]
                stats_ref[half + at:half + at + 1, :] = total[:, b * 128:(b + 1) * 128]
            step += 1


def logits_call(unit, groups, early=None):
    rows = groups[0][0].shape[0]
    count = len(groups) * rows
    samples = unit.shape[0]
    flat = [part for group in groups for part in group]
    lines = 2 * count // 128
    if early is not None:
        lines += early.shape[0]
        flat.append(early)
    return pl.pallas_call(
        functools.partial(logits_kernel, len(groups), len(groups[0]), early is not None),
        out_shape=(
            jax.ShapeDtypeStruct((samples, count), jnp.float32),
            jax.ShapeDtypeStruct((lines, 128), jnp.float32),
        ),
        in_specs=[whole] * (1 + len(flat)),
        out_specs=(whole, whole),
        compiler_params=params,
        cost_estimate=pl.CostEstimate(
            flops=2 * samples * count * unit.shape[1],
            bytes_accessed=4 * samples * count,
            transcendentals=samples * count,
        ),
        name="logits",
    )(unit, *flat)


def grad_kernel(first, steps, depth, unit_t_ref, shifted_ref, scale_ref, weight_ref, at_ref, grad_ref, keep_ref, send_ref):
    samples = shifted_ref.shape[0]
    half = unit_t_ref.shape[0] // 2
    per = chunk // 128
    w, n = lax.axis_index("wide"), lax.axis_index("narrow")
    base = (w * lax.axis_size("narrow") + n) * samples
    cand = lax.broadcasted_iota(jnp.int32, (samples, chunk), 0) + base

    def row(ref, at):
        return jnp.concatenate([ref[at + b:at + b + 1, :] for b in range(per)], axis=1)

    def far_row(ref, at):
        lines = []
        for b in range(at, at + per):
            g, z = divmod(b, depth)
            offset = jnp.where(n % 2 == 0, 4 * z + g, 4 * z + (g % 2) * 2 + g // 2)
            lines.append(ref[pl.ds(jnp.bitwise_xor(w, offset), 1), :])
        return jnp.concatenate(lines, axis=1)

    for out, at in enumerate(steps):
        cols = slice((at - first) * chunk, (at - first + 1) * chunk)
        scale, weight, spot = row(scale_ref, at * per), far_row(weight_ref, at * per), far_row(at_ref, at * per)
        soft = shifted_ref[:, cols] * scale
        grad = (weight * jnp.where(cand == spot, soft - 1.0, soft)).astype(jnp.bfloat16)
        out_cols = slice(out * chunk, (out + 1) * chunk)
        grad_ref[:, out_cols] = grad
        shares = logit_scale * jnp.dot(unit_t_ref[...], grad, preferred_element_type=jnp.float32)
        keep_ref[:, out_cols] = shares[:half]
        send_ref[:, out_cols] = shares[half:].astype(jnp.bfloat16)


def grad_call(unit_t, shifted, scale, weight, spots, first, steps, depth):
    samples = shifted.shape[0]
    width = unit_t.shape[0]
    count = len(steps) * chunk
    return pl.pallas_call(
        functools.partial(grad_kernel, first, steps, depth),
        out_shape=(
            jax.ShapeDtypeStruct((samples, count), jnp.bfloat16),
            jax.ShapeDtypeStruct((width // 2, count), jnp.float32),
            jax.ShapeDtypeStruct((width // 2, count), jnp.bfloat16),
        ),
        in_specs=[whole] * 5,
        out_specs=(whole,) * 3,
        compiler_params=params,
        cost_estimate=pl.CostEstimate(
            flops=2 * samples * count * width, bytes_accessed=6 * samples * count, transcendentals=0
        ),
        name="grads",
    )(unit_t, shifted, scale, weight, spots)


def proxy_kernel(grad_count, group_count, part_count, rows, *refs):
    grad_refs, refs = refs[:grad_count], refs[grad_count:]
    parts = refs[:group_count * part_count]
    *picked_refs, out_ref = refs[group_count * part_count:]
    size, cols = parts[0].shape
    grads = [ref.at[:, at:at + size] for ref in grad_refs for at in range(0, ref.shape[1], size)]
    n = lax.axis_index("narrow")
    places = []
    for k in range(part_count):
        if part_count == 1:
            places.append(slice(0, cols))
        else:
            places.append(pl.ds(pl.multiple_of((n ^ k) * cols, cols), cols))
    tiles = [(ref, row) for ref in picked_refs for row in range(0, ref.shape[0], rows)]
    for tile, (picked_ref, row) in enumerate(tiles):
        at, here = slice(tile * rows, (tile + 1) * rows), slice(row, row + rows)
        sums = []
        for k in range(part_count):
            total = None
            for g in range(group_count):
                prod = jnp.dot(
                    grads[g][at, :], parts[g * part_count + k][...], preferred_element_type=jnp.float32
                )
                total = prod if total is None else total + prod
            sums.append(logit_scale * total)
        picked = [picked_ref[here, place] for place in places]
        square = functools.reduce(jnp.add, [jnp.sum(p * p, axis=1, keepdims=True) for p in picked])
        inverse = 1.0 / jnp.sqrt(square + epsilon)
        inner = functools.reduce(jnp.add, [jnp.sum(p * s, axis=1, keepdims=True) for p, s in zip(picked, sums)])
        slope = inner * inverse * inverse
        for place, p, s in zip(places, picked, sums):
            out_ref[at, place] = (s - p * slope) * inverse


def proxy_call(grads, groups, picked):
    samples, width = grads[0].shape[0], picked[0].shape[1]
    count = sum(grad.shape[1] for grad in grads)
    flat = [part for group in groups for part in group]
    return pl.pallas_call(
        functools.partial(proxy_kernel, len(grads), len(groups), len(groups[0]), 256),
        out_shape=jax.ShapeDtypeStruct((samples, width), jnp.float32),
        in_specs=[whole] * (len(grads) + len(flat) + len(picked)),
        out_specs=whole,
        compiler_params=params,
        cost_estimate=pl.CostEstimate(
            flops=2 * samples * count * width, bytes_accessed=4 * samples * count, transcendentals=0
        ),
        name="proxy_grads",
    )(*grads, *flat, *picked)


def merge_kernel(flips, swap, with_scale, *refs):
    ins, out_ref = refs[:-1], refs[-1]
    if with_scale:
        own_ref, ins = ins[-1], ins[:-1]
    blocks = ins[0].shape[0] // 2
    for b in range(blocks):
        spots = [swap(f, b) for f in flips]
        tops = [ref[at:at + 1, :] for ref, at in zip(ins, spots)]
        totals = [ref[blocks + at:blocks + at + 1, :] for ref, at in zip(ins, spots)]
        top = functools.reduce(jnp.maximum, tops)
        total = functools.reduce(
            jnp.add, [t * jnp.exp2((m - top) * exp2_scale) for m, t in zip(tops, totals)]
        )
        if with_scale:
            out_ref[b:b + 1, :] = jnp.exp2((own_ref[b:b + 1, :] - top) * exp2_scale) / total
        else:
            out_ref[b:b + 1, :] = top
            out_ref[blocks + b:blocks + b + 1, :] = total


def merge(stats, flips, swap, own=None):
    lines = stats[0].shape[0]
    if own is not None:
        stats, lines = [*stats, own], lines // 2
    return pl.pallas_call(
        functools.partial(merge_kernel, flips, swap, own is not None),
        out_shape=jax.ShapeDtypeStruct((lines, 128), jnp.float32),
        in_specs=[whole] * len(stats),
        out_specs=whole,
        compiler_params=params,
        cost_estimate=light,
        name="merge_stats",
    )(*stats)


def stack_kernel(places, *refs):
    rows = refs[0].shape[0]
    for k, ref in zip(places, refs):
        refs[-1][k * rows:(k + 1) * rows, :] = ref[...]


def stack_call(parts, places):
    rows, cols = parts[0].shape
    return pl.pallas_call(
        functools.partial(stack_kernel, places),
        out_shape=jax.ShapeDtypeStruct((len(parts) * rows, cols), parts[0].dtype),
        in_specs=[whole] * len(parts),
        out_specs=whole,
        compiler_params=params,
        cost_estimate=light,
        name="stack_blocks",
    )(*parts)


def add_kernel(ins, outs, size, *refs):
    for name, out_ref in zip(outs, refs[len(ins):]):
        total = None
        for places, ref in zip(ins, refs):
            if name in places:
                at = places.index(name)
                term = ref[:, at * size:(at + 1) * size].astype(jnp.float32)
                total = term if total is None else total + term
        out_ref[...] = total.astype(out_ref.dtype)


def add_call(arrays, ins, outs, size, dtype=jnp.bfloat16, cost=light):
    rows = arrays[0].shape[0]
    result = pl.pallas_call(
        functools.partial(add_kernel, ins, outs, size),
        out_shape=[jax.ShapeDtypeStruct((rows, size), dtype) for _ in outs],
        in_specs=[whole] * len(arrays),
        out_specs=[whole] * len(outs),
        compiler_params=params,
        cost_estimate=cost,
        name="add_shares",
    )(*arrays)
    return result


def own_kernel(ins, count, size, *refs):
    cols = size // count
    for k, out_ref in enumerate(refs[len(ins):]):
        total = None
        for places, ref in zip(ins, refs):
            at = places.index("J") * size + k * cols
            term = ref[:, at:at + cols].astype(jnp.float32)
            total = term if total is None else total + term
        out_ref[...] = total.astype(out_ref.dtype)


def own_call(arrays, ins, count, size):
    rows = arrays[0].shape[0]
    return pl.pallas_call(
        functools.partial(own_kernel, ins, count, size),
        out_shape=[
            jax.ShapeDtypeStruct((rows, size // count), jnp.bfloat16 if k else jnp.float32) for k in range(count)
        ],
        in_specs=[whole] * len(arrays),
        out_specs=[whole] * count,
        compiler_params=params,
        cost_estimate=light,
        name="add_shares_z",
    )(*arrays)


def prep_kernel(part_count, *refs):
    *picked_refs, unit_ref, unit_t_ref = refs
    width = picked_refs[0].shape[1]
    cols = width // part_count
    tiles = [(ref, row) for ref in picked_refs for row in range(0, ref.shape[0], 256)]
    n = lax.axis_index("narrow")
    for line, (picked_ref, row) in enumerate(tiles):
        line *= 256
        at = slice(row, row + 256)
        if part_count == 1:
            picked = picked_ref[at, :]
        else:
            picked = jnp.concatenate(
                [picked_ref[at, pl.ds(pl.multiple_of((n ^ k) * cols, cols), cols)] for k in range(part_count)],
                axis=1,
            )
        lengths = jnp.sqrt(jnp.sum(picked * picked, axis=1, keepdims=True) + epsilon)
        unit = picked / lengths
        unit_ref[line:line + 256, :] = unit.astype(jnp.bfloat16)
        unit_t_ref[:, line:line + 256] = unit.T.astype(jnp.bfloat16)


def prep_call(picked, part_count):
    samples, width = sum(p.shape[0] for p in picked), picked[0].shape[1]
    return pl.pallas_call(
        functools.partial(prep_kernel, part_count),
        out_shape=(
            jax.ShapeDtypeStruct((samples, width), jnp.bfloat16),
            jax.ShapeDtypeStruct((width, samples), jnp.bfloat16),
        ),
        in_specs=[whole] * len(picked),
        out_specs=(whole, whole),
        compiler_params=params,
        cost_estimate=pl.CostEstimate(flops=4 * samples * width, bytes_accessed=8 * samples * width, transcendentals=0),
        name="unit_rows",
    )(*picked)


def finish_kernel(*refs):
    ins, out_ref = refs[:-1], refs[-1]
    total = functools.reduce(jnp.add, [ref[...].astype(jnp.float32) for ref in ins])
    out_ref[...] = total.T


def finish_call(own, others):
    return pl.pallas_call(
        finish_kernel,
        out_shape=jax.ShapeDtypeStruct((own.shape[1], own.shape[0]), jnp.float32),
        in_specs=[whole] * (1 + len(others)),
        out_specs=whole,
        compiler_params=params,
        cost_estimate=light,
        name="feature_sums",
    )(own, *others)


def join_kernel(own_ref, other_ref, out_ref):
    cols = own_ref.shape[1]
    n = lax.axis_index("narrow")
    out_ref[:, pl.ds(pl.multiple_of(n * cols, cols), cols)] = own_ref[...]
    out_ref[:, pl.ds(pl.multiple_of((1 - n) * cols, cols), cols)] = other_ref[...]


def join_call(own, other):
    return pl.pallas_call(
        join_kernel,
        out_shape=jax.ShapeDtypeStruct((own.shape[0], 2 * own.shape[1]), jnp.float32),
        in_specs=[whole] * 2,
        out_specs=whole,
        compiler_params=params,
        cost_estimate=light,
        name="feature_grad",
    )(own, other)


def make(wide, narrow):
    depth = wide // 4
    sizes = (wide, narrow)
    send = functools.partial(exchange, sizes=sizes)

    def to_t(x):
        return send(x, partner=lambda w, n: (w ^ t_bit(n), n))

    def to_s(x):
        return send(x, partner=lambda w, n: (w ^ s_bit(n), n))

    def to_ts(x):
        return send(x, partner=lambda w, n: (w ^ 3, n))

    def to_z(x, k):
        return send(x, partner=lambda w, n: (w ^ (k << 2), n))

    far_first = sorted(range(1, depth), key=lambda k: (k == 1, k))

    def reach(parts, order=far_first):
        return [to_z(parts[k] if isinstance(parts, dict) else parts, k) for k in order]

    def to_core(x, k):
        return send(x, partner=lambda w, n: (w, n ^ k))

    def per_device(features, proxies, sample_ids, positives, loss_weight):
        samples = sample_ids.shape[0]
        rows, width = features.shape
        w = lax.axis_index("wide")
        n = lax.axis_index("narrow")

        if narrow == 2:
            cols = width // 2
            part = jnp.where(n == 0, features[:, :cols], features[:, cols:])
        else:
            part = features
        zs = reach(part, far_first[::-1])
        near = samples // 4
        picked = [
            proxies.at[ids].get(mode="promise_in_bounds", wrap_negative_indices=False)
            for ids in (sample_ids[:near], sample_ids[near:])
        ]
        *zs, picked[0] = lax.optimization_barrier((*zs, picked[0]))
        group_j = stack_call([part] + zs, [0] + far_first[::-1])
        group_s, group_t, picked[1] = lax.optimization_barrier((to_s(group_j), to_t(group_j), picked[1]))
        group_d = to_s(group_t)
        groups = [(group_j,), (group_t,), (group_s,)]
        if narrow == 2:
            others = [to_core(group_j, 1), to_core(group_s, 1), to_core(group_t, 1)]
            groups = [(*group, other) for group, other in zip(groups, others)]

        unit, unit_t = prep_call(picked, 2 if narrow == 2 else 1)
        if narrow != 2:
            unit_t = jnp.take(unit_t.reshape(narrow, width // narrow, samples), n ^ jnp.arange(narrow), axis=0)
            unit_t = unit_t.reshape(width, samples)

        spots = positives.reshape(wide, rows)
        weight = loss_weight.reshape(wide, rows)

        shifted_early, stats_early = logits_call(unit, groups)
        group_d, stats_early = lax.optimization_barrier((group_d, stats_early))
        groups.append((group_d, to_core(group_d, 1)) if narrow == 2 else (group_d,))
        shifted_late, own = logits_call(unit, groups[3:], stats_early)
        stats = own

        def swap_groups(flip, b):
            g, z = divmod(b, depth)
            return ((g % 2) * 2 + g // 2) * depth + z if flip else b

        for bit in range(narrow.bit_length() - 1):
            stats = merge([stats, to_core(stats, 1 << bit)], (0, int(bit == 0)), swap_groups)
        others = reach(stats)
        stats = merge([stats] + others, [0] + far_first, lambda k, b: b ^ k)
        others = [to_t(stats), to_s(stats), to_ts(stats)]
        scale = merge([stats] + others, (0, 1, 2, 3), lambda k, b: b ^ (k * depth), own)

        per = depth * rows // chunk
        order_t, order_s, order_j = range(per, 2 * per), range(2 * per, 3 * per), range(per)
        size = depth * rows
        low = jnp.bfloat16
        grad_d, keep_d, send_d = grad_call(
            unit_t, shifted_late, scale, weight, spots, 3 * per, tuple(range(3 * per, 4 * per)), depth
        )
        grad_r, keep_r, send_r = grad_call(
            unit_t, shifted_early, scale, weight, spots, 0, (*order_t, *order_s), depth
        )

        def within(keep, out, names):
            for bit in range(narrow.bit_length() - 2, 0, -1):
                keep = keep + to_core(out, 1 << bit).astype(jnp.float32)
                half = keep.shape[0] // 2
                keep, out = keep[:half], keep[half:].astype(low)
            return [keep, to_core(out, 1)], [names, names.translate(str.maketrans("TS", "ST"))]

        arrays, places = within(keep_d, send_d, "D")
        arrays[1], send_r = lax.optimization_barrier((arrays[1], send_r))
        sum_d, = add_call(arrays, places, "D", size)
        unit_t, sum_d = lax.optimization_barrier((unit_t, sum_d))
        grad_j, keep_j, send_j = grad_call(
            unit_t, shifted_early, scale, weight, spots, 0, tuple(order_j), depth
        )
        from_d = to_s(sum_d)
        arrays, places = within(keep_r, send_r, "TS")
        arrays_j, places_j = within(keep_j, send_j, "J")
        sum_s, = add_call(arrays, places, "S", size)
        from_s = to_s(sum_s)
        from_d, grad_j, _ = lax.optimization_barrier((from_d, grad_j, sum_s))
        sum_t, = add_call([*arrays, from_d], [*places, "T"], "T", size)
        from_t = to_t(sum_t)
        sum_j, = add_call([*arrays_j, from_s], [*places_j, "J"], "J", size, jnp.float32, heavy)
        mine, *others = own_call([sum_j, from_t], "JJ", depth, size)
        others = reach(dict(enumerate(others, 1)))
        proxy_grad = proxy_call(
            [grad_d, grad_r, grad_j], [groups[3], groups[1], groups[2], groups[0]], picked
        )
        *others, proxy_grad = lax.optimization_barrier((*others, proxy_grad))
        mine = finish_call(mine, others)
        if narrow == 2:
            feature_grad = join_call(mine, to_core(mine, 1))
        else:
            mine = mine[None]
            for bit in range(narrow.bit_length() - 1):
                mine = jnp.concatenate([mine, to_core(mine, 1 << bit)], axis=0)
            feature_grad = jnp.take(mine, n ^ jnp.arange(narrow), axis=0).transpose(1, 0, 2).reshape(rows, width)
        return (feature_grad, proxy_grad)

    return per_device


def solution(mesh):
    placed = (P("wide", None), P(("wide", "narrow"), None), P(("wide", "narrow")), P(), P())
    return jax.shard_map(
        make(mesh.shape["wide"], mesh.shape["narrow"]),
        mesh=mesh,
        in_specs=placed,
        out_specs=(P("wide", None), P(("wide", "narrow"), None)),
        check_vma=False,
    )
```

```python
import functools
import math

import jax
import jax.numpy as jnp
from jax import lax
from jax.experimental import pallas as pl
from jax.experimental.pallas import tpu as pltpu
from jax.sharding import PartitionSpec as P

logit_scale = 3.0
epsilon = 1e-06
exp2_scale = logit_scale * math.log2(math.e)
chunk = 256
both = ("wide", "narrow")
whole = pl.BlockSpec(memory_space=pltpu.VMEM)
params = pltpu.CompilerParams(vmem_limit_bytes=8 * 1024 * 1024)
light = pl.CostEstimate(flops=0, bytes_accessed=1 << 19, transcendentals=0)
heavy = pl.CostEstimate(flops=0, bytes_accessed=10 << 20, transcendentals=0)


def t_bit(n):
    return 1 if n % 2 == 0 else 2


def s_bit(n):
    return 3 - t_bit(n)


def exchange(x, sizes, partner):
    wide, narrow = sizes
    pairs = []
    for w in range(wide):
        for n in range(narrow):
            pw, pn = partner(w, n)
            pairs.append((w * narrow + n, pw * narrow + pn))
    return lax.ppermute(x, both, pairs)


def logits_kernel(group_count, part_count, with_early, unit_ref, *refs):
    parts = refs[: group_count * part_count]
    shifted_ref, stats_ref = refs[-2:]
    per = chunk // 128
    first = 0
    if with_early:
        early_ref = refs[group_count * part_count]
        first = early_ref.shape[0] // 2
        half = stats_ref.shape[0] // 2
        stats_ref[0:first, :] = early_ref[0:first, :]
        stats_ref[half:half + first, :] = early_ref[first:, :]
    half = stats_ref.shape[0] // 2
    step = 0
    for g in range(group_count):
        group = parts[g * part_count:(g + 1) * part_count]
        cols = group[0].shape[1]
        for row in range(0, group[0].shape[0], chunk):
            dots = None
            for k, part in enumerate(group):
                prod = lax.dot_general(
                    unit_ref[:, k * cols:(k + 1) * cols], part[row:row + chunk, :],
                    (((1,), (1,)), ((), ())), preferred_element_type=jnp.float32,
                )
                dots = prod if dots is None else dots + prod
            top = jnp.max(dots, axis=0, keepdims=True)
            shifted = jnp.exp2((dots - top) * exp2_scale)
            total = jnp.sum(shifted, axis=0, keepdims=True)
            shifted_ref[:, step * chunk:(step + 1) * chunk] = shifted
            for b in range(per):
                at = first + step * per + b
                stats_ref[at:at + 1, :] = top[:, b * 128:(b + 1) * 128]
                stats_ref[half + at:half + at + 1, :] = total[:, b * 128:(b + 1) * 128]
            step += 1


def logits_call(unit, groups, early=None):
    rows = groups[0][0].shape[0]
    count = len(groups) * rows
    samples = unit.shape[0]
    flat = [part for group in groups for part in group]
    lines = 2 * count // 128
    if early is not None:
        lines += early.shape[0]
        flat.append(early)
    return pl.pallas_call(
        functools.partial(logits_kernel, len(groups), len(groups[0]), early is not None),
        out_shape=(
            jax.ShapeDtypeStruct((samples, count), jnp.float32),
            jax.ShapeDtypeStruct((lines, 128), jnp.float32),
        ),
        in_specs=[whole] * (1 + len(flat)),
        out_specs=(whole, whole),
        compiler_params=params,
        cost_estimate=pl.CostEstimate(
            flops=2 * samples * count * unit.shape[1],
            bytes_accessed=4 * samples * count,
            transcendentals=samples * count,
        ),
        name="logits",
    )(unit, *flat)


def grad_kernel(first, steps, depth, unit_t_ref, shifted_ref, scale_ref, weight_ref, at_ref, grad_ref, keep_ref, send_ref):
    samples = shifted_ref.shape[0]
    half = unit_t_ref.shape[0] // 2
    per = chunk // 128
    w, n = lax.axis_index("wide"), lax.axis_index("narrow")
    base = (w * lax.axis_size("narrow") + n) * samples
    cand = lax.broadcasted_iota(jnp.int32, (samples, chunk), 0) + base

    def row(ref, at):
        return jnp.concatenate([ref[at + b:at + b + 1, :] for b in range(per)], axis=1)

    def far_row(ref, at):
        lines = []
        for b in range(at, at + per):
            g, z = divmod(b, depth)
            offset = jnp.where(n % 2 == 0, 4 * z + g, 4 * z + (g % 2) * 2 + g // 2)
            lines.append(ref[pl.ds(jnp.bitwise_xor(w, offset), 1), :])
        return jnp.concatenate(lines, axis=1)

    for out, at in enumerate(steps):
        cols = slice((at - first) * chunk, (at - first + 1) * chunk)
        scale, weight, spot = row(scale_ref, at * per), far_row(weight_ref, at * per), far_row(at_ref, at * per)
        soft = shifted_ref[:, cols] * scale
        grad = (weight * jnp.where(cand == spot, soft - 1.0, soft)).astype(jnp.bfloat16)
        out_cols = slice(out * chunk, (out + 1) * chunk)
        grad_ref[:, out_cols] = grad
        shares = logit_scale * jnp.dot(unit_t_ref[...], grad, preferred_element_type=jnp.float32)
        keep_ref[:, out_cols] = shares[:half]
        send_ref[:, out_cols] = shares[half:].astype(jnp.bfloat16)


def grad_call(unit_t, shifted, scale, weight, spots, first, steps, depth):
    samples = shifted.shape[0]
    width = unit_t.shape[0]
    count = len(steps) * chunk
    return pl.pallas_call(
        functools.partial(grad_kernel, first, steps, depth),
        out_shape=(
            jax.ShapeDtypeStruct((samples, count), jnp.bfloat16),
            jax.ShapeDtypeStruct((width // 2, count), jnp.float32),
            jax.ShapeDtypeStruct((width // 2, count), jnp.bfloat16),
        ),
        in_specs=[whole] * 5,
        out_specs=(whole,) * 3,
        compiler_params=params,
        cost_estimate=pl.CostEstimate(
            flops=2 * samples * count * width, bytes_accessed=6 * samples * count, transcendentals=0
        ),
        name="grads",
    )(unit_t, shifted, scale, weight, spots)


def proxy_kernel(grad_count, group_count, part_count, rows, *refs):
    grad_refs, refs = refs[:grad_count], refs[grad_count:]
    parts = refs[:group_count * part_count]
    *picked_refs, out_ref = refs[group_count * part_count:]
    size, cols = parts[0].shape
    grads = [ref.at[:, at:at + size] for ref in grad_refs for at in range(0, ref.shape[1], size)]
    n = lax.axis_index("narrow")
    places = []
    for k in range(part_count):
        if part_count == 1:
            places.append(slice(0, cols))
        else:
            places.append(pl.ds(pl.multiple_of((n ^ k) * cols, cols), cols))
    tiles = [(ref, row) for ref in picked_refs for row in range(0, ref.shape[0], rows)]
    for tile, (picked_ref, row) in enumerate(tiles):
        at, here = slice(tile * rows, (tile + 1) * rows), slice(row, row + rows)
        sums = []
        for k in range(part_count):
            total = None
            for g in range(group_count):
                prod = jnp.dot(
                    grads[g][at, :], parts[g * part_count + k][...], preferred_element_type=jnp.float32
                )
                total = prod if total is None else total + prod
            sums.append(logit_scale * total)
        picked = [picked_ref[here, place] for place in places]
        square = functools.reduce(jnp.add, [jnp.sum(p * p, axis=1, keepdims=True) for p in picked])
        inverse = 1.0 / jnp.sqrt(square + epsilon)
        inner = functools.reduce(jnp.add, [jnp.sum(p * s, axis=1, keepdims=True) for p, s in zip(picked, sums)])
        slope = inner * inverse * inverse
        for place, p, s in zip(places, picked, sums):
            out_ref[at, place] = (s - p * slope) * inverse


def proxy_call(grads, groups, picked):
    samples, width = grads[0].shape[0], picked[0].shape[1]
    count = sum(grad.shape[1] for grad in grads)
    flat = [part for group in groups for part in group]
    return pl.pallas_call(
        functools.partial(proxy_kernel, len(grads), len(groups), len(groups[0]), 256),
        out_shape=jax.ShapeDtypeStruct((samples, width), jnp.float32),
        in_specs=[whole] * (len(grads) + len(flat) + len(picked)),
        out_specs=whole,
        compiler_params=params,
        cost_estimate=pl.CostEstimate(
            flops=2 * samples * count * width, bytes_accessed=4 * samples * count, transcendentals=0
        ),
        name="proxy_grads",
    )(*grads, *flat, *picked)


def merge_kernel(flips, swap, with_scale, *refs):
    ins, out_ref = refs[:-1], refs[-1]
    if with_scale:
        own_ref, ins = ins[-1], ins[:-1]
    blocks = ins[0].shape[0] // 2
    for b in range(blocks):
        spots = [swap(f, b) for f in flips]
        tops = [ref[at:at + 1, :] for ref, at in zip(ins, spots)]
        totals = [ref[blocks + at:blocks + at + 1, :] for ref, at in zip(ins, spots)]
        top = functools.reduce(jnp.maximum, tops)
        total = functools.reduce(
            jnp.add, [t * jnp.exp2((m - top) * exp2_scale) for m, t in zip(tops, totals)]
        )
        if with_scale:
            out_ref[b:b + 1, :] = jnp.exp2((own_ref[b:b + 1, :] - top) * exp2_scale) / total
        else:
            out_ref[b:b + 1, :] = top
            out_ref[blocks + b:blocks + b + 1, :] = total


def merge(stats, flips, swap, own=None):
    lines = stats[0].shape[0]
    if own is not None:
        stats, lines = [*stats, own], lines // 2
    return pl.pallas_call(
        functools.partial(merge_kernel, flips, swap, own is not None),
        out_shape=jax.ShapeDtypeStruct((lines, 128), jnp.float32),
        in_specs=[whole] * len(stats),
        out_specs=whole,
        compiler_params=params,
        cost_estimate=light,
        name="merge_stats",
    )(*stats)


def stack_kernel(places, *refs):
    rows = refs[0].shape[0]
    for k, ref in zip(places, refs):
        refs[-1][k * rows:(k + 1) * rows, :] = ref[...]


def stack_call(parts, places):
    rows, cols = parts[0].shape
    return pl.pallas_call(
        functools.partial(stack_kernel, places),
        out_shape=jax.ShapeDtypeStruct((len(parts) * rows, cols), parts[0].dtype),
        in_specs=[whole] * len(parts),
        out_specs=whole,
        compiler_params=params,
        cost_estimate=light,
        name="stack_blocks",
    )(*parts)


def add_kernel(ins, outs, size, *refs):
    for name, out_ref in zip(outs, refs[len(ins):]):
        total = None
        for places, ref in zip(ins, refs):
            if name in places:
                at = places.index(name)
                term = ref[:, at * size:(at + 1) * size].astype(jnp.float32)
                total = term if total is None else total + term
        out_ref[...] = total.astype(out_ref.dtype)


def add_call(arrays, ins, outs, size, dtype=jnp.bfloat16, cost=light):
    rows = arrays[0].shape[0]
    result = pl.pallas_call(
        functools.partial(add_kernel, ins, outs, size),
        out_shape=[jax.ShapeDtypeStruct((rows, size), dtype) for _ in outs],
        in_specs=[whole] * len(arrays),
        out_specs=[whole] * len(outs),
        compiler_params=params,
        cost_estimate=cost,
        name="add_shares",
    )(*arrays)
    return result


def own_kernel(ins, count, size, *refs):
    cols = size // count
    for k, out_ref in enumerate(refs[len(ins):]):
        total = None
        for places, ref in zip(ins, refs):
            at = places.index("J") * size + k * cols
            term = ref[:, at:at + cols].astype(jnp.float32)
            total = term if total is None else total + term
        out_ref[...] = total.astype(out_ref.dtype)


def own_call(arrays, ins, count, size):
    rows = arrays[0].shape[0]
    return pl.pallas_call(
        functools.partial(own_kernel, ins, count, size),
        out_shape=[
            jax.ShapeDtypeStruct((rows, size // count), jnp.bfloat16 if k else jnp.float32) for k in range(count)
        ],
        in_specs=[whole] * len(arrays),
        out_specs=[whole] * count,
        compiler_params=params,
        cost_estimate=light,
        name="add_shares_z",
    )(*arrays)


def prep_kernel(part_count, *refs):
    *picked_refs, unit_ref, unit_t_ref = refs
    width = picked_refs[0].shape[1]
    cols = width // part_count
    tiles = [(ref, row) for ref in picked_refs for row in range(0, ref.shape[0], 256)]
    n = lax.axis_index("narrow")
    for line, (picked_ref, row) in enumerate(tiles):
        line *= 256
        at = slice(row, row + 256)
        if part_count == 1:
            picked = picked_ref[at, :]
        else:
            picked = jnp.concatenate(
                [picked_ref[at, pl.ds(pl.multiple_of((n ^ k) * cols, cols), cols)] for k in range(part_count)],
                axis=1,
            )
        lengths = jnp.sqrt(jnp.sum(picked * picked, axis=1, keepdims=True) + epsilon)
        unit = picked / lengths
        unit_ref[line:line + 256, :] = unit.astype(jnp.bfloat16)
        unit_t_ref[:, line:line + 256] = unit.T.astype(jnp.bfloat16)


def prep_call(picked, part_count):
    samples, width = sum(p.shape[0] for p in picked), picked[0].shape[1]
    return pl.pallas_call(
        functools.partial(prep_kernel, part_count),
        out_shape=(
            jax.ShapeDtypeStruct((samples, width), jnp.bfloat16),
            jax.ShapeDtypeStruct((width, samples), jnp.bfloat16),
        ),
        in_specs=[whole] * len(picked),
        out_specs=(whole, whole),
        compiler_params=params,
        cost_estimate=pl.CostEstimate(flops=4 * samples * width, bytes_accessed=8 * samples * width, transcendentals=0),
        name="unit_rows",
    )(*picked)


def finish_kernel(*refs):
    ins, out_ref = refs[:-1], refs[-1]
    total = functools.reduce(jnp.add, [ref[...].astype(jnp.float32) for ref in ins])
    out_ref[...] = total.T


def finish_call(own, others):
    return pl.pallas_call(
        finish_kernel,
        out_shape=jax.ShapeDtypeStruct((own.shape[1], own.shape[0]), jnp.float32),
        in_specs=[whole] * (1 + len(others)),
        out_specs=whole,
        compiler_params=params,
        cost_estimate=light,
        name="feature_sums",
    )(own, *others)


def join_kernel(own_ref, other_ref, out_ref):
    cols = own_ref.shape[1]
    n = lax.axis_index("narrow")
    out_ref[:, pl.ds(pl.multiple_of(n * cols, cols), cols)] = own_ref[...]
    out_ref[:, pl.ds(pl.multiple_of((1 - n) * cols, cols), cols)] = other_ref[...]


def join_call(own, other):
    return pl.pallas_call(
        join_kernel,
        out_shape=jax.ShapeDtypeStruct((own.shape[0], 2 * own.shape[1]), jnp.float32),
        in_specs=[whole] * 2,
        out_specs=whole,
        compiler_params=params,
        cost_estimate=light,
        name="feature_grad",
    )(own, other)


def make(wide, narrow):
    depth = wide // 4
    sizes = (wide, narrow)
    send = functools.partial(exchange, sizes=sizes)

    def to_t(x):
        return send(x, partner=lambda w, n: (w ^ t_bit(n), n))

    def to_s(x):
        return send(x, partner=lambda w, n: (w ^ s_bit(n), n))

    def to_ts(x):
        return send(x, partner=lambda w, n: (w ^ 3, n))

    def to_z(x, k):
        return send(x, partner=lambda w, n: (w ^ (k << 2), n))

    far_first = sorted(range(1, depth), key=lambda k: (k == 1, k))

    def reach(parts, order=far_first):
        return [to_z(parts[k] if isinstance(parts, dict) else parts, k) for k in order]

    def to_core(x, k):
        return send(x, partner=lambda w, n: (w, n ^ k))

    def per_device(features, proxies, sample_ids, positives, loss_weight):
        samples = sample_ids.shape[0]
        rows, width = features.shape
        w = lax.axis_index("wide")
        n = lax.axis_index("narrow")

        if narrow == 2:
            cols = width // 2
            part = jnp.where(n == 0, features[:, :cols], features[:, cols:])
        else:
            part = features
        zs = reach(part, far_first[::-1])
        near = samples // 4
        picked = [
            proxies.at[ids].get(mode="promise_in_bounds", wrap_negative_indices=False)
            for ids in (sample_ids[:near], sample_ids[near:])
        ]
        *zs, picked[0] = lax.optimization_barrier((*zs, picked[0]))
        group_j = stack_call([part] + zs, [0] + far_first[::-1])
        group_s, group_t, picked[1] = lax.optimization_barrier((to_s(group_j), to_t(group_j), picked[1]))
        group_d = to_s(group_t)
        groups = [(group_j,), (group_t,), (group_s,)]
        if narrow == 2:
            others = [to_core(group_j, 1), to_core(group_s, 1), to_core(group_t, 1)]
            groups = [(*group, other) for group, other in zip(groups, others)]

        unit, unit_t = prep_call(picked, 2 if narrow == 2 else 1)
        if narrow != 2:
            unit_t = jnp.take(unit_t.reshape(narrow, width // narrow, samples), n ^ jnp.arange(narrow), axis=0)
            unit_t = unit_t.reshape(width, samples)

        spots = positives.reshape(wide, rows)
        weight = loss_weight.reshape(wide, rows)

        shifted_early, stats_early = logits_call(unit, groups)
        group_d, stats_early = lax.optimization_barrier((group_d, stats_early))
        groups.append((group_d, to_core(group_d, 1)) if narrow == 2 else (group_d,))
        shifted_late, own = logits_call(unit, groups[3:], stats_early)
        stats = own

        def swap_groups(flip, b):
            g, z = divmod(b, depth)
            return ((g % 2) * 2 + g // 2) * depth + z if flip else b

        for bit in range(narrow.bit_length() - 1):
            stats = merge([stats, to_core(stats, 1 << bit)], (0, int(bit == 0)), swap_groups)
        others = reach(stats)
        stats = merge([stats] + others, [0] + far_first, lambda k, b: b ^ k)
        others = [to_t(stats), to_s(stats), to_ts(stats)]
        scale = merge([stats] + others, (0, 1, 2, 3), lambda k, b: b ^ (k * depth), own)

        per = depth * rows // chunk
        order_t, order_s, order_j = range(per, 2 * per), range(2 * per, 3 * per), range(per)
        size = depth * rows
        low = jnp.bfloat16
        grad_d, keep_d, send_d = grad_call(
            unit_t, shifted_late, scale, weight, spots, 3 * per, tuple(range(3 * per, 4 * per)), depth
        )
        grad_r, keep_r, send_r = grad_call(
            unit_t, shifted_early, scale, weight, spots, 0, (*order_t, *order_s), depth
        )

        def within(keep, out, names):
            for bit in range(narrow.bit_length() - 2, 0, -1):
                keep = keep + to_core(out, 1 << bit).astype(jnp.float32)
                half = keep.shape[0] // 2
                keep, out = keep[:half], keep[half:].astype(low)
            return [keep, to_core(out, 1)], [names, names.translate(str.maketrans("TS", "ST"))]

        arrays, places = within(keep_d, send_d, "D")
        arrays[1], send_r = lax.optimization_barrier((arrays[1], send_r))
        sum_d, = add_call(arrays, places, "D", size)
        unit_t, sum_d = lax.optimization_barrier((unit_t, sum_d))
        grad_j, keep_j, send_j = grad_call(
            unit_t, shifted_early, scale, weight, spots, 0, tuple(order_j), depth
        )
        from_d = to_s(sum_d)
        arrays, places = within(keep_r, send_r, "TS")
        arrays_j, places_j = within(keep_j, send_j, "J")
        sum_s, = add_call(arrays, places, "S", size)
        from_s = to_s(sum_s)
        from_d, grad_j, _ = lax.optimization_barrier((from_d, grad_j, sum_s))
        sum_t, = add_call([*arrays, from_d], [*places, "T"], "T", size)
        from_t = to_t(sum_t)
        sum_j, = add_call([*arrays_j, from_s], [*places_j, "J"], "J", size, jnp.float32, heavy)
        proxy_grad = proxy_call(
            [grad_d, grad_r, grad_j], [groups[3], groups[1], groups[2], groups[0]], picked
        )
        from_t, proxy_grad, sum_j = lax.optimization_barrier((from_t, proxy_grad, sum_j))
        mine, *others = own_call([sum_j, from_t], "JJ", depth, size)
        mine = finish_call(mine, reach(dict(enumerate(others, 1))))
        if narrow == 2:
            feature_grad = join_call(mine, to_core(mine, 1))
        else:
            mine = mine[None]
            for bit in range(narrow.bit_length() - 1):
                mine = jnp.concatenate([mine, to_core(mine, 1 << bit)], axis=0)
            feature_grad = jnp.take(mine, n ^ jnp.arange(narrow), axis=0).transpose(1, 0, 2).reshape(rows, width)
        return (feature_grad, proxy_grad)

    return per_device


def solution(mesh):
    placed = (P("wide", None), P(("wide", "narrow"), None), P(("wide", "narrow")), P(), P())
    return jax.shard_map(
        make(mesh.shape["wide"], mesh.shape["narrow"]),
        mesh=mesh,
        in_specs=placed,
        out_specs=(P("wide", None), P(("wide", "narrow"), None)),
        check_vma=False,
    )
```

```python
import functools
import math

import jax
import jax.numpy as jnp
from jax import lax
from jax.experimental import pallas as pl
from jax.experimental.pallas import tpu as pltpu
from jax.sharding import PartitionSpec as P

logit_scale = 3.0
epsilon = 1e-06
exp2_scale = logit_scale * math.log2(math.e)
chunk = 256
both = ("wide", "narrow")
whole = pl.BlockSpec(memory_space=pltpu.VMEM)
params = pltpu.CompilerParams(vmem_limit_bytes=8 * 1024 * 1024)
light = pl.CostEstimate(flops=0, bytes_accessed=1 << 19, transcendentals=0)
heavy = pl.CostEstimate(flops=0, bytes_accessed=10 << 20, transcendentals=0)


def t_bit(n):
    return 1 if n % 2 == 0 else 2


def s_bit(n):
    return 3 - t_bit(n)


def exchange(x, sizes, partner, movers=None):
    wide, narrow = sizes
    pairs = []
    for w in range(wide):
        for n in range(narrow):
            pw, pn = partner(w, n) if movers is None or n in movers else (w, n)
            pairs.append((w * narrow + n, pw * narrow + pn))
    return lax.ppermute(x, both, pairs)


def logits_kernel(group_count, part_count, with_early, unit_ref, *refs):
    parts = refs[: group_count * part_count]
    shifted_ref, stats_ref = refs[-2:]
    per = chunk // 128
    first = 0
    if with_early:
        early_ref = refs[group_count * part_count]
        first = early_ref.shape[0] // 2
        half = stats_ref.shape[0] // 2
        stats_ref[0:first, :] = early_ref[0:first, :]
        stats_ref[half:half + first, :] = early_ref[first:, :]
    half = stats_ref.shape[0] // 2
    step = 0
    for g in range(group_count):
        group = parts[g * part_count:(g + 1) * part_count]
        cols = group[0].shape[1]
        for row in range(0, group[0].shape[0], chunk):
            dots = None
            for k, part in enumerate(group):
                prod = lax.dot_general(
                    unit_ref[:, k * cols:(k + 1) * cols], part[row:row + chunk, :],
                    (((1,), (1,)), ((), ())), preferred_element_type=jnp.float32,
                )
                dots = prod if dots is None else dots + prod
            top = jnp.max(dots, axis=0, keepdims=True)
            shifted = jnp.exp2((dots - top) * exp2_scale)
            total = jnp.sum(shifted, axis=0, keepdims=True)
            shifted_ref[:, step * chunk:(step + 1) * chunk] = shifted
            for b in range(per):
                at = first + step * per + b
                stats_ref[at:at + 1, :] = top[:, b * 128:(b + 1) * 128]
                stats_ref[half + at:half + at + 1, :] = total[:, b * 128:(b + 1) * 128]
            step += 1


def logits_call(unit, groups, early=None):
    rows = groups[0][0].shape[0]
    count = len(groups) * rows
    samples = unit.shape[0]
    flat = [part for group in groups for part in group]
    lines = 2 * count // 128
    if early is not None:
        lines += early.shape[0]
        flat.append(early)
    return pl.pallas_call(
        functools.partial(logits_kernel, len(groups), len(groups[0]), early is not None),
        out_shape=(
            jax.ShapeDtypeStruct((samples, count), jnp.float32),
            jax.ShapeDtypeStruct((lines, 128), jnp.float32),
        ),
        in_specs=[whole] * (1 + len(flat)),
        out_specs=(whole, whole),
        compiler_params=params,
        cost_estimate=pl.CostEstimate(
            flops=2 * samples * count * unit.shape[1],
            bytes_accessed=4 * samples * count,
            transcendentals=samples * count,
        ),
        name="logits",
    )(unit, *flat)


def grad_kernel(first, steps, depth, unit_t_ref, shifted_ref, scale_ref, weight_ref, at_ref, grad_ref, keep_ref, send_ref):
    samples = shifted_ref.shape[0]
    half = unit_t_ref.shape[0] // 2
    per = chunk // 128
    w, n = lax.axis_index("wide"), lax.axis_index("narrow")
    base = (w * lax.axis_size("narrow") + n) * samples
    cand = lax.broadcasted_iota(jnp.int32, (samples, chunk), 0) + base

    def row(ref, at):
        return jnp.concatenate([ref[at + b:at + b + 1, :] for b in range(per)], axis=1)

    def far_row(ref, at):
        lines = []
        for b in range(at, at + per):
            g, z = divmod(b, depth)
            offset = jnp.where(n % 2 == 0, 4 * z + g, 4 * z + (g % 2) * 2 + g // 2)
            lines.append(ref[pl.ds(jnp.bitwise_xor(w, offset), 1), :])
        return jnp.concatenate(lines, axis=1)

    for out, at in enumerate(steps):
        cols = slice((at - first) * chunk, (at - first + 1) * chunk)
        scale, weight, spot = row(scale_ref, at * per), far_row(weight_ref, at * per), far_row(at_ref, at * per)
        soft = shifted_ref[:, cols] * scale
        grad = (weight * jnp.where(cand == spot, soft - 1.0, soft)).astype(jnp.bfloat16)
        out_cols = slice(out * chunk, (out + 1) * chunk)
        grad_ref[:, out_cols] = grad
        shares = logit_scale * jnp.dot(unit_t_ref[...], grad, preferred_element_type=jnp.float32)
        keep_ref[:, out_cols] = shares[:half]
        send_ref[:, out_cols] = shares[half:].astype(jnp.bfloat16)


def grad_call(unit_t, shifted, scale, weight, spots, first, steps, depth):
    samples = shifted.shape[0]
    width = unit_t.shape[0]
    count = len(steps) * chunk
    return pl.pallas_call(
        functools.partial(grad_kernel, first, steps, depth),
        out_shape=(
            jax.ShapeDtypeStruct((samples, count), jnp.bfloat16),
            jax.ShapeDtypeStruct((width // 2, count), jnp.float32),
            jax.ShapeDtypeStruct((width // 2, count), jnp.bfloat16),
        ),
        in_specs=[whole] * 5,
        out_specs=(whole,) * 3,
        compiler_params=params,
        cost_estimate=pl.CostEstimate(
            flops=2 * samples * count * width, bytes_accessed=6 * samples * count, transcendentals=0
        ),
        name="grads",
    )(unit_t, shifted, scale, weight, spots)


def proxy_kernel(grad_count, group_count, part_count, rows, *refs):
    grad_refs, refs = refs[:grad_count], refs[grad_count:]
    parts = refs[:group_count * part_count]
    *picked_refs, out_ref = refs[group_count * part_count:]
    size, cols = parts[0].shape
    grads = [ref.at[:, at:at + size] for ref in grad_refs for at in range(0, ref.shape[1], size)]
    n = lax.axis_index("narrow")
    places = []
    for k in range(part_count):
        if part_count == 1:
            places.append(slice(0, cols))
        else:
            places.append(pl.ds(pl.multiple_of((n ^ k) * cols, cols), cols))
    tiles = [(ref, row) for ref in picked_refs for row in range(0, ref.shape[0], rows)]
    for tile, (picked_ref, row) in enumerate(tiles):
        at, here = slice(tile * rows, (tile + 1) * rows), slice(row, row + rows)
        sums = []
        for k in range(part_count):
            total = None
            for g in range(group_count):
                prod = jnp.dot(
                    grads[g][at, :], parts[g * part_count + k][...], preferred_element_type=jnp.float32
                )
                total = prod if total is None else total + prod
            sums.append(logit_scale * total)
        picked = [picked_ref[here, place] for place in places]
        square = functools.reduce(jnp.add, [jnp.sum(p * p, axis=1, keepdims=True) for p in picked])
        inverse = 1.0 / jnp.sqrt(square + epsilon)
        inner = functools.reduce(jnp.add, [jnp.sum(p * s, axis=1, keepdims=True) for p, s in zip(picked, sums)])
        slope = inner * inverse * inverse
        for place, p, s in zip(places, picked, sums):
            out_ref[at, place] = (s - p * slope) * inverse


def proxy_call(grads, groups, picked):
    samples, width = grads[0].shape[0], picked[0].shape[1]
    count = sum(grad.shape[1] for grad in grads)
    flat = [part for group in groups for part in group]
    return pl.pallas_call(
        functools.partial(proxy_kernel, len(grads), len(groups), len(groups[0]), 256),
        out_shape=jax.ShapeDtypeStruct((samples, width), jnp.float32),
        in_specs=[whole] * (len(grads) + len(flat) + len(picked)),
        out_specs=whole,
        compiler_params=params,
        cost_estimate=pl.CostEstimate(
            flops=2 * samples * count * width, bytes_accessed=4 * samples * count, transcendentals=0
        ),
        name="proxy_grads",
    )(*grads, *flat, *picked)


def merge_kernel(flips, swap, with_scale, *refs):
    ins, out_ref = refs[:-1], refs[-1]
    if with_scale:
        own_ref, ins = ins[-1], ins[:-1]
    blocks = ins[0].shape[0] // 2
    for b in range(blocks):
        spots = [swap(f, b) for f in flips]
        tops = [ref[at:at + 1, :] for ref, at in zip(ins, spots)]
        totals = [ref[blocks + at:blocks + at + 1, :] for ref, at in zip(ins, spots)]
        top = functools.reduce(jnp.maximum, tops)
        total = functools.reduce(
            jnp.add, [t * jnp.exp2((m - top) * exp2_scale) for m, t in zip(tops, totals)]
        )
        if with_scale:
            out_ref[b:b + 1, :] = jnp.exp2((own_ref[b:b + 1, :] - top) * exp2_scale) / total
        else:
            out_ref[b:b + 1, :] = top
            out_ref[blocks + b:blocks + b + 1, :] = total


def merge(stats, flips, swap, own=None):
    lines = stats[0].shape[0]
    if own is not None:
        stats, lines = [*stats, own], lines // 2
    return pl.pallas_call(
        functools.partial(merge_kernel, flips, swap, own is not None),
        out_shape=jax.ShapeDtypeStruct((lines, 128), jnp.float32),
        in_specs=[whole] * len(stats),
        out_specs=whole,
        compiler_params=params,
        cost_estimate=light,
        name="merge_stats",
    )(*stats)


def scale_kernel(swap, own_ref, merged_ref, other_ref, out_ref):
    blocks = out_ref.shape[0]
    odd = lax.axis_index("narrow") % 2 == 1
    for b in range(blocks):
        far = swap(1, b)
        top = jnp.where(odd, merged_ref[b:b + 1, :], other_ref[far:far + 1, :])
        total = jnp.where(
            odd, merged_ref[blocks + b:blocks + b + 1, :], other_ref[blocks + far:blocks + far + 1, :]
        )
        out_ref[b:b + 1, :] = jnp.exp2((own_ref[b:b + 1, :] - top) * exp2_scale) / total


def scale_call(own, merged, other, swap):
    return pl.pallas_call(
        functools.partial(scale_kernel, swap),
        out_shape=jax.ShapeDtypeStruct((own.shape[0] // 2, 128), jnp.float32),
        in_specs=[whole] * 3,
        out_specs=whole,
        compiler_params=params,
        cost_estimate=light,
        name="scale_rows",
    )(own, merged, other)


def stack_kernel(places, *refs):
    rows = refs[0].shape[0]
    for k, ref in zip(places, refs):
        refs[-1][k * rows:(k + 1) * rows, :] = ref[...]


def stack_call(parts, places):
    rows, cols = parts[0].shape
    return pl.pallas_call(
        functools.partial(stack_kernel, places),
        out_shape=jax.ShapeDtypeStruct((len(parts) * rows, cols), parts[0].dtype),
        in_specs=[whole] * len(parts),
        out_specs=whole,
        compiler_params=params,
        cost_estimate=light,
        name="stack_blocks",
    )(*parts)


def add_kernel(ins, outs, size, *refs):
    for name, out_ref in zip(outs, refs[len(ins):]):
        total = None
        for places, ref in zip(ins, refs):
            if name in places:
                at = places.index(name)
                term = ref[:, at * size:(at + 1) * size].astype(jnp.float32)
                total = term if total is None else total + term
        out_ref[...] = total.astype(out_ref.dtype)


def add_call(arrays, ins, outs, size, dtype=jnp.bfloat16, cost=light):
    rows = arrays[0].shape[0]
    result = pl.pallas_call(
        functools.partial(add_kernel, ins, outs, size),
        out_shape=[jax.ShapeDtypeStruct((rows, size), dtype) for _ in outs],
        in_specs=[whole] * len(arrays),
        out_specs=[whole] * len(outs),
        compiler_params=params,
        cost_estimate=cost,
        name="add_shares",
    )(*arrays)
    return result


def own_kernel(ins, count, size, *refs):
    cols = size // count
    for k, out_ref in enumerate(refs[len(ins):]):
        total = None
        for places, ref in zip(ins, refs):
            at = places.index("J") * size + k * cols
            term = ref[:, at:at + cols].astype(jnp.float32)
            total = term if total is None else total + term
        out_ref[...] = total.astype(out_ref.dtype)


def own_call(arrays, ins, count, size):
    rows = arrays[0].shape[0]
    return pl.pallas_call(
        functools.partial(own_kernel, ins, count, size),
        out_shape=[
            jax.ShapeDtypeStruct((rows, size // count), jnp.bfloat16 if k else jnp.float32) for k in range(count)
        ],
        in_specs=[whole] * len(arrays),
        out_specs=[whole] * count,
        compiler_params=params,
        cost_estimate=light,
        name="add_shares_z",
    )(*arrays)


def prep_kernel(part_count, *refs):
    *picked_refs, unit_ref, unit_t_ref = refs
    width = picked_refs[0].shape[1]
    cols = width // part_count
    tiles = [(ref, row) for ref in picked_refs for row in range(0, ref.shape[0], 256)]
    n = lax.axis_index("narrow")
    for line, (picked_ref, row) in enumerate(tiles):
        line *= 256
        at = slice(row, row + 256)
        if part_count == 1:
            picked = picked_ref[at, :]
        else:
            picked = jnp.concatenate(
                [picked_ref[at, pl.ds(pl.multiple_of((n ^ k) * cols, cols), cols)] for k in range(part_count)],
                axis=1,
            )
        lengths = jnp.sqrt(jnp.sum(picked * picked, axis=1, keepdims=True) + epsilon)
        unit = picked / lengths
        unit_ref[line:line + 256, :] = unit.astype(jnp.bfloat16)
        unit_t_ref[:, line:line + 256] = unit.T.astype(jnp.bfloat16)


def prep_call(picked, part_count):
    samples, width = sum(p.shape[0] for p in picked), picked[0].shape[1]
    return pl.pallas_call(
        functools.partial(prep_kernel, part_count),
        out_shape=(
            jax.ShapeDtypeStruct((samples, width), jnp.bfloat16),
            jax.ShapeDtypeStruct((width, samples), jnp.bfloat16),
        ),
        in_specs=[whole] * len(picked),
        out_specs=(whole, whole),
        compiler_params=params,
        cost_estimate=pl.CostEstimate(flops=4 * samples * width, bytes_accessed=8 * samples * width, transcendentals=0),
        name="unit_rows",
    )(*picked)


def finish_kernel(*refs):
    ins, out_ref = refs[:-1], refs[-1]
    total = functools.reduce(jnp.add, [ref[...].astype(jnp.float32) for ref in ins])
    out_ref[...] = total.T


def finish_call(own, others):
    return pl.pallas_call(
        finish_kernel,
        out_shape=jax.ShapeDtypeStruct((own.shape[1], own.shape[0]), jnp.float32),
        in_specs=[whole] * (1 + len(others)),
        out_specs=whole,
        compiler_params=params,
        cost_estimate=light,
        name="feature_sums",
    )(own, *others)


def join_kernel(own_ref, other_ref, out_ref):
    cols = own_ref.shape[1]
    n = lax.axis_index("narrow")
    out_ref[:, pl.ds(pl.multiple_of(n * cols, cols), cols)] = own_ref[...]
    out_ref[:, pl.ds(pl.multiple_of((1 - n) * cols, cols), cols)] = other_ref[...]


def join_call(own, other):
    return pl.pallas_call(
        join_kernel,
        out_shape=jax.ShapeDtypeStruct((own.shape[0], 2 * own.shape[1]), jnp.float32),
        in_specs=[whole] * 2,
        out_specs=whole,
        compiler_params=params,
        cost_estimate=light,
        name="feature_grad",
    )(own, other)


def make(wide, narrow):
    depth = wide // 4
    sizes = (wide, narrow)
    send = functools.partial(exchange, sizes=sizes)

    def to_t(x, movers=None):
        return send(x, partner=lambda w, n: (w ^ t_bit(n), n), movers=movers)

    def to_s(x, movers=None):
        return send(x, partner=lambda w, n: (w ^ s_bit(n), n), movers=movers)

    def to_ts(x, movers=None):
        return send(x, partner=lambda w, n: (w ^ 3, n), movers=movers)

    def to_z(x, k, movers=None):
        return send(x, partner=lambda w, n: (w ^ (k << 2), n), movers=movers)

    far_first = sorted(range(1, depth), key=lambda k: (k == 1, k))

    def reach(parts, order=far_first, movers=None):
        return [to_z(parts[k] if isinstance(parts, dict) else parts, k, movers) for k in order]

    def to_core(x, k):
        return send(x, partner=lambda w, n: (w, n ^ k))

    def per_device(features, proxies, sample_ids, positives, loss_weight):
        samples = sample_ids.shape[0]
        rows, width = features.shape
        w = lax.axis_index("wide")
        n = lax.axis_index("narrow")

        if narrow == 2:
            cols = width // 2
            part = jnp.where(n == 0, features[:, :cols], features[:, cols:])
        else:
            part = features
        zs = reach(part, far_first[::-1])
        near = samples // 4
        picked = [
            proxies.at[ids].get(mode="promise_in_bounds", wrap_negative_indices=False)
            for ids in (sample_ids[:near], sample_ids[near:])
        ]
        *zs, picked[0] = lax.optimization_barrier((*zs, picked[0]))
        group_j = stack_call([part] + zs, [0] + far_first[::-1])
        group_s, group_t, picked[1] = lax.optimization_barrier((to_s(group_j), to_t(group_j), picked[1]))
        group_d = to_s(group_t)
        groups = [(group_j,), (group_t,), (group_s,)]
        if narrow == 2:
            others = [to_core(group_j, 1), to_core(group_s, 1), to_core(group_t, 1)]
            groups = [(*group, other) for group, other in zip(groups, others)]

        unit, unit_t = prep_call(picked, 2 if narrow == 2 else 1)
        if narrow != 2:
            unit_t = jnp.take(unit_t.reshape(narrow, width // narrow, samples), n ^ jnp.arange(narrow), axis=0)
            unit_t = unit_t.reshape(width, samples)

        spots = positives.reshape(wide, rows)
        weight = loss_weight.reshape(wide, rows)

        shifted_early, stats_early = logits_call(unit, groups)
        group_d, stats_early = lax.optimization_barrier((group_d, stats_early))
        groups.append((group_d, to_core(group_d, 1)) if narrow == 2 else (group_d,))
        shifted_late, own = logits_call(unit, groups[3:], stats_early)
        stats = own

        def swap_groups(flip, b):
            g, z = divmod(b, depth)
            return ((g % 2) * 2 + g // 2) * depth + z if flip else b

        for bit in range(narrow.bit_length() - 1):
            stats = merge([stats, to_core(stats, 1 << bit)], (0, int(bit == 0)), swap_groups)
        one = (1,) if narrow == 2 else None
        others = reach(stats, movers=one)
        stats = merge([stats] + others, [0] + far_first, lambda k, b: b ^ k)
        others = [to_t(stats, one), to_s(stats, one), to_ts(stats, one)]
        last = [stats] + others, (0, 1, 2, 3), lambda k, b: b ^ (k * depth)
        if narrow == 2:
            stats = merge(*last)
            scale = scale_call(own, stats, to_core(stats, 1), swap_groups)
        else:
            scale = merge(*last, own)

        per = depth * rows // chunk
        order_t, order_s, order_j = range(per, 2 * per), range(2 * per, 3 * per), range(per)
        size = depth * rows
        low = jnp.bfloat16
        grad_d, keep_d, send_d = grad_call(
            unit_t, shifted_late, scale, weight, spots, 3 * per, tuple(range(3 * per, 4 * per)), depth
        )
        grad_r, keep_r, send_r = grad_call(
            unit_t, shifted_early, scale, weight, spots, 0, (*order_t, *order_s), depth
        )

        def within(keep, out, names):
            for bit in range(narrow.bit_length() - 2, 0, -1):
                keep = keep + to_core(out, 1 << bit).astype(jnp.float32)
                half = keep.shape[0] // 2
                keep, out = keep[:half], keep[half:].astype(low)
            return [keep, to_core(out, 1)], [names, names.translate(str.maketrans("TS", "ST"))]

        arrays, places = within(keep_d, send_d, "D")
        arrays[1], send_r = lax.optimization_barrier((arrays[1], send_r))
        sum_d, = add_call(arrays, places, "D", size)
        unit_t, sum_d = lax.optimization_barrier((unit_t, sum_d))
        grad_j, keep_j, send_j = grad_call(
            unit_t, shifted_early, scale, weight, spots, 0, tuple(order_j), depth
        )
        from_d = to_s(sum_d)
        arrays, places = within(keep_r, send_r, "TS")
        arrays_j, places_j = within(keep_j, send_j, "J")
        sum_s, = add_call(arrays, places, "S", size)
        from_s = to_s(sum_s)
        from_d, grad_j, _ = lax.optimization_barrier((from_d, grad_j, sum_s))
        sum_t, = add_call([*arrays, from_d], [*places, "T"], "T", size)
        from_t = to_t(sum_t)
        sum_j, = add_call([*arrays_j, from_s], [*places_j, "J"], "J", size, jnp.float32, heavy)
        proxy_grad = proxy_call(
            [grad_d, grad_r, grad_j], [groups[3], groups[1], groups[2], groups[0]], picked
        )
        from_t, proxy_grad, sum_j = lax.optimization_barrier((from_t, proxy_grad, sum_j))
        mine, *others = own_call([sum_j, from_t], "JJ", depth, size)
        mine = finish_call(mine, reach(dict(enumerate(others, 1))))
        if narrow == 2:
            feature_grad = join_call(mine, to_core(mine, 1))
        else:
            mine = mine[None]
            for bit in range(narrow.bit_length() - 1):
                mine = jnp.concatenate([mine, to_core(mine, 1 << bit)], axis=0)
            feature_grad = jnp.take(mine, n ^ jnp.arange(narrow), axis=0).transpose(1, 0, 2).reshape(rows, width)
        return (feature_grad, proxy_grad)

    return per_device


def solution(mesh):
    placed = (P("wide", None), P(("wide", "narrow"), None), P(("wide", "narrow")), P(), P())
    return jax.shard_map(
        make(mesh.shape["wide"], mesh.shape["narrow"]),
        mesh=mesh,
        in_specs=placed,
        out_specs=(P("wide", None), P(("wide", "narrow"), None)),
        check_vma=False,
    )
```

```python
import functools
import math

import jax
import jax.numpy as jnp
from jax import lax
from jax.experimental import pallas as pl
from jax.experimental.pallas import tpu as pltpu
from jax.sharding import PartitionSpec as P

logit_scale = 3.0
epsilon = 1e-06
exp2_scale = logit_scale * math.log2(math.e)
chunk = 256
both = ("wide", "narrow")
whole = pl.BlockSpec(memory_space=pltpu.VMEM)
params = pltpu.CompilerParams(vmem_limit_bytes=8 * 1024 * 1024)
light = pl.CostEstimate(flops=0, bytes_accessed=1 << 19, transcendentals=0)
heavy = pl.CostEstimate(flops=0, bytes_accessed=10 << 20, transcendentals=0)


def t_bit(n):
    return 1 if n % 2 == 0 else 2


def s_bit(n):
    return 3 - t_bit(n)


def exchange(x, sizes, partner):
    wide, narrow = sizes
    pairs = []
    for w in range(wide):
        for n in range(narrow):
            pw, pn = partner(w, n)
            pairs.append((w * narrow + n, pw * narrow + pn))
    return lax.ppermute(x, both, pairs)


def logits_kernel(group_count, part_count, with_early, unit_ref, *refs):
    parts = refs[: group_count * part_count]
    shifted_ref, stats_ref = refs[-2:]
    per = chunk // 128
    first = 0
    if with_early:
        early_ref = refs[group_count * part_count]
        first = early_ref.shape[0] // 2
        half = stats_ref.shape[0] // 2
        stats_ref[0:first, :] = early_ref[0:first, :]
        stats_ref[half:half + first, :] = early_ref[first:, :]
    half = stats_ref.shape[0] // 2
    step = 0
    for g in range(group_count):
        group = parts[g * part_count:(g + 1) * part_count]
        cols = group[0].shape[1]
        for row in range(0, group[0].shape[0], chunk):
            dots = None
            for k, part in enumerate(group):
                prod = lax.dot_general(
                    unit_ref[:, k * cols:(k + 1) * cols], part[row:row + chunk, :],
                    (((1,), (1,)), ((), ())), preferred_element_type=jnp.float32,
                )
                dots = prod if dots is None else dots + prod
            top = jnp.max(dots, axis=0, keepdims=True)
            shifted = jnp.exp2((dots - top) * exp2_scale)
            total = jnp.sum(shifted, axis=0, keepdims=True)
            shifted_ref[:, step * chunk:(step + 1) * chunk] = shifted
            for b in range(per):
                at = first + step * per + b
                stats_ref[at:at + 1, :] = top[:, b * 128:(b + 1) * 128]
                stats_ref[half + at:half + at + 1, :] = total[:, b * 128:(b + 1) * 128]
            step += 1


def logits_call(unit, groups, early=None):
    rows = groups[0][0].shape[0]
    count = len(groups) * rows
    samples = unit.shape[0]
    flat = [part for group in groups for part in group]
    lines = 2 * count // 128
    if early is not None:
        lines += early.shape[0]
        flat.append(early)
    return pl.pallas_call(
        functools.partial(logits_kernel, len(groups), len(groups[0]), early is not None),
        out_shape=(
            jax.ShapeDtypeStruct((samples, count), jnp.float32),
            jax.ShapeDtypeStruct((lines, 128), jnp.float32),
        ),
        in_specs=[whole] * (1 + len(flat)),
        out_specs=(whole, whole),
        compiler_params=params,
        cost_estimate=pl.CostEstimate(
            flops=2 * samples * count * unit.shape[1],
            bytes_accessed=4 * samples * count,
            transcendentals=samples * count,
        ),
        name="logits",
    )(unit, *flat)


def grad_kernel(first, steps, depth, unit_t_ref, shifted_ref, scale_ref, weight_ref, at_ref, grad_ref, keep_ref, send_ref):
    samples = shifted_ref.shape[0]
    half = unit_t_ref.shape[0] // 2
    per = chunk // 128
    w, n = lax.axis_index("wide"), lax.axis_index("narrow")
    base = (w * lax.axis_size("narrow") + n) * samples
    cand = lax.broadcasted_iota(jnp.int32, (samples, chunk), 0) + base

    def row(ref, at):
        return jnp.concatenate([ref[at + b:at + b + 1, :] for b in range(per)], axis=1)

    def far_row(ref, at):
        lines = []
        for b in range(at, at + per):
            g, z = divmod(b, depth)
            offset = jnp.where(n % 2 == 0, 4 * z + g, 4 * z + (g % 2) * 2 + g // 2)
            lines.append(ref[pl.ds(jnp.bitwise_xor(w, offset), 1), :])
        return jnp.concatenate(lines, axis=1)

    for out, at in enumerate(steps):
        cols = slice((at - first) * chunk, (at - first + 1) * chunk)
        scale, weight, spot = row(scale_ref, at * per), far_row(weight_ref, at * per), far_row(at_ref, at * per)
        soft = shifted_ref[:, cols] * scale
        grad = (weight * jnp.where(cand == spot, soft - 1.0, soft)).astype(jnp.bfloat16)
        out_cols = slice(out * chunk, (out + 1) * chunk)
        grad_ref[:, out_cols] = grad
        shares = logit_scale * jnp.dot(unit_t_ref[...], grad, preferred_element_type=jnp.float32)
        keep_ref[:, out_cols] = shares[:half]
        send_ref[:, out_cols] = shares[half:].astype(jnp.bfloat16)


def grad_call(unit_t, shifted, scale, weight, spots, first, steps, depth):
    samples = shifted.shape[0]
    width = unit_t.shape[0]
    count = len(steps) * chunk
    return pl.pallas_call(
        functools.partial(grad_kernel, first, steps, depth),
        out_shape=(
            jax.ShapeDtypeStruct((samples, count), jnp.bfloat16),
            jax.ShapeDtypeStruct((width // 2, count), jnp.float32),
            jax.ShapeDtypeStruct((width // 2, count), jnp.bfloat16),
        ),
        in_specs=[whole] * 5,
        out_specs=(whole,) * 3,
        compiler_params=params,
        cost_estimate=pl.CostEstimate(
            flops=2 * samples * count * width, bytes_accessed=6 * samples * count, transcendentals=0
        ),
        name="grads",
    )(unit_t, shifted, scale, weight, spots)


def proxy_kernel(grad_count, group_count, part_count, rows, *refs):
    grad_refs, refs = refs[:grad_count], refs[grad_count:]
    parts = refs[:group_count * part_count]
    *picked_refs, out_ref = refs[group_count * part_count:]
    size, cols = parts[0].shape
    grads = [ref.at[:, at:at + size] for ref in grad_refs for at in range(0, ref.shape[1], size)]
    n = lax.axis_index("narrow")
    places = []
    for k in range(part_count):
        if part_count == 1:
            places.append(slice(0, cols))
        else:
            places.append(pl.ds(pl.multiple_of((n ^ k) * cols, cols), cols))
    tiles = [(ref, row) for ref in picked_refs for row in range(0, ref.shape[0], rows)]
    for tile, (picked_ref, row) in enumerate(tiles):
        at, here = slice(tile * rows, (tile + 1) * rows), slice(row, row + rows)
        sums = []
        for k in range(part_count):
            total = None
            for g in range(group_count):
                prod = jnp.dot(
                    grads[g][at, :], parts[g * part_count + k][...], preferred_element_type=jnp.float32
                )
                total = prod if total is None else total + prod
            sums.append(logit_scale * total)
        picked = [picked_ref[here, place] for place in places]
        square = functools.reduce(jnp.add, [jnp.sum(p * p, axis=1, keepdims=True) for p in picked])
        inverse = 1.0 / jnp.sqrt(square + epsilon)
        inner = functools.reduce(jnp.add, [jnp.sum(p * s, axis=1, keepdims=True) for p, s in zip(picked, sums)])
        slope = inner * inverse * inverse
        for place, p, s in zip(places, picked, sums):
            out_ref[at, place] = (s - p * slope) * inverse


def proxy_call(grads, groups, picked):
    samples, width = grads[0].shape[0], picked[0].shape[1]
    count = sum(grad.shape[1] for grad in grads)
    flat = [part for group in groups for part in group]
    return pl.pallas_call(
        functools.partial(proxy_kernel, len(grads), len(groups), len(groups[0]), 256),
        out_shape=jax.ShapeDtypeStruct((samples, width), jnp.float32),
        in_specs=[whole] * (len(grads) + len(flat) + len(picked)),
        out_specs=whole,
        compiler_params=params,
        cost_estimate=pl.CostEstimate(
            flops=2 * samples * count * width, bytes_accessed=4 * samples * count, transcendentals=0
        ),
        name="proxy_grads",
    )(*grads, *flat, *picked)


def merge_kernel(flips, swap, with_scale, *refs):
    ins, out_ref = refs[:-1], refs[-1]
    if with_scale:
        own_ref, ins = ins[-1], ins[:-1]
    blocks = ins[0].shape[0] // 2
    for b in range(blocks):
        spots = [swap(f, b) for f in flips]
        tops = [ref[at:at + 1, :] for ref, at in zip(ins, spots)]
        totals = [ref[blocks + at:blocks + at + 1, :] for ref, at in zip(ins, spots)]
        top = functools.reduce(jnp.maximum, tops)
        total = functools.reduce(
            jnp.add, [t * jnp.exp2((m - top) * exp2_scale) for m, t in zip(tops, totals)]
        )
        if with_scale:
            out_ref[b:b + 1, :] = jnp.exp2((own_ref[b:b + 1, :] - top) * exp2_scale) / total
        else:
            out_ref[b:b + 1, :] = top
            out_ref[blocks + b:blocks + b + 1, :] = total


def merge(stats, flips, swap, own=None):
    lines = stats[0].shape[0]
    if own is not None:
        stats, lines = [*stats, own], lines // 2
    return pl.pallas_call(
        functools.partial(merge_kernel, flips, swap, own is not None),
        out_shape=jax.ShapeDtypeStruct((lines, 128), jnp.float32),
        in_specs=[whole] * len(stats),
        out_specs=whole,
        compiler_params=params,
        cost_estimate=light,
        name="merge_stats",
    )(*stats)


def stack_kernel(places, *refs):
    rows = refs[0].shape[0]
    for k, ref in zip(places, refs):
        refs[-1][k * rows:(k + 1) * rows, :] = ref[...]


def stack_call(parts, places):
    rows, cols = parts[0].shape
    return pl.pallas_call(
        functools.partial(stack_kernel, places),
        out_shape=jax.ShapeDtypeStruct((len(parts) * rows, cols), parts[0].dtype),
        in_specs=[whole] * len(parts),
        out_specs=whole,
        compiler_params=params,
        cost_estimate=light,
        name="stack_blocks",
    )(*parts)


def add_kernel(ins, outs, size, *refs):
    for name, out_ref in zip(outs, refs[len(ins):]):
        total = None
        for places, ref in zip(ins, refs):
            if name in places:
                at = places.index(name)
                term = ref[:, at * size:(at + 1) * size].astype(jnp.float32)
                total = term if total is None else total + term
        out_ref[...] = total.astype(out_ref.dtype)


def add_call(arrays, ins, outs, size, dtype=jnp.bfloat16, cost=light):
    rows = arrays[0].shape[0]
    result = pl.pallas_call(
        functools.partial(add_kernel, ins, outs, size),
        out_shape=[jax.ShapeDtypeStruct((rows, size), dtype) for _ in outs],
        in_specs=[whole] * len(arrays),
        out_specs=[whole] * len(outs),
        compiler_params=params,
        cost_estimate=cost,
        name="add_shares",
    )(*arrays)
    return result


def own_kernel(ins, count, size, *refs):
    cols = size // count
    for k, out_ref in enumerate(refs[len(ins):]):
        total = None
        for places, ref in zip(ins, refs):
            at = places.index("J") * size + k * cols
            term = ref[:, at:at + cols].astype(jnp.float32)
            total = term if total is None else total + term
        out_ref[...] = total.astype(out_ref.dtype)


def own_call(arrays, ins, count, size):
    rows = arrays[0].shape[0]
    return pl.pallas_call(
        functools.partial(own_kernel, ins, count, size),
        out_shape=[
            jax.ShapeDtypeStruct((rows, size // count), jnp.bfloat16 if k else jnp.float32) for k in range(count)
        ],
        in_specs=[whole] * len(arrays),
        out_specs=[whole] * count,
        compiler_params=params,
        cost_estimate=light,
        name="add_shares_z",
    )(*arrays)


def prep_kernel(part_count, *refs):
    *picked_refs, unit_ref, unit_t_ref = refs
    width = picked_refs[0].shape[1]
    cols = width // part_count
    tiles = [(ref, row) for ref in picked_refs for row in range(0, ref.shape[0], 256)]
    n = lax.axis_index("narrow")
    for line, (picked_ref, row) in enumerate(tiles):
        line *= 256
        at = slice(row, row + 256)
        if part_count == 1:
            picked = picked_ref[at, :]
        else:
            picked = jnp.concatenate(
                [picked_ref[at, pl.ds(pl.multiple_of((n ^ k) * cols, cols), cols)] for k in range(part_count)],
                axis=1,
            )
        lengths = jnp.sqrt(jnp.sum(picked * picked, axis=1, keepdims=True) + epsilon)
        unit = picked / lengths
        unit_ref[line:line + 256, :] = unit.astype(jnp.bfloat16)
        unit_t_ref[:, line:line + 256] = unit.T.astype(jnp.bfloat16)


def prep_call(picked, part_count):
    samples, width = sum(p.shape[0] for p in picked), picked[0].shape[1]
    return pl.pallas_call(
        functools.partial(prep_kernel, part_count),
        out_shape=(
            jax.ShapeDtypeStruct((samples, width), jnp.bfloat16),
            jax.ShapeDtypeStruct((width, samples), jnp.bfloat16),
        ),
        in_specs=[whole] * len(picked),
        out_specs=(whole, whole),
        compiler_params=params,
        cost_estimate=pl.CostEstimate(flops=4 * samples * width, bytes_accessed=8 * samples * width, transcendentals=0),
        name="unit_rows",
    )(*picked)


def finish_kernel(*refs):
    ins, out_ref = refs[:-1], refs[-1]
    total = functools.reduce(jnp.add, [ref[...].astype(jnp.float32) for ref in ins])
    out_ref[...] = total.T


def finish_call(own, others):
    return pl.pallas_call(
        finish_kernel,
        out_shape=jax.ShapeDtypeStruct((own.shape[1], own.shape[0]), jnp.float32),
        in_specs=[whole] * (1 + len(others)),
        out_specs=whole,
        compiler_params=params,
        cost_estimate=light,
        name="feature_sums",
    )(own, *others)


def join_kernel(own_ref, other_ref, out_ref):
    cols = own_ref.shape[1]
    n = lax.axis_index("narrow")
    out_ref[:, pl.ds(pl.multiple_of(n * cols, cols), cols)] = own_ref[...]
    out_ref[:, pl.ds(pl.multiple_of((1 - n) * cols, cols), cols)] = other_ref[...]


def join_call(own, other):
    return pl.pallas_call(
        join_kernel,
        out_shape=jax.ShapeDtypeStruct((own.shape[0], 2 * own.shape[1]), jnp.float32),
        in_specs=[whole] * 2,
        out_specs=whole,
        compiler_params=params,
        cost_estimate=light,
        name="feature_grad",
    )(own, other)


def make(wide, narrow):
    depth = wide // 4
    sizes = (wide, narrow)
    send = functools.partial(exchange, sizes=sizes)

    def to_t(x):
        return send(x, partner=lambda w, n: (w ^ t_bit(n), n))

    def to_s(x):
        return send(x, partner=lambda w, n: (w ^ s_bit(n), n))

    def to_ts(x):
        return send(x, partner=lambda w, n: (w ^ 3, n))

    def to_z(x, k):
        return send(x, partner=lambda w, n: (w ^ (k << 2), n))

    far_first = sorted(range(1, depth), key=lambda k: (k == 1, k))

    def reach(parts, order=far_first):
        return [to_z(parts[k] if isinstance(parts, dict) else parts, k) for k in order]

    def to_core(x, k):
        return send(x, partner=lambda w, n: (w, n ^ k))

    def per_device(features, proxies, sample_ids, positives, loss_weight):
        samples = sample_ids.shape[0]
        rows, width = features.shape
        w = lax.axis_index("wide")
        n = lax.axis_index("narrow")

        if narrow == 2:
            cols = width // 2
            part = jnp.where(n == 0, features[:, :cols], features[:, cols:])
        else:
            part = features
        zs = reach(part, far_first[::-1])
        near = samples // 4
        picked = [
            proxies.at[ids].get(mode="promise_in_bounds", wrap_negative_indices=False)
            for ids in (sample_ids[:near], sample_ids[near:])
        ]
        *zs, picked[0] = lax.optimization_barrier((*zs, picked[0]))
        group_j = stack_call([part] + zs, [0] + far_first[::-1])
        group_s, group_t, picked[1] = lax.optimization_barrier((to_s(group_j), to_t(group_j), picked[1]))
        group_d = to_s(group_t)
        groups = [(group_j,), (group_t,), (group_s,)]
        if narrow == 2:
            others = [to_core(group_j, 1), to_core(group_s, 1), to_core(group_t, 1)]
            groups = [(*group, other) for group, other in zip(groups, others)]

        unit, unit_t = prep_call(picked, 2 if narrow == 2 else 1)
        if narrow != 2:
            unit_t = jnp.take(unit_t.reshape(narrow, width // narrow, samples), n ^ jnp.arange(narrow), axis=0)
            unit_t = unit_t.reshape(width, samples)

        spots = positives.reshape(wide, rows)
        weight = loss_weight.reshape(wide, rows)

        shifted_early, stats_early = logits_call(unit, groups)
        group_d, stats_early = lax.optimization_barrier((group_d, stats_early))
        groups.append((group_d, to_core(group_d, 1)) if narrow == 2 else (group_d,))
        shifted_late, own = logits_call(unit, groups[3:], stats_early)
        stats = own

        def swap_groups(flip, b):
            g, z = divmod(b, depth)
            return ((g % 2) * 2 + g // 2) * depth + z if flip else b

        for bit in range(narrow.bit_length() - 1):
            stats = merge([stats, to_core(stats, 1 << bit)], (0, int(bit == 0)), swap_groups)
        far_last = list(range(depth - 1, 0, -1))
        others = reach(stats, far_last)
        stats = merge([stats] + others, [0] + far_last, lambda k, b: b ^ k)
        others = [to_t(stats), to_s(stats), to_ts(stats)]
        scale = merge([stats] + others, (0, 1, 2, 3), lambda k, b: b ^ (k * depth), own)

        per = depth * rows // chunk
        order_t, order_s, order_j = range(per, 2 * per), range(2 * per, 3 * per), range(per)
        size = depth * rows
        low = jnp.bfloat16
        grad_d, keep_d, send_d = grad_call(
            unit_t, shifted_late, scale, weight, spots, 3 * per, tuple(range(3 * per, 4 * per)), depth
        )
        grad_r, keep_r, send_r = grad_call(
            unit_t, shifted_early, scale, weight, spots, 0, (*order_t, *order_s), depth
        )

        def within(keep, out, names):
            for bit in range(narrow.bit_length() - 2, 0, -1):
                keep = keep + to_core(out, 1 << bit).astype(jnp.float32)
                half = keep.shape[0] // 2
                keep, out = keep[:half], keep[half:].astype(low)
            return [keep, to_core(out, 1)], [names, names.translate(str.maketrans("TS", "ST"))]

        arrays, places = within(keep_d, send_d, "D")
        arrays[1], send_r = lax.optimization_barrier((arrays[1], send_r))
        sum_d, = add_call(arrays, places, "D", size)
        unit_t, sum_d = lax.optimization_barrier((unit_t, sum_d))
        grad_j, keep_j, send_j = grad_call(
            unit_t, shifted_early, scale, weight, spots, 0, tuple(order_j), depth
        )
        from_d = to_s(sum_d)
        arrays, places = within(keep_r, send_r, "TS")
        arrays_j, places_j = within(keep_j, send_j, "J")
        sum_s, = add_call(arrays, places, "S", size)
        from_s = to_s(sum_s)
        from_d, grad_j, _ = lax.optimization_barrier((from_d, grad_j, sum_s))
        sum_t, = add_call([*arrays, from_d], [*places, "T"], "T", size)
        from_t = to_t(sum_t)
        sum_j, = add_call([*arrays_j, from_s], [*places_j, "J"], "J", size, jnp.float32, heavy)
        proxy_grad = proxy_call(
            [grad_d, grad_r, grad_j], [groups[3], groups[1], groups[2], groups[0]], picked
        )
        from_t, proxy_grad, sum_j = lax.optimization_barrier((from_t, proxy_grad, sum_j))
        mine, *others = own_call([sum_j, from_t], "JJ", depth, size)
        mine = finish_call(mine, reach(dict(enumerate(others, 1))))
        if narrow == 2:
            feature_grad = join_call(mine, to_core(mine, 1))
        else:
            mine = mine[None]
            for bit in range(narrow.bit_length() - 1):
                mine = jnp.concatenate([mine, to_core(mine, 1 << bit)], axis=0)
            feature_grad = jnp.take(mine, n ^ jnp.arange(narrow), axis=0).transpose(1, 0, 2).reshape(rows, width)
        return (feature_grad, proxy_grad)

    return per_device


def solution(mesh):
    placed = (P("wide", None), P(("wide", "narrow"), None), P(("wide", "narrow")), P(), P())
    return jax.shard_map(
        make(mesh.shape["wide"], mesh.shape["narrow"]),
        mesh=mesh,
        in_specs=placed,
        out_specs=(P("wide", None), P(("wide", "narrow"), None)),
        check_vma=False,
    )
```

```python
import functools
import math

import jax
import jax.numpy as jnp
from jax import lax
from jax.experimental import pallas as pl
from jax.experimental.pallas import tpu as pltpu
from jax.sharding import PartitionSpec as P

logit_scale = 3.0
epsilon = 1e-06
exp2_scale = logit_scale * math.log2(math.e)
chunk = 256
both = ("wide", "narrow")
whole = pl.BlockSpec(memory_space=pltpu.VMEM)
params = pltpu.CompilerParams(vmem_limit_bytes=8 * 1024 * 1024)
light = pl.CostEstimate(flops=0, bytes_accessed=1 << 19, transcendentals=0)
heavy = pl.CostEstimate(flops=0, bytes_accessed=10 << 20, transcendentals=0)


def t_bit(n):
    return 1 if n % 2 == 0 else 2


def s_bit(n):
    return 3 - t_bit(n)


def exchange(x, sizes, partner):
    wide, narrow = sizes
    pairs = []
    for w in range(wide):
        for n in range(narrow):
            pw, pn = partner(w, n)
            pairs.append((w * narrow + n, pw * narrow + pn))
    return lax.ppermute(x, both, pairs)


def logits_kernel(group_count, part_count, with_early, unit_ref, *refs):
    parts = refs[: group_count * part_count]
    shifted_ref, stats_ref = refs[-2:]
    per = chunk // 128
    first = 0
    if with_early:
        early_ref = refs[group_count * part_count]
        first = early_ref.shape[0] // 2
        half = stats_ref.shape[0] // 2
        stats_ref[0:first, :] = early_ref[0:first, :]
        stats_ref[half:half + first, :] = early_ref[first:, :]
    half = stats_ref.shape[0] // 2
    step = 0
    for g in range(group_count):
        group = parts[g * part_count:(g + 1) * part_count]
        cols = group[0].shape[1]
        for row in range(0, group[0].shape[0], chunk):
            dots = None
            for k, part in enumerate(group):
                prod = lax.dot_general(
                    unit_ref[:, k * cols:(k + 1) * cols], part[row:row + chunk, :],
                    (((1,), (1,)), ((), ())), preferred_element_type=jnp.float32,
                )
                dots = prod if dots is None else dots + prod
            top = jnp.max(dots, axis=0, keepdims=True)
            shifted = jnp.exp2((dots - top) * exp2_scale)
            total = jnp.sum(shifted, axis=0, keepdims=True)
            shifted_ref[:, step * chunk:(step + 1) * chunk] = shifted
            for b in range(per):
                at = first + step * per + b
                stats_ref[at:at + 1, :] = top[:, b * 128:(b + 1) * 128]
                stats_ref[half + at:half + at + 1, :] = total[:, b * 128:(b + 1) * 128]
            step += 1


def logits_call(unit, groups, early=None):
    rows = groups[0][0].shape[0]
    count = len(groups) * rows
    samples = unit.shape[0]
    flat = [part for group in groups for part in group]
    lines = 2 * count // 128
    if early is not None:
        lines += early.shape[0]
        flat.append(early)
    return pl.pallas_call(
        functools.partial(logits_kernel, len(groups), len(groups[0]), early is not None),
        out_shape=(
            jax.ShapeDtypeStruct((samples, count), jnp.float32),
            jax.ShapeDtypeStruct((lines, 128), jnp.float32),
        ),
        in_specs=[whole] * (1 + len(flat)),
        out_specs=(whole, whole),
        compiler_params=params,
        cost_estimate=pl.CostEstimate(
            flops=2 * samples * count * unit.shape[1],
            bytes_accessed=4 * samples * count,
            transcendentals=samples * count,
        ),
        name="logits",
    )(unit, *flat)


def grad_kernel(first, steps, depth, unit_t_ref, shifted_ref, scale_ref, weight_ref, at_ref, grad_ref, keep_ref, send_ref):
    samples = shifted_ref.shape[0]
    half = unit_t_ref.shape[0] // 2
    per = chunk // 128
    w, n = lax.axis_index("wide"), lax.axis_index("narrow")
    base = (w * lax.axis_size("narrow") + n) * samples
    cand = lax.broadcasted_iota(jnp.int32, (samples, chunk), 0) + base

    def row(ref, at):
        return jnp.concatenate([ref[at + b:at + b + 1, :] for b in range(per)], axis=1)

    def far_row(ref, at):
        lines = []
        for b in range(at, at + per):
            g, z = divmod(b, depth)
            offset = jnp.where(n % 2 == 0, 4 * z + g, 4 * z + (g % 2) * 2 + g // 2)
            lines.append(ref[pl.ds(jnp.bitwise_xor(w, offset), 1), :])
        return jnp.concatenate(lines, axis=1)

    for out, at in enumerate(steps):
        cols = slice((at - first) * chunk, (at - first + 1) * chunk)
        scale, weight, spot = row(scale_ref, at * per), far_row(weight_ref, at * per), far_row(at_ref, at * per)
        soft = shifted_ref[:, cols] * scale
        grad = (weight * jnp.where(cand == spot, soft - 1.0, soft)).astype(jnp.bfloat16)
        out_cols = slice(out * chunk, (out + 1) * chunk)
        grad_ref[:, out_cols] = grad
        shares = logit_scale * jnp.dot(unit_t_ref[...], grad, preferred_element_type=jnp.float32)
        keep_ref[:, out_cols] = shares[:half]
        send_ref[:, out_cols] = shares[half:].astype(jnp.bfloat16)


def grad_call(unit_t, shifted, scale, weight, spots, first, steps, depth):
    samples = shifted.shape[0]
    width = unit_t.shape[0]
    count = len(steps) * chunk
    return pl.pallas_call(
        functools.partial(grad_kernel, first, steps, depth),
        out_shape=(
            jax.ShapeDtypeStruct((samples, count), jnp.bfloat16),
            jax.ShapeDtypeStruct((width // 2, count), jnp.float32),
            jax.ShapeDtypeStruct((width // 2, count), jnp.bfloat16),
        ),
        in_specs=[whole] * 5,
        out_specs=(whole,) * 3,
        compiler_params=params,
        cost_estimate=pl.CostEstimate(
            flops=2 * samples * count * width, bytes_accessed=6 * samples * count, transcendentals=0
        ),
        name="grads",
    )(unit_t, shifted, scale, weight, spots)


def proxy_kernel(grad_count, group_count, part_count, rows, *refs):
    grad_refs, refs = refs[:grad_count], refs[grad_count:]
    parts = refs[:group_count * part_count]
    *picked_refs, out_ref = refs[group_count * part_count:]
    size, cols = parts[0].shape
    grads = [ref.at[:, at:at + size] for ref in grad_refs for at in range(0, ref.shape[1], size)]
    n = lax.axis_index("narrow")
    places = []
    for k in range(part_count):
        if part_count == 1:
            places.append(slice(0, cols))
        else:
            places.append(pl.ds(pl.multiple_of((n ^ k) * cols, cols), cols))
    tiles = [(ref, row) for ref in picked_refs for row in range(0, ref.shape[0], rows)]
    for tile, (picked_ref, row) in enumerate(tiles):
        at, here = slice(tile * rows, (tile + 1) * rows), slice(row, row + rows)
        sums = []
        for k in range(part_count):
            total = None
            for g in range(group_count):
                prod = jnp.dot(
                    grads[g][at, :], parts[g * part_count + k][...], preferred_element_type=jnp.float32
                )
                total = prod if total is None else total + prod
            sums.append(logit_scale * total)
        picked = [picked_ref[here, place] for place in places]
        square = functools.reduce(jnp.add, [jnp.sum(p * p, axis=1, keepdims=True) for p in picked])
        inverse = 1.0 / jnp.sqrt(square + epsilon)
        inner = functools.reduce(jnp.add, [jnp.sum(p * s, axis=1, keepdims=True) for p, s in zip(picked, sums)])
        slope = inner * inverse * inverse
        for place, p, s in zip(places, picked, sums):
            out_ref[at, place] = (s - p * slope) * inverse


def proxy_call(grads, groups, picked):
    samples, width = grads[0].shape[0], picked[0].shape[1]
    count = sum(grad.shape[1] for grad in grads)
    flat = [part for group in groups for part in group]
    return pl.pallas_call(
        functools.partial(proxy_kernel, len(grads), len(groups), len(groups[0]), 256),
        out_shape=jax.ShapeDtypeStruct((samples, width), jnp.float32),
        in_specs=[whole] * (len(grads) + len(flat) + len(picked)),
        out_specs=whole,
        compiler_params=params,
        cost_estimate=pl.CostEstimate(
            flops=2 * samples * count * width, bytes_accessed=4 * samples * count, transcendentals=0
        ),
        name="proxy_grads",
    )(*grads, *flat, *picked)


def merge_kernel(flips, swap, with_scale, *refs):
    ins, out_ref = refs[:-1], refs[-1]
    if with_scale:
        own_ref, ins = ins[-1], ins[:-1]
    blocks = ins[0].shape[0] // 2
    for b in range(blocks):
        spots = [swap(f, b) for f in flips]
        tops = [ref[at:at + 1, :] for ref, at in zip(ins, spots)]
        totals = [ref[blocks + at:blocks + at + 1, :] for ref, at in zip(ins, spots)]
        top = functools.reduce(jnp.maximum, tops)
        total = functools.reduce(
            jnp.add, [t * jnp.exp2((m - top) * exp2_scale) for m, t in zip(tops, totals)]
        )
        if with_scale:
            out_ref[b:b + 1, :] = jnp.exp2((own_ref[b:b + 1, :] - top) * exp2_scale) / total
        else:
            out_ref[b:b + 1, :] = top
            out_ref[blocks + b:blocks + b + 1, :] = total


def merge(stats, flips, swap, own=None):
    lines = stats[0].shape[0]
    if own is not None:
        stats, lines = [*stats, own], lines // 2
    return pl.pallas_call(
        functools.partial(merge_kernel, flips, swap, own is not None),
        out_shape=jax.ShapeDtypeStruct((lines, 128), jnp.float32),
        in_specs=[whole] * len(stats),
        out_specs=whole,
        compiler_params=params,
        cost_estimate=light,
        name="merge_stats",
    )(*stats)


def stack_kernel(places, *refs):
    rows = refs[0].shape[0]
    for k, ref in zip(places, refs):
        refs[-1][k * rows:(k + 1) * rows, :] = ref[...]


def stack_call(parts, places):
    rows, cols = parts[0].shape
    return pl.pallas_call(
        functools.partial(stack_kernel, places),
        out_shape=jax.ShapeDtypeStruct((len(parts) * rows, cols), parts[0].dtype),
        in_specs=[whole] * len(parts),
        out_specs=whole,
        compiler_params=params,
        cost_estimate=light,
        name="stack_blocks",
    )(*parts)


def add_kernel(ins, outs, size, *refs):
    for name, out_ref in zip(outs, refs[len(ins):]):
        total = None
        for places, ref in zip(ins, refs):
            if name in places:
                at = places.index(name)
                term = ref[:, at * size:(at + 1) * size].astype(jnp.float32)
                total = term if total is None else total + term
        out_ref[...] = total.astype(out_ref.dtype)


def add_call(arrays, ins, outs, size, dtype=jnp.bfloat16, cost=light):
    rows = arrays[0].shape[0]
    result = pl.pallas_call(
        functools.partial(add_kernel, ins, outs, size),
        out_shape=[jax.ShapeDtypeStruct((rows, size), dtype) for _ in outs],
        in_specs=[whole] * len(arrays),
        out_specs=[whole] * len(outs),
        compiler_params=params,
        cost_estimate=cost,
        name="add_shares",
    )(*arrays)
    return result


def own_kernel(ins, count, size, *refs):
    cols = size // count
    for k, out_ref in enumerate(refs[len(ins):]):
        total = None
        for places, ref in zip(ins, refs):
            at = places.index("J") * size + k * cols
            term = ref[:, at:at + cols].astype(jnp.float32)
            total = term if total is None else total + term
        out_ref[...] = total.astype(out_ref.dtype)


def own_call(arrays, ins, count, size):
    rows = arrays[0].shape[0]
    return pl.pallas_call(
        functools.partial(own_kernel, ins, count, size),
        out_shape=[
            jax.ShapeDtypeStruct((rows, size // count), jnp.bfloat16 if k else jnp.float32) for k in range(count)
        ],
        in_specs=[whole] * len(arrays),
        out_specs=[whole] * count,
        compiler_params=params,
        cost_estimate=light,
        name="add_shares_z",
    )(*arrays)


def prep_kernel(part_count, *refs):
    *picked_refs, unit_ref, unit_t_ref = refs
    width = picked_refs[0].shape[1]
    cols = width // part_count
    tiles = [(ref, row) for ref in picked_refs for row in range(0, ref.shape[0], 256)]
    n = lax.axis_index("narrow")
    for line, (picked_ref, row) in enumerate(tiles):
        line *= 256
        at = slice(row, row + 256)
        if part_count == 1:
            picked = picked_ref[at, :]
        else:
            picked = jnp.concatenate(
                [picked_ref[at, pl.ds(pl.multiple_of((n ^ k) * cols, cols), cols)] for k in range(part_count)],
                axis=1,
            )
        lengths = jnp.sqrt(jnp.sum(picked * picked, axis=1, keepdims=True) + epsilon)
        unit = picked / lengths
        unit_ref[line:line + 256, :] = unit.astype(jnp.bfloat16)
        unit_t_ref[:, line:line + 256] = unit.T.astype(jnp.bfloat16)


def prep_call(picked, part_count):
    samples, width = sum(p.shape[0] for p in picked), picked[0].shape[1]
    return pl.pallas_call(
        functools.partial(prep_kernel, part_count),
        out_shape=(
            jax.ShapeDtypeStruct((samples, width), jnp.bfloat16),
            jax.ShapeDtypeStruct((width, samples), jnp.bfloat16),
        ),
        in_specs=[whole] * len(picked),
        out_specs=(whole, whole),
        compiler_params=params,
        cost_estimate=pl.CostEstimate(flops=4 * samples * width, bytes_accessed=8 * samples * width, transcendentals=0),
        name="unit_rows",
    )(*picked)


def finish_kernel(*refs):
    ins, out_ref = refs[:-1], refs[-1]
    total = functools.reduce(jnp.add, [ref[...].astype(jnp.float32) for ref in ins])
    out_ref[...] = total.T


def finish_call(own, others):
    return pl.pallas_call(
        finish_kernel,
        out_shape=jax.ShapeDtypeStruct((own.shape[1], own.shape[0]), jnp.float32),
        in_specs=[whole] * (1 + len(others)),
        out_specs=whole,
        compiler_params=params,
        cost_estimate=light,
        name="feature_sums",
    )(own, *others)


def join_kernel(own_ref, other_ref, out_ref):
    cols = own_ref.shape[1]
    n = lax.axis_index("narrow")
    out_ref[:, pl.ds(pl.multiple_of(n * cols, cols), cols)] = own_ref[...]
    out_ref[:, pl.ds(pl.multiple_of((1 - n) * cols, cols), cols)] = other_ref[...]


def join_call(own, other):
    return pl.pallas_call(
        join_kernel,
        out_shape=jax.ShapeDtypeStruct((own.shape[0], 2 * own.shape[1]), jnp.float32),
        in_specs=[whole] * 2,
        out_specs=whole,
        compiler_params=params,
        cost_estimate=light,
        name="feature_grad",
    )(own, other)


def make(wide, narrow):
    depth = wide // 4
    sizes = (wide, narrow)
    send = functools.partial(exchange, sizes=sizes)

    def to_t(x):
        return send(x, partner=lambda w, n: (w ^ t_bit(n), n))

    def to_s(x):
        return send(x, partner=lambda w, n: (w ^ s_bit(n), n))

    def to_ts(x):
        return send(x, partner=lambda w, n: (w ^ 3, n))

    def to_z(x, k):
        return send(x, partner=lambda w, n: (w ^ (k << 2), n))

    far_first = sorted(range(1, depth), key=lambda k: (k == 1, k))

    def reach(parts, order=far_first):
        return [to_z(parts[k] if isinstance(parts, dict) else parts, k) for k in order]

    def to_core(x, k):
        return send(x, partner=lambda w, n: (w, n ^ k))

    def per_device(features, proxies, sample_ids, positives, loss_weight):
        samples = sample_ids.shape[0]
        rows, width = features.shape
        w = lax.axis_index("wide")
        n = lax.axis_index("narrow")

        if narrow == 2:
            cols = width // 2
            part = jnp.where(n == 0, features[:, :cols], features[:, cols:])
        else:
            part = features
        zs = reach(part)
        near = samples // 4
        picked = [
            proxies.at[ids].get(mode="promise_in_bounds", wrap_negative_indices=False)
            for ids in (sample_ids[:near], sample_ids[near:])
        ]
        *zs, picked[0] = lax.optimization_barrier((*zs, picked[0]))
        group_j = stack_call([part] + zs, [0] + far_first)
        group_t, group_s, picked[1] = lax.optimization_barrier((to_t(group_j), to_s(group_j), picked[1]))
        group_d = to_s(group_t)
        groups = [(group_j,), (group_t,), (group_s,)]
        if narrow == 2:
            others = [to_core(group_j, 1), to_core(group_s, 1), to_core(group_t, 1)]
            groups = [(*group, other) for group, other in zip(groups, others)]

        unit, unit_t = prep_call(picked, 2 if narrow == 2 else 1)
        if narrow != 2:
            unit_t = jnp.take(unit_t.reshape(narrow, width // narrow, samples), n ^ jnp.arange(narrow), axis=0)
            unit_t = unit_t.reshape(width, samples)

        spots = positives.reshape(wide, rows)
        weight = loss_weight.reshape(wide, rows)

        shifted_early, stats_early = logits_call(unit, groups)
        group_d, stats_early = lax.optimization_barrier((group_d, stats_early))
        groups.append((group_d, to_core(group_d, 1)) if narrow == 2 else (group_d,))
        shifted_late, own = logits_call(unit, groups[3:], stats_early)
        stats = own

        def swap_groups(flip, b):
            g, z = divmod(b, depth)
            return ((g % 2) * 2 + g // 2) * depth + z if flip else b

        for bit in range(narrow.bit_length() - 1):
            stats = merge([stats, to_core(stats, 1 << bit)], (0, int(bit == 0)), swap_groups)
        others = reach(stats)
        stats = merge([stats] + others, [0] + far_first, lambda k, b: b ^ k)
        others = [to_t(stats), to_s(stats), to_ts(stats)]
        scale = merge([stats] + others, (0, 1, 2, 3), lambda k, b: b ^ (k * depth), own)

        per = depth * rows // chunk
        order_t, order_s, order_j = range(per, 2 * per), range(2 * per, 3 * per), range(per)
        size = depth * rows
        low = jnp.bfloat16
        grad_d, keep_d, send_d = grad_call(
            unit_t, shifted_late, scale, weight, spots, 3 * per, tuple(range(3 * per, 4 * per)), depth
        )
        grad_r, keep_r, send_r = grad_call(
            unit_t, shifted_early, scale, weight, spots, 0, (*order_t, *order_s), depth
        )

        def within(keep, out, names):
            for bit in range(narrow.bit_length() - 2, 0, -1):
                keep = keep + to_core(out, 1 << bit).astype(jnp.float32)
                half = keep.shape[0] // 2
                keep, out = keep[:half], keep[half:].astype(low)
            return [keep, to_core(out, 1)], [names, names.translate(str.maketrans("TS", "ST"))]

        arrays, places = within(keep_d, send_d, "D")
        arrays[1], send_r = lax.optimization_barrier((arrays[1], send_r))
        sum_d, = add_call(arrays, places, "D", size)
        unit_t, sum_d = lax.optimization_barrier((unit_t, sum_d))
        grad_j, keep_j, send_j = grad_call(
            unit_t, shifted_early, scale, weight, spots, 0, tuple(order_j), depth
        )
        from_d = to_s(sum_d)
        arrays, places = within(keep_r, send_r, "TS")
        arrays_j, places_j = within(keep_j, send_j, "J")
        sum_s, = add_call(arrays, places, "S", size)
        from_s = to_s(sum_s)
        from_d, grad_j, _ = lax.optimization_barrier((from_d, grad_j, sum_s))
        sum_t, = add_call([*arrays, from_d], [*places, "T"], "T", size)
        from_t = to_t(sum_t)
        sum_j, = add_call([*arrays_j, from_s], [*places_j, "J"], "J", size, jnp.float32, heavy)
        proxy_grad = proxy_call(
            [grad_d, grad_r, grad_j], [groups[3], groups[1], groups[2], groups[0]], picked
        )
        from_t, proxy_grad, sum_j = lax.optimization_barrier((from_t, proxy_grad, sum_j))
        mine, *others = own_call([sum_j, from_t], "JJ", depth, size)
        mine = finish_call(mine, reach(dict(enumerate(others, 1))))
        if narrow == 2:
            feature_grad = join_call(mine, to_core(mine, 1))
        else:
            mine = mine[None]
            for bit in range(narrow.bit_length() - 1):
                mine = jnp.concatenate([mine, to_core(mine, 1 << bit)], axis=0)
            feature_grad = jnp.take(mine, n ^ jnp.arange(narrow), axis=0).transpose(1, 0, 2).reshape(rows, width)
        return (feature_grad, proxy_grad)

    return per_device


def solution(mesh):
    placed = (P("wide", None), P(("wide", "narrow"), None), P(("wide", "narrow")), P(), P())
    return jax.shard_map(
        make(mesh.shape["wide"], mesh.shape["narrow"]),
        mesh=mesh,
        in_specs=placed,
        out_specs=(P("wide", None), P(("wide", "narrow"), None)),
        check_vma=False,
    )
```

```python
import functools
import math

import jax
import jax.numpy as jnp
from jax import lax
from jax.experimental import pallas as pl
from jax.experimental.pallas import tpu as pltpu
from jax.sharding import PartitionSpec as P

logit_scale = 3.0
epsilon = 1e-06
exp2_scale = logit_scale * math.log2(math.e)
chunk = 256
both = ("wide", "narrow")
whole = pl.BlockSpec(memory_space=pltpu.VMEM)
params = pltpu.CompilerParams(vmem_limit_bytes=8 * 1024 * 1024)
light = pl.CostEstimate(flops=0, bytes_accessed=1 << 19, transcendentals=0)
heavy = pl.CostEstimate(flops=0, bytes_accessed=10 << 20, transcendentals=0)


def t_bit(n):
    return 1 if n % 2 == 0 else 2


def s_bit(n):
    return 3 - t_bit(n)


def exchange(x, sizes, partner):
    wide, narrow = sizes
    pairs = []
    for w in range(wide):
        for n in range(narrow):
            pw, pn = partner(w, n)
            pairs.append((w * narrow + n, pw * narrow + pn))
    return lax.ppermute(x, both, pairs)


def logits_kernel(group_count, part_count, with_early, unit_ref, *refs):
    parts = refs[: group_count * part_count]
    shifted_ref, stats_ref = refs[-2:]
    per = chunk // 128
    first = 0
    if with_early:
        early_ref = refs[group_count * part_count]
        first = early_ref.shape[0] // 2
        half = stats_ref.shape[0] // 2
        stats_ref[0:first, :] = early_ref[0:first, :]
        stats_ref[half:half + first, :] = early_ref[first:, :]
    half = stats_ref.shape[0] // 2
    step = 0
    for g in range(group_count):
        group = parts[g * part_count:(g + 1) * part_count]
        cols = group[0].shape[1]
        for row in range(0, group[0].shape[0], chunk):
            dots = None
            for k, part in enumerate(group):
                prod = lax.dot_general(
                    unit_ref[:, k * cols:(k + 1) * cols], part[row:row + chunk, :],
                    (((1,), (1,)), ((), ())), preferred_element_type=jnp.float32,
                )
                dots = prod if dots is None else dots + prod
            top = jnp.max(dots, axis=0, keepdims=True)
            shifted = jnp.exp2((dots - top) * exp2_scale)
            total = jnp.sum(shifted, axis=0, keepdims=True)
            shifted_ref[:, step * chunk:(step + 1) * chunk] = shifted
            for b in range(per):
                at = first + step * per + b
                stats_ref[at:at + 1, :] = top[:, b * 128:(b + 1) * 128]
                stats_ref[half + at:half + at + 1, :] = total[:, b * 128:(b + 1) * 128]
            step += 1


def logits_call(unit, groups, early=None):
    rows = groups[0][0].shape[0]
    count = len(groups) * rows
    samples = unit.shape[0]
    flat = [part for group in groups for part in group]
    lines = 2 * count // 128
    if early is not None:
        lines += early.shape[0]
        flat.append(early)
    return pl.pallas_call(
        functools.partial(logits_kernel, len(groups), len(groups[0]), early is not None),
        out_shape=(
            jax.ShapeDtypeStruct((samples, count), jnp.float32),
            jax.ShapeDtypeStruct((lines, 128), jnp.float32),
        ),
        in_specs=[whole] * (1 + len(flat)),
        out_specs=(whole, whole),
        compiler_params=params,
        cost_estimate=pl.CostEstimate(
            flops=2 * samples * count * unit.shape[1],
            bytes_accessed=4 * samples * count,
            transcendentals=samples * count,
        ),
        name="logits",
    )(unit, *flat)


def grad_kernel(first, steps, depth, unit_t_ref, shifted_ref, scale_ref, weight_ref, at_ref, grad_ref, keep_ref, send_ref):
    samples = shifted_ref.shape[0]
    half = unit_t_ref.shape[0] // 2
    per = chunk // 128
    w, n = lax.axis_index("wide"), lax.axis_index("narrow")
    base = (w * lax.axis_size("narrow") + n) * samples
    cand = lax.broadcasted_iota(jnp.int32, (samples, chunk), 0) + base

    def row(ref, at):
        return jnp.concatenate([ref[at + b:at + b + 1, :] for b in range(per)], axis=1)

    def far_row(ref, at):
        lines = []
        for b in range(at, at + per):
            g, z = divmod(b, depth)
            offset = jnp.where(n % 2 == 0, 4 * z + g, 4 * z + (g % 2) * 2 + g // 2)
            lines.append(ref[pl.ds(jnp.bitwise_xor(w, offset), 1), :])
        return jnp.concatenate(lines, axis=1)

    for out, at in enumerate(steps):
        cols = slice((at - first) * chunk, (at - first + 1) * chunk)
        scale, weight, spot = row(scale_ref, at * per), far_row(weight_ref, at * per), far_row(at_ref, at * per)
        soft = shifted_ref[:, cols] * scale
        grad = (weight * jnp.where(cand == spot, soft - 1.0, soft)).astype(jnp.bfloat16)
        out_cols = slice(out * chunk, (out + 1) * chunk)
        grad_ref[:, out_cols] = grad
        shares = logit_scale * jnp.dot(unit_t_ref[...], grad, preferred_element_type=jnp.float32)
        keep_ref[:, out_cols] = shares[:half]
        send_ref[:, out_cols] = shares[half:].astype(jnp.bfloat16)


def grad_call(unit_t, shifted, scale, weight, spots, first, steps, depth):
    samples = shifted.shape[0]
    width = unit_t.shape[0]
    count = len(steps) * chunk
    return pl.pallas_call(
        functools.partial(grad_kernel, first, steps, depth),
        out_shape=(
            jax.ShapeDtypeStruct((samples, count), jnp.bfloat16),
            jax.ShapeDtypeStruct((width // 2, count), jnp.float32),
            jax.ShapeDtypeStruct((width // 2, count), jnp.bfloat16),
        ),
        in_specs=[whole] * 5,
        out_specs=(whole,) * 3,
        compiler_params=params,
        cost_estimate=pl.CostEstimate(
            flops=2 * samples * count * width, bytes_accessed=6 * samples * count, transcendentals=0
        ),
        name="grads",
    )(unit_t, shifted, scale, weight, spots)


def proxy_kernel(grad_count, group_count, part_count, rows, *refs):
    grad_refs, refs = refs[:grad_count], refs[grad_count:]
    parts = refs[:group_count * part_count]
    *picked_refs, out_ref = refs[group_count * part_count:]
    size, cols = parts[0].shape
    grads = [ref.at[:, at:at + size] for ref in grad_refs for at in range(0, ref.shape[1], size)]
    n = lax.axis_index("narrow")
    places = []
    for k in range(part_count):
        if part_count == 1:
            places.append(slice(0, cols))
        else:
            places.append(pl.ds(pl.multiple_of((n ^ k) * cols, cols), cols))
    tiles = [(ref, row) for ref in picked_refs for row in range(0, ref.shape[0], rows)]
    for tile, (picked_ref, row) in enumerate(tiles):
        at, here = slice(tile * rows, (tile + 1) * rows), slice(row, row + rows)
        sums = []
        for k in range(part_count):
            total = None
            for g in range(group_count):
                prod = jnp.dot(
                    grads[g][at, :], parts[g * part_count + k][...], preferred_element_type=jnp.float32
                )
                total = prod if total is None else total + prod
            sums.append(logit_scale * total)
        picked = [picked_ref[here, place] for place in places]
        square = functools.reduce(jnp.add, [jnp.sum(p * p, axis=1, keepdims=True) for p in picked])
        inverse = 1.0 / jnp.sqrt(square + epsilon)
        inner = functools.reduce(jnp.add, [jnp.sum(p * s, axis=1, keepdims=True) for p, s in zip(picked, sums)])
        slope = inner * inverse * inverse
        for place, p, s in zip(places, picked, sums):
            out_ref[at, place] = (s - p * slope) * inverse


def proxy_call(grads, groups, picked):
    samples, width = grads[0].shape[0], picked[0].shape[1]
    count = sum(grad.shape[1] for grad in grads)
    flat = [part for group in groups for part in group]
    return pl.pallas_call(
        functools.partial(proxy_kernel, len(grads), len(groups), len(groups[0]), 256),
        out_shape=jax.ShapeDtypeStruct((samples, width), jnp.float32),
        in_specs=[whole] * (len(grads) + len(flat) + len(picked)),
        out_specs=whole,
        compiler_params=params,
        cost_estimate=pl.CostEstimate(
            flops=2 * samples * count * width, bytes_accessed=4 * samples * count, transcendentals=0
        ),
        name="proxy_grads",
    )(*grads, *flat, *picked)


def merge_kernel(flips, swap, with_scale, *refs):
    ins, out_ref = refs[:-1], refs[-1]
    if with_scale:
        own_ref, ins = ins[-1], ins[:-1]
    blocks = ins[0].shape[0] // 2
    for b in range(blocks):
        spots = [swap(f, b) for f in flips]
        tops = [ref[at:at + 1, :] for ref, at in zip(ins, spots)]
        totals = [ref[blocks + at:blocks + at + 1, :] for ref, at in zip(ins, spots)]
        top = functools.reduce(jnp.maximum, tops)
        total = functools.reduce(
            jnp.add, [t * jnp.exp2((m - top) * exp2_scale) for m, t in zip(tops, totals)]
        )
        if with_scale:
            out_ref[b:b + 1, :] = jnp.exp2((own_ref[b:b + 1, :] - top) * exp2_scale) / total
        else:
            out_ref[b:b + 1, :] = top
            out_ref[blocks + b:blocks + b + 1, :] = total


def merge(stats, flips, swap, own=None):
    lines = stats[0].shape[0]
    if own is not None:
        stats, lines = [*stats, own], lines // 2
    return pl.pallas_call(
        functools.partial(merge_kernel, flips, swap, own is not None),
        out_shape=jax.ShapeDtypeStruct((lines, 128), jnp.float32),
        in_specs=[whole] * len(stats),
        out_specs=whole,
        compiler_params=params,
        cost_estimate=light,
        name="merge_stats",
    )(*stats)


def stack_kernel(places, *refs):
    rows = refs[0].shape[0]
    for k, ref in zip(places, refs):
        refs[-1][k * rows:(k + 1) * rows, :] = ref[...]


def stack_call(parts, places):
    rows, cols = parts[0].shape
    return pl.pallas_call(
        functools.partial(stack_kernel, places),
        out_shape=jax.ShapeDtypeStruct((len(parts) * rows, cols), parts[0].dtype),
        in_specs=[whole] * len(parts),
        out_specs=whole,
        compiler_params=params,
        cost_estimate=light,
        name="stack_blocks",
    )(*parts)


def add_kernel(ins, outs, size, *refs):
    for name, out_ref in zip(outs, refs[len(ins):]):
        total = None
        for places, ref in zip(ins, refs):
            if name in places:
                at = places.index(name)
                term = ref[:, at * size:(at + 1) * size].astype(jnp.float32)
                total = term if total is None else total + term
        out_ref[...] = total.astype(out_ref.dtype)


def add_call(arrays, ins, outs, size, dtype=jnp.bfloat16, cost=light):
    rows = arrays[0].shape[0]
    result = pl.pallas_call(
        functools.partial(add_kernel, ins, outs, size),
        out_shape=[jax.ShapeDtypeStruct((rows, size), dtype) for _ in outs],
        in_specs=[whole] * len(arrays),
        out_specs=[whole] * len(outs),
        compiler_params=params,
        cost_estimate=cost,
        name="add_shares",
    )(*arrays)
    return result


def own_kernel(ins, count, size, *refs):
    cols = size // count
    for k, out_ref in enumerate(refs[len(ins):]):
        total = None
        for places, ref in zip(ins, refs):
            at = places.index("J") * size + k * cols
            term = ref[:, at:at + cols].astype(jnp.float32)
            total = term if total is None else total + term
        out_ref[...] = total.astype(out_ref.dtype)


def own_call(arrays, ins, count, size):
    rows = arrays[0].shape[0]
    return pl.pallas_call(
        functools.partial(own_kernel, ins, count, size),
        out_shape=[
            jax.ShapeDtypeStruct((rows, size // count), jnp.bfloat16 if k else jnp.float32) for k in range(count)
        ],
        in_specs=[whole] * len(arrays),
        out_specs=[whole] * count,
        compiler_params=params,
        cost_estimate=light,
        name="add_shares_z",
    )(*arrays)


def prep_kernel(part_count, *refs):
    *picked_refs, unit_ref, unit_t_ref = refs
    width = picked_refs[0].shape[1]
    cols = width // part_count
    tiles = [(ref, row) for ref in picked_refs for row in range(0, ref.shape[0], 256)]
    n = lax.axis_index("narrow")
    for line, (picked_ref, row) in enumerate(tiles):
        line *= 256
        at = slice(row, row + 256)
        if part_count == 1:
            picked = picked_ref[at, :]
        else:
            picked = jnp.concatenate(
                [picked_ref[at, pl.ds(pl.multiple_of((n ^ k) * cols, cols), cols)] for k in range(part_count)],
                axis=1,
            )
        lengths = jnp.sqrt(jnp.sum(picked * picked, axis=1, keepdims=True) + epsilon)
        unit = picked / lengths
        unit_ref[line:line + 256, :] = unit.astype(jnp.bfloat16)
        unit_t_ref[:, line:line + 256] = unit.T.astype(jnp.bfloat16)


def prep_call(picked, part_count):
    samples, width = sum(p.shape[0] for p in picked), picked[0].shape[1]
    return pl.pallas_call(
        functools.partial(prep_kernel, part_count),
        out_shape=(
            jax.ShapeDtypeStruct((samples, width), jnp.bfloat16),
            jax.ShapeDtypeStruct((width, samples), jnp.bfloat16),
        ),
        in_specs=[whole] * len(picked),
        out_specs=(whole, whole),
        compiler_params=params,
        cost_estimate=pl.CostEstimate(flops=4 * samples * width, bytes_accessed=8 * samples * width, transcendentals=0),
        name="unit_rows",
    )(*picked)


def finish_kernel(*refs):
    ins, out_ref = refs[:-1], refs[-1]
    total = functools.reduce(jnp.add, [ref[...].astype(jnp.float32) for ref in ins])
    out_ref[...] = total.T


def finish_call(own, others):
    return pl.pallas_call(
        finish_kernel,
        out_shape=jax.ShapeDtypeStruct((own.shape[1], own.shape[0]), jnp.float32),
        in_specs=[whole] * (1 + len(others)),
        out_specs=whole,
        compiler_params=params,
        cost_estimate=light,
        name="feature_sums",
    )(own, *others)


def join_kernel(own_ref, other_ref, out_ref):
    cols = own_ref.shape[1]
    n = lax.axis_index("narrow")
    out_ref[:, pl.ds(pl.multiple_of(n * cols, cols), cols)] = own_ref[...]
    out_ref[:, pl.ds(pl.multiple_of((1 - n) * cols, cols), cols)] = other_ref[...]


def join_call(own, other):
    return pl.pallas_call(
        join_kernel,
        out_shape=jax.ShapeDtypeStruct((own.shape[0], 2 * own.shape[1]), jnp.float32),
        in_specs=[whole] * 2,
        out_specs=whole,
        compiler_params=params,
        cost_estimate=light,
        name="feature_grad",
    )(own, other)


def make(wide, narrow):
    depth = wide // 4
    sizes = (wide, narrow)
    send = functools.partial(exchange, sizes=sizes)

    def to_t(x):
        return send(x, partner=lambda w, n: (w ^ t_bit(n), n))

    def to_s(x):
        return send(x, partner=lambda w, n: (w ^ s_bit(n), n))

    def to_ts(x):
        return send(x, partner=lambda w, n: (w ^ 3, n))

    def to_z(x, k):
        return send(x, partner=lambda w, n: (w ^ (k << 2), n))

    far_first = sorted(range(1, depth), key=lambda k: (k == 1, k))

    def reach(parts, order=far_first):
        return [to_z(parts[k] if isinstance(parts, dict) else parts, k) for k in order]

    def to_core(x, k):
        return send(x, partner=lambda w, n: (w, n ^ k))

    def per_device(features, proxies, sample_ids, positives, loss_weight):
        samples = sample_ids.shape[0]
        rows, width = features.shape
        w = lax.axis_index("wide")
        n = lax.axis_index("narrow")

        if narrow == 2:
            cols = width // 2
            part = jnp.where(n == 0, features[:, :cols], features[:, cols:])
        else:
            part = features
        zs = reach(part, far_first[::-1])
        near = samples // 4
        picked = [
            proxies.at[ids].get(mode="promise_in_bounds", wrap_negative_indices=False)
            for ids in (sample_ids[:near], sample_ids[near:])
        ]
        *zs, picked[0] = lax.optimization_barrier((*zs, picked[0]))
        group_j = stack_call([part] + zs, [0] + far_first[::-1])
        group_t, group_s, picked[1] = lax.optimization_barrier((to_t(group_j), to_s(group_j), picked[1]))
        group_d = to_s(group_t)
        groups = [(group_j,), (group_t,), (group_s,)]
        if narrow == 2:
            others = [to_core(group_j, 1), to_core(group_s, 1), to_core(group_t, 1)]
            groups = [(*group, other) for group, other in zip(groups, others)]

        unit, unit_t = prep_call(picked, 2 if narrow == 2 else 1)
        if narrow != 2:
            unit_t = jnp.take(unit_t.reshape(narrow, width // narrow, samples), n ^ jnp.arange(narrow), axis=0)
            unit_t = unit_t.reshape(width, samples)

        spots = positives.reshape(wide, rows)
        weight = loss_weight.reshape(wide, rows)

        shifted_early, stats_early = logits_call(unit, groups)
        group_d, stats_early = lax.optimization_barrier((group_d, stats_early))
        groups.append((group_d, to_core(group_d, 1)) if narrow == 2 else (group_d,))
        shifted_late, own = logits_call(unit, groups[3:], stats_early)
        stats = own

        def swap_groups(flip, b):
            g, z = divmod(b, depth)
            return ((g % 2) * 2 + g // 2) * depth + z if flip else b

        for bit in range(narrow.bit_length() - 1):
            stats = merge([stats, to_core(stats, 1 << bit)], (0, int(bit == 0)), swap_groups)
        others = reach(stats)
        stats = merge([stats] + others, [0] + far_first, lambda k, b: b ^ k)
        others = [to_t(stats), to_s(stats), to_ts(stats)]
        scale = merge([stats] + others, (0, 1, 2, 3), lambda k, b: b ^ (k * depth), own)

        per = depth * rows // chunk
        order_t, order_s, order_j = range(per, 2 * per), range(2 * per, 3 * per), range(per)
        size = depth * rows
        low = jnp.bfloat16
        grad_d, keep_d, send_d = grad_call(
            unit_t, shifted_late, scale, weight, spots, 3 * per, tuple(range(3 * per, 4 * per)), depth
        )
        grad_r, keep_r, send_r = grad_call(
            unit_t, shifted_early, scale, weight, spots, 0, (*order_t, *order_s), depth
        )

        def within(keep, out, names):
            for bit in range(narrow.bit_length() - 2, 0, -1):
                keep = keep + to_core(out, 1 << bit).astype(jnp.float32)
                half = keep.shape[0] // 2
                keep, out = keep[:half], keep[half:].astype(low)
            return [keep, to_core(out, 1)], [names, names.translate(str.maketrans("TS", "ST"))]

        arrays, places = within(keep_d, send_d, "D")
        arrays[1], send_r = lax.optimization_barrier((arrays[1], send_r))
        sum_d, = add_call(arrays, places, "D", size)
        unit_t, sum_d = lax.optimization_barrier((unit_t, sum_d))
        grad_j, keep_j, send_j = grad_call(
            unit_t, shifted_early, scale, weight, spots, 0, tuple(order_j), depth
        )
        from_d = to_s(sum_d)
        arrays, places = within(keep_r, send_r, "TS")
        arrays_j, places_j = within(keep_j, send_j, "J")
        sum_s, = add_call(arrays, places, "S", size)
        from_s = to_s(sum_s)
        from_d, grad_j, _ = lax.optimization_barrier((from_d, grad_j, sum_s))
        sum_t, = add_call([*arrays, from_d], [*places, "T"], "T", size)
        from_t = to_t(sum_t)
        sum_j, = add_call([*arrays_j, from_s], [*places_j, "J"], "J", size, jnp.float32, heavy)
        mine, *others = own_call([sum_j, from_t], "JJ", depth, size)
        others = reach(dict(enumerate(others, 1)))
        proxy_grad = proxy_call(
            [grad_d, grad_r, grad_j], [groups[3], groups[1], groups[2], groups[0]], picked
        )
        *others, proxy_grad = lax.optimization_barrier((*others, proxy_grad))
        mine = finish_call(mine, others)
        if narrow == 2:
            feature_grad = join_call(mine, to_core(mine, 1))
        else:
            mine = mine[None]
            for bit in range(narrow.bit_length() - 1):
                mine = jnp.concatenate([mine, to_core(mine, 1 << bit)], axis=0)
            feature_grad = jnp.take(mine, n ^ jnp.arange(narrow), axis=0).transpose(1, 0, 2).reshape(rows, width)
        return (feature_grad, proxy_grad)

    return per_device


def solution(mesh):
    placed = (P("wide", None), P(("wide", "narrow"), None), P(("wide", "narrow")), P(), P())
    return jax.shard_map(
        make(mesh.shape["wide"], mesh.shape["narrow"]),
        mesh=mesh,
        in_specs=placed,
        out_specs=(P("wide", None), P(("wide", "narrow"), None)),
        check_vma=False,
    )
```
